256 devices in a mesh: dp: 4 (over x), gy: 8 (over y, core), gx: 8 (over z).
Axes of the slice: x: 4, y: 4, z: 8, core: 2. Of those that a mesh axis runs over, the one named last changes fastest.
Arguments:
- tiles: bfloat16 [4, 128, 256, 768], P('dp', 'gy', 'gx'), may hold values from -6 to 6
- cotangent: bfloat16 [4, 128, 256, 768], P('dp', 'gy', 'gx'), may hold values from -6 to 6
- tissue: int32 [4, 128, 256], P('dp', 'gy', 'gx'), may hold values from 0 to 1, as said below
- w_qkv: bfloat16 [768, 2304], replicated, may hold values from -0.21875 to 0.21875
- w_proj: bfloat16 [768, 768], replicated, may hold values from -0.21875 to 0.21875
Outputs:
- out_tiles: bfloat16 [4, 128, 256, 768], P('dp', 'gy', 'gx')
- grad_tiles: bfloat16 [4, 128, 256, 768], P('dp', 'gy', 'gx')
- grad_qkv: float32 [768, 2304], P(('dp', 'gy', 'gx'))
- grad_proj: float32 [768, 768], P(('dp', 'gy', 'gx'))
The draws below stay inside these ranges and needn't reach their ends.
Inputs may be any that keep to these rules, and one draw needn't show every extreme that they name: Within each slide, grid row of 16 tiles and block of 32 tile columns, every window either holds no tissue tile or holds one at its centre cell. Two blocks of the same slide and grid row whose column block indices differ by half their number hold together at most 2 windows with tissue; in every draw some such pair holds exactly 2, all in one block.
All inputs are finite; a program needn't handle non-finite values.
Results may differ from the reference program's by a relative error of at most 0.0095.
Values may be sent and summed in bfloat16 or wider, within the bound.
No kernel may reach another device: no remote copies, remote signals or barrier semaphores. Data moves between devices by JAX's collectives and lax.ppermute only.
A program may use at most 128 MiB of HBM per device.

```python
import math
import jax
import jax.numpy as jnp
from jax import lax

D = 768
HEADS = 12
WIN = 16
WCOLS_DEV = 2
HALF = 1
SLIDES = 4
ROWS = 128
COLS = 256


def draw_tissue(key, part):
    key = jax.random.fold_in(key, 7)
    key_dense, key_sparse, key_side, key_order, key_cells = jax.random.split(key, 5)
    grid_rows = ROWS // WIN
    blocks = COLS // (WIN * WCOLS_DEV)
    pairs = blocks // 2
    shape = (SLIDES, grid_rows, pairs)
    dense = jax.random.randint(key_dense, shape, HALF, WCOLS_DEV + 1)
    first = (jnp.arange(SLIDES)[:, None, None] == 0) & (jnp.arange(grid_rows)[None, :, None] == 0) & (jnp.arange(pairs)[None, None, :] == 0)
    dense = jnp.where(first, WCOLS_DEV, dense)
    sparse = jax.random.randint(key_sparse, shape, 0, WCOLS_DEV - dense + 1)
    sparse = jnp.where(first, 0, sparse)
    side = jax.random.randint(key_side, shape, 0, 2)
    lower = jnp.where(side == 1, dense, sparse)
    upper = jnp.where(side == 1, sparse, dense)
    counts = jnp.concatenate([lower, upper], axis=-1)
    scores = jax.random.randint(key_order, (SLIDES, grid_rows, blocks, WCOLS_DEV), 0, 1 << 20)
    scores = scores * WCOLS_DEV + jnp.arange(WCOLS_DEV, dtype=jnp.int32)
    ranks = jnp.argsort(jnp.argsort(scores, axis=-1), axis=-1)
    occupied = ranks < counts[..., None]
    cells = jax.random.randint(key_cells, (SLIDES, grid_rows, blocks, WCOLS_DEV, WIN, WIN), 0, 10) < 7
    centre = (jnp.arange(WIN)[:, None] == WIN // 2) & (jnp.arange(WIN)[None, :] == WIN // 2)
    cells = cells | centre
    field = occupied[..., None, None] & cells
    field = field.transpose(0, 1, 4, 2, 3, 5).reshape(SLIDES, ROWS, COLS)
    return field.astype(jnp.int32)


def levels(stream_key, dims, cuts, low, largest):
    gain, own = 1.0, jax.random.fold_in(stream_key, 6)
    for dim, parts in cuts:
        heights = jnp.exp(jax.random.uniform(jax.random.fold_in(own, dim), (parts,), jnp.float32, low / len(cuts), largest / len(cuts)))
        gain = gain * jnp.repeat(heights, dims[dim] // parts).reshape([-1 if axis == dim else 1 for axis in range(len(dims))])
    return gain


def scatter_about(own_key, extent, deviation, most, pieces=(), held_as=jnp.bfloat16):
    result = jax.random.normal(own_key, extent, jnp.float32) * deviation
    if len(pieces) > 0:
        result = levels(own_key, extent, pieces, -0.22, 0.18) * result
    return jnp.clip(result, min=-most, max=most).astype(held_as)


def setup_inputs(seed: int = 0) -> dict:
    arg_keys = jax.random.split(jax.random.key(seed), 6)
    return {
        "tiles": scatter_about(arg_keys[0], (SLIDES, ROWS, COLS, D), 1.0, 6.0, ((0, 4), (1, 8), (2, 8))),
        "cotangent": scatter_about(arg_keys[1], (SLIDES, ROWS, COLS, D), 1.0, 6.0, ((0, 4), (1, 8), (2, 8))),
        "tissue": draw_tissue(jax.random.fold_in(arg_keys[5], 71), 0),
        "w_qkv": scatter_about(arg_keys[3], (D, 3 * D), D ** -0.5, 0.21875),
        "w_proj": scatter_about(arg_keys[4], (D, D), D ** -0.5, 0.21875),
    }


def window_pass(tiles_win, cot_win, tissue_win, w_qkv, w_proj, heads):
    slots, cells, width = tiles_win.shape
    head_size = width // heads
    scale = 1.0 / math.sqrt(head_size)
    xf = tiles_win.astype(jnp.float32)
    mean = lax.optimization_barrier(jnp.mean(xf, -1, keepdims=True))
    centred = xf - mean
    inv = lax.rsqrt(lax.optimization_barrier(jnp.mean(centred * centred, -1, keepdims=True)) + 1e-05)
    normed = centred * inv
    hidden = normed.astype(jnp.bfloat16).reshape(slots * cells, width)
    qkv = jnp.dot(hidden, w_qkv, preferred_element_type=jnp.float32)
    qkv = lax.optimization_barrier(qkv.astype(jnp.bfloat16)).astype(jnp.float32)
    qkv = qkv.reshape(slots, cells, 3, heads, head_size)
    query = qkv[:, :, 0]
    keys = qkv[:, :, 1]
    values = qkv[:, :, 2]
    empty = (lax.optimization_barrier(jnp.sum(tissue_win, -1, keepdims=True)) == 0).astype(jnp.float32)
    live = jnp.maximum(tissue_win, empty)
    scores = jnp.einsum('sqhe,skhe->shqk', query, keys) * scale
    weights = jnp.exp(scores) * live[:, None, None, :]
    probs = weights / lax.optimization_barrier(jnp.sum(weights, -1, keepdims=True))
    probs_b = lax.optimization_barrier(probs.astype(jnp.bfloat16)).astype(jnp.float32)
    attended = jnp.einsum('shqk,skhe->sqhe', probs_b, values).astype(jnp.bfloat16)
    attended = attended.reshape(slots * cells, width)
    branch = jnp.dot(attended, w_proj, preferred_element_type=jnp.float32).reshape(slots, cells, width)
    qmask = tissue_win[..., None]
    out = (xf + qmask * branch).astype(jnp.bfloat16)
    cot_f = cot_win.astype(jnp.float32)
    dbranch = (cot_f * qmask).astype(jnp.bfloat16).reshape(slots * cells, width)
    grad_proj = jnp.dot(attended.T, dbranch, preferred_element_type=jnp.float32)
    dattended = jnp.dot(dbranch, w_proj.T, preferred_element_type=jnp.float32)
    dattended = lax.optimization_barrier(dattended.astype(jnp.bfloat16)).astype(jnp.float32)
    dattended = dattended.reshape(slots, cells, heads, head_size)
    dprobs = jnp.einsum('sqhe,skhe->shqk', dattended, values)
    dvalues = jnp.einsum('shqk,sqhe->skhe', probs_b, dattended)
    dscores = probs * (dprobs - lax.optimization_barrier(jnp.sum(probs * dprobs, -1, keepdims=True)))
    dscores = lax.optimization_barrier(dscores.astype(jnp.bfloat16)).astype(jnp.float32)
    dquery = jnp.einsum('shqk,skhe->sqhe', dscores, keys) * scale
    dkeys = jnp.einsum('shqk,sqhe->skhe', dscores, query) * scale
    dqkv = jnp.stack([dquery, dkeys, dvalues], axis=2).astype(jnp.bfloat16)
    dqkv = dqkv.reshape(slots * cells, 3 * width)
    grad_qkv = jnp.dot(hidden.T, dqkv, preferred_element_type=jnp.float32)
    dhidden = jnp.dot(dqkv, w_qkv.T, preferred_element_type=jnp.float32).reshape(slots, cells, width)
    dnorm = inv * (dhidden - lax.optimization_barrier(jnp.mean(dhidden, -1, keepdims=True)) - normed * lax.optimization_barrier(jnp.mean(dhidden * normed, -1, keepdims=True)))
    grad_in = (cot_f + dnorm).astype(jnp.bfloat16)
    return (out, grad_in, grad_qkv, grad_proj)

def reference(tiles, cotangent, tissue, w_qkv, w_proj):
    half_win = WIN // 2
    shifted = jnp.roll(tiles, (-half_win, -half_win), (1, 2))
    slides, rows, cols, width = shifted.shape
    grid_rows = rows // WIN
    grid_cols = cols // WIN

    def split_windows(field):
        feats = field.shape[3]
        field = field.reshape(slides, grid_rows, WIN, grid_cols, WIN, feats)
        return field.transpose(0, 1, 3, 2, 4, 5).reshape(slides * grid_rows * grid_cols, WIN * WIN, feats)

    def join_windows(field):
        field = field.reshape(slides, grid_rows, grid_cols, WIN, WIN, width)
        return field.transpose(0, 1, 3, 2, 4, 5).reshape(slides, rows, cols, width)
    tiles_win = split_windows(shifted)
    cot_win = split_windows(cotangent)
    tissue_win = split_windows(tissue.astype(jnp.float32)[..., None])[..., 0]

    def one(carry, item):
        x_one, g_one, t_one = item

        def busy(unused):
            out, grad_in, g_qkv, g_proj = window_pass(x_one[None], g_one[None], t_one[None], w_qkv, w_proj, HEADS)
            return (out[0], grad_in[0], g_qkv, g_proj)

        def quiet(unused):
            return (x_one, g_one, jnp.zeros((width, 3 * width), jnp.float32), jnp.zeros((width, width), jnp.float32))
        out, grad_in, g_qkv, g_proj = lax.cond(jnp.sum(t_one) > 0, busy, quiet, 0)
        return ((carry[0] + g_qkv, carry[1] + g_proj), (out, grad_in))
    start = (jnp.zeros((width, 3 * width), jnp.float32), jnp.zeros((width, width), jnp.float32))
    (total_qkv, total_proj), (outs, grads) = lax.scan(one, start, (tiles_win, cot_win, tissue_win))
    scale = 1.0 / math.sqrt(slides * grid_rows * grid_cols)
    return (join_windows(outs), join_windows(grads), total_qkv * scale, total_proj * scale)
```

```python
import math

import jax
import jax.numpy as jnp
from jax import lax
from jax.experimental import pallas as pl
from jax.experimental.pallas import tpu as pltpu
from jax.sharding import PartitionSpec as P

F32 = jnp.float32
BF = jnp.bfloat16
D = 768
WIN = 16
CELLS = WIN * WIN
GROUPS = 3
GW = D // GROUPS
HEAD_SCALE = 0.125
VMEM = 56 * 1024 * 1024


def nn(a, b):
    return lax.dot_general(a, b, (((1,), (0,)), ((), ())), preferred_element_type=F32)


def nt(a, b):
    return lax.dot_general(a, b, (((1,), (1,)), ((), ())), preferred_element_type=F32)


def tn(a, b):
    return lax.dot_general(a, b, (((0,), (0,)), ((), ())), preferred_element_type=F32)


def full(shape):
    return pl.BlockSpec(shape, lambda *g: (0,) * len(shape))


def cost(flops, size):
    return pl.CostEstimate(flops=int(flops), bytes_accessed=int(size), transcendentals=0)


def branch_kernel(cot_ref, tis_ref, wp_ref, db_ref, da_ref):
    for w in range(2):
        db = cot_ref[:, w].reshape(CELLS, D) * jnp.tile(tis_ref[w], (1, D // 128))
        db_ref[w] = db
        da_ref[w] = nt(db, wp_ref[...]).astype(BF)


def branch(cot, tis, w_proj):
    shape = jax.ShapeDtypeStruct((2, CELLS, D), BF)
    return pl.pallas_call(
        branch_kernel,
        out_shape=[shape, shape],
        compiler_params=pltpu.CompilerParams(vmem_limit_bytes=VMEM),
        cost_estimate=cost(6e8, 4e6),
        name="branch",
    )(cot, tis, w_proj)


def moments(x):
    mean = jnp.mean(x, -1, keepdims=True)
    centred = x - mean
    inv = lax.rsqrt(jnp.mean(centred * centred, -1, keepdims=True) + 1e-05)
    return centred * inv, inv


def head_pair(q2, k2, v2, da2, ones2):
    lane = lax.broadcasted_iota(jnp.int32, (1, 128), 1)
    sel_a = (lane < 64).astype(BF)
    sel_b = (lane >= 64).astype(BF)
    ka, kb, va, vb = k2 * sel_a, k2 * sel_b, v2 * sel_a, v2 * sel_b
    wa = jnp.exp(nt(q2, ka)).astype(BF)
    wb = jnp.exp(nt(q2, kb)).astype(BF)
    both = nn(wa, jnp.concatenate([va, ones2 * sel_a], 1)) + nn(
        wb, jnp.concatenate([vb, ones2 * sel_b], 1)
    )
    rinv = 1.0 / both[:, 128:]
    attended = both[:, :128] * rinv
    lhs = jnp.concatenate([da2, (da2.astype(F32) * attended).astype(BF)], 1)
    minus_a = jnp.broadcast_to(-sel_a, (CELLS, 128))
    minus_b = jnp.broadcast_to(-sel_b, (CELLS, 128))
    dsa = (wa.astype(F32) * nt(lhs, jnp.concatenate([va, minus_a], 1))).astype(BF)
    dsb = (wb.astype(F32) * nt(lhs, jnp.concatenate([vb, minus_b], 1))).astype(BF)
    dq = (nn(dsa, ka) + nn(dsb, kb)) * (rinv * HEAD_SCALE)
    dan = (da2.astype(F32) * rinv).astype(BF)
    qn = (q2.astype(F32) * rinv).astype(BF)
    dv = tn(wa, dan * sel_a) + tn(wb, dan * sel_b)
    dk = tn(dsa, qn * sel_a) + tn(dsb, qn * sel_b)
    return attended.astype(BF), dq.astype(BF), dk.astype(BF), dv.astype(BF)


def main_kernel(
    tiles_ref, below_ref, right_ref, diag_ref, src_ref, tis_ref, live_ref,
    wq_ref, wk_ref, wv_ref, da_ref, db_ref,
    keep_ref, send_ref, att_ref, dqkv_ref, xw_ref,
    hid_ref, hid_t_ref, alls_ref,
):
    step = pl.program_id(0)

    def order():
        column = lax.broadcasted_iota(jnp.int32, (D, D), 1)
        return jnp.where(column == src_ref[...], 1.0, 0.0).astype(BF)

    def put(grad):
        keep_ref[...] = grad[: D // 2].astype(BF)
        send_ref[...] = grad[D // 2 :].astype(BF)

    @pl.when(step == 0)
    def _():
        own = tiles_ref[8:16].astype(F32)
        low = below_ref[...].astype(F32)
        right = right_ref[...].astype(F32)
        diag = diag_ref[...].astype(F32)
        perm = order()
        for w in range(2):
            if w == 0:
                top, bottom = own[:, 8:24], low[:, 8:24]
            else:
                top = jnp.concatenate([own[:, 24:32], right], 1)
                bottom = jnp.concatenate([low[:, 24:32], diag], 1)
            x = jnp.concatenate([top, bottom], 0).reshape(CELLS, D)
            xw_ref[w] = x.astype(BF)
            normed, _ = moments(x)
            hidden = normed.astype(BF)
            hid_ref[w] = hidden
            hid_t_ref[:, w * CELLS : (w + 1) * CELLS] = nt(perm, hidden).astype(BF)

    @pl.when(step < GROUPS)
    def _():
        for w in range(2):
            hidden = hid_ref[w]
            query = (nn(hidden, wq_ref[...])).astype(BF) * BF(HEAD_SCALE)
            tis2 = tis_ref[w]
            tis4 = jnp.concatenate([tis2, tis2], 1)
            key = nn(hidden, wk_ref[...]).astype(BF) * tis4
            value = nn(hidden, wv_ref[...]).astype(BF) * tis4
            for p in range(2):
                s = slice(p * 128, (p + 1) * 128)
                att, dq, dk, dv = head_pair(
                    query[:, s], key[:, s], value[:, s], da_ref[w, :, s], live_ref[w]
                )
                att_ref[w, :, s] = att
                dqkv_ref[0, w, :, s] = dq
                dqkv_ref[0, w, :, slice(GW + p * 128, GW + (p + 1) * 128)] = dk * tis2
                dqkv_ref[0, w, :, slice(2 * GW + p * 128, 2 * GW + (p + 1) * 128)] = dv * tis2
        alls_ref[step] = att_ref[...].reshape(2 * CELLS, GW)
        put(nn(hid_t_ref[...], dqkv_ref[0].reshape(2 * CELLS, D)))

    @pl.when(step == GROUPS)
    def _():
        attended = jnp.concatenate([alls_ref[g] for g in range(GROUPS)], 1)
        att_t = nt(order(), attended).astype(BF)
        put(nn(att_t, db_ref[...].reshape(2 * CELLS, D)))


def main(tiles, below, right, diag, src, tis, live, w_qkv, da, db):
    def columns(block):
        return pl.BlockSpec((D, GW), lambda g: (0, block * GROUPS + jnp.minimum(g, GROUPS - 1)))

    part = pl.BlockSpec((2, CELLS, GW), lambda g: (0, 0, jnp.minimum(g, GROUPS - 1)))
    half = pl.BlockSpec((D // 2, D), lambda g: (0, g))
    wide = (GROUPS + 1) * D
    return pl.pallas_call(
        main_kernel,
        grid=(GROUPS + 1,),
        in_specs=[
            full((16, 32, D)), full((8, 32, D)), full((8, 8, D)), full((8, 8, D)),
            full((D, 1)), full((2, CELLS, 128)), full((2, CELLS, 128)),
            columns(0), columns(1), columns(2), part, full((2, CELLS, D)),
        ],
        out_specs=[
            half, half, part,
            pl.BlockSpec((1, 2, CELLS, D), lambda g: (jnp.minimum(g, GROUPS - 1), 0, 0, 0)),
            full((2, CELLS, D)),
        ],
        out_shape=[
            jax.ShapeDtypeStruct((D // 2, wide), BF),
            jax.ShapeDtypeStruct((D // 2, wide), BF),
            jax.ShapeDtypeStruct((2, CELLS, D), BF),
            jax.ShapeDtypeStruct((GROUPS, 2, CELLS, D), BF),
            jax.ShapeDtypeStruct((2, CELLS, D), BF),
        ],
        scratch_shapes=[
            pltpu.VMEM((2, CELLS, D), BF),
            pltpu.VMEM((D, 2 * CELLS), BF),
            pltpu.VMEM((GROUPS, 2 * CELLS, GW), BF),
        ],
        compiler_params=pltpu.CompilerParams(vmem_limit_bytes=VMEM),
        cost_estimate=cost(6e9, 16e6),
        name="heads",
    )(tiles, below, right, diag, src, tis, live, w_qkv, w_qkv, w_qkv, da, db)


def outs_kernel(
    xw_ref, cot_ref, tis_ref, att_ref, dqkv_ref, wq_ref, wk_ref, wv_ref, wp_ref,
    out_ref, grad_ref, acc_ref,
):
    step = pl.program_id(0)
    weights = jnp.concatenate([wq_ref[...], wk_ref[...], wv_ref[...]], 1)
    for w in range(2):
        part = nt(dqkv_ref[0, w], weights)

        @pl.when(step == 0)
        def _():
            acc_ref[w] = part

        @pl.when(step > 0)
        def _():
            acc_ref[w] += part

    @pl.when(step == GROUPS - 1)
    def _():
        for w in range(2):
            x = xw_ref[w].astype(F32)
            tis = jnp.tile(tis_ref[w].astype(F32), (1, D // 128))
            out = x + tis * nn(att_ref[w], wp_ref[...])
            out_ref[:, w] = out.astype(BF).reshape(WIN, WIN, D)
            normed, inv = moments(x)
            dh = acc_ref[w]
            dnorm = inv * (
                dh
                - jnp.mean(dh, -1, keepdims=True)
                - normed * jnp.mean(dh * normed, -1, keepdims=True)
            )
            grad = cot_ref[:, w].reshape(CELLS, D).astype(F32) + dnorm
            grad_ref[:, w] = grad.astype(BF).reshape(WIN, WIN, D)


def outs(xw, cot, tis, att, dqkv, w_qkv, w_proj):
    def columns(block):
        return pl.BlockSpec((D, GW), lambda g: (0, block * GROUPS + g))

    shape = jax.ShapeDtypeStruct((WIN, 2, WIN, D), BF)
    out, grad = pl.pallas_call(
        outs_kernel,
        grid=(GROUPS,),
        in_specs=[
            full((2, CELLS, D)), full((WIN, 2, WIN, D)), full((2, CELLS, 128)), full((2, CELLS, D)),
            pl.BlockSpec((1, 2, CELLS, D), lambda g: (g, 0, 0, 0)),
            columns(0), columns(1), columns(2), full((D, D)),
        ],
        out_specs=[full((WIN, 2, WIN, D))] * 2,
        out_shape=[shape, shape],
        scratch_shapes=[pltpu.VMEM((2, CELLS, D), F32)],
        compiler_params=pltpu.CompilerParams(vmem_limit_bytes=VMEM),
        cost_estimate=cost(2.4e9, 12e6),
        name="outs",
    )(xw, cot, tis, att, dqkv, w_qkv, w_qkv, w_qkv, w_proj)
    return out.reshape(1, WIN, 2 * WIN, D), grad.reshape(1, WIN, 2 * WIN, D)


def send(value, axis, move):
    devices = lax.axis_size(axis)
    return lax.ppermute(value, axis, [(i, move(i) % devices) for i in range(devices)])


def add(*terms):
    total = terms[0].astype(F32)
    for term in terms[1:]:
        total = total + term.astype(F32)
    return total.astype(BF)


def ring_of_four(blocks, axis, step):
    _, _, width = blocks.shape
    n = width // 2
    from_low = send(blocks[2, :, :n], axis, lambda j: j + step)
    from_high = send(blocks[2, :, n:], axis, lambda j: j - step)
    up = jnp.concatenate([add(blocks[1, :, :n], from_low), blocks[1, :, n:]], 1)
    down = jnp.concatenate([blocks[3, :, :n], add(blocks[3, :, n:], from_high)], 1)
    got_up = send(up, axis, lambda j: j + step)
    got_down = send(down, axis, lambda j: j - step)
    return add(blocks[0], got_up, got_down)


def row_order():
    dp = lax.axis_index("dp")
    gy = lax.axis_index("gy")
    y, core = gy // 2, gy % 2
    at = jnp.arange(D, dtype=jnp.int32)
    rest = at % 24
    y_of = (at // 24 % 4 + y) % 4
    dp_of = (at // 96 % 4 + dp) % 4
    core_of = (at // 384 + core) % 2
    return (((dp_of * 8 + y_of * 2 + core_of) * 24 + rest)[:, None]).astype(jnp.int32)


def shards(tiles, cotangent, tissue, w_qkv, w_proj):
    mine = tiles[0]
    below = send(mine[:8], "gy", lambda i: i - 1)
    right = send(mine[8:, :8], "gx", lambda i: i - 1)
    ny, nx = lax.axis_size("gy"), lax.axis_size("gx")
    diag = lax.ppermute(
        mine[:8, :8],
        ("gy", "gx"),
        [
            (a * nx + b, (a - 1) % ny * nx + (b - 1) % nx)
            for a in range(ny)
            for b in range(nx)
        ],
    )
    cells = tissue.reshape(WIN, 2, WIN).transpose(1, 0, 2).reshape(2, CELLS, 1)
    empty = jnp.max(cells, 1, keepdims=True) == 0
    tis = jnp.broadcast_to(cells.astype(BF), (2, CELLS, 128))
    live = jnp.broadcast_to(jnp.where(empty, 1, cells).astype(BF), (2, CELLS, 128))
    cot = cotangent.reshape(WIN, 2, WIN, D)
    db, da = branch(cot, tis, w_proj)
    keep, give, att, dqkv, xw = main(
        mine, below, right, diag, row_order(), tis, live, w_qkv, da, db
    )
    rows = add(keep, send(give, "gy", lambda i: i ^ 1))
    rows = ring_of_four(rows.reshape(4, 96, -1), "dp", 1)
    rows = ring_of_four(rows.reshape(4, 24, -1), "gy", 2)
    parts = lax.all_to_all(rows.reshape(8, 3, -1), "gx", 0, 0)
    total = jnp.sum(parts.astype(F32), 0) * (1.0 / math.sqrt(512))
    grad_qkv = total[:, : 3 * D].reshape(3, GROUPS, 3, GW).transpose(0, 2, 1, 3)
    out, grad = outs(xw, cot, tis, att, dqkv, w_qkv, w_proj)
    return out, grad, grad_qkv.reshape(3, 3 * D), total[:, 3 * D :]


def solution(mesh):
    block = P("dp", "gy", "gx", None)
    in_specs = (block, block, P("dp", "gy", "gx"), P(), P())
    out_specs = (block, block, P(("dp", "gy", "gx"), None), P(("dp", "gy", "gx"), None))
    return jax.shard_map(
        shards, mesh=mesh, in_specs=in_specs, out_specs=out_specs, check_vma=False
    )
```

```python
import math

import jax
import jax.numpy as jnp
from jax import lax
from jax.experimental import pallas as pl
from jax.experimental.pallas import tpu as pltpu
from jax.sharding import PartitionSpec as P

F32 = jnp.float32
BF = jnp.bfloat16
D = 768
WIN = 16
CELLS = WIN * WIN
GROUPS = 3
GW = D // GROUPS
HEAD_SCALE = 0.125
VMEM = 56 * 1024 * 1024


def nn(a, b):
    return lax.dot_general(a, b, (((1,), (0,)), ((), ())), preferred_element_type=F32)


def nt(a, b):
    return lax.dot_general(a, b, (((1,), (1,)), ((), ())), preferred_element_type=F32)


def tn(a, b):
    return lax.dot_general(a, b, (((0,), (0,)), ((), ())), preferred_element_type=F32)


def full(shape):
    return pl.BlockSpec(shape, lambda *g: (0,) * len(shape))


def cost(flops, size):
    return pl.CostEstimate(flops=int(flops), bytes_accessed=int(size), transcendentals=0)


def branch_kernel(cot_ref, tissue_ref, wp_ref, db_ref, da_ref, tis_ref, live_ref):
    grid = tissue_ref[...].astype(F32).astype(BF)
    cell = lax.broadcasted_iota(jnp.int32, (CELLS, 1), 0)
    row_of = lax.broadcasted_iota(jnp.int32, (CELLS, WIN), 1) == (cell >> 4)
    rows = nn(row_of.astype(F32).astype(BF), grid)
    lane = lax.broadcasted_iota(jnp.int32, (CELLS, 2 * WIN), 1)
    ones = jnp.ones((2 * WIN, 128), BF)
    for w in range(2):
        own = jnp.where(lane == (cell & 15) + w * WIN, rows, 0.0).astype(BF)
        tis = nn(own, ones)
        some = jnp.max(jnp.max(tis, 0, keepdims=True), 1, keepdims=True)
        tis_ref[w] = tis.astype(BF)
        live_ref[w] = jnp.maximum(tis, 1.0 - some).astype(BF)
        db = cot_ref[:, w].reshape(CELLS, D) * jnp.tile(tis.astype(BF), (1, D // 128))
        db_ref[w] = db
        da_ref[w] = nt(db, wp_ref[...]).astype(BF)


def branch(cot, tissue, w_proj):
    shape = jax.ShapeDtypeStruct((2, CELLS, D), BF)
    mask = jax.ShapeDtypeStruct((2, CELLS, 128), BF)
    return pl.pallas_call(
        branch_kernel,
        out_shape=[shape, shape, mask, mask],
        compiler_params=pltpu.CompilerParams(vmem_limit_bytes=VMEM),
        cost_estimate=cost(6e8, 4e6),
        name="branch",
    )(cot, tissue, w_proj)


def row_order(first):
    gy = lax.axis_index("gy")
    dp, y, core = lax.axis_index("dp"), gy >> 1, gy & 1
    at = lax.broadcasted_iota(jnp.int32, (D, 1), 0)
    block = ((at.astype(F32) + 0.5) * (1.0 / 24)).astype(jnp.int32)
    outer, inner = (block >> 2) & 3, block & 3
    if first == "dp":
        dp_of, y_of = (outer + dp) & 3, (inner + y) & 3
    else:
        dp_of, y_of = (inner + dp) & 3, (outer + y) & 3
    core_of = ((block >> 4) + core) & 1
    source = (dp_of * 8 + y_of * 2 + core_of) * 24 + at - block * 24
    column = lax.broadcasted_iota(jnp.int32, (D, D), 1)
    return jnp.where(column == source, 1.0, 0.0).astype(BF)


def moments(x):
    mean = jnp.mean(x, -1, keepdims=True)
    centred = x - mean
    inv = lax.rsqrt(jnp.mean(centred * centred, -1, keepdims=True) + 1e-05)
    return centred * inv, inv


def head_pair(q2, k2, v2, da2, ones2):
    lane = lax.broadcasted_iota(jnp.int32, (1, 128), 1)
    sel_a = (lane < 64).astype(BF)
    sel_b = (lane >= 64).astype(BF)
    ka, kb, va, vb = k2 * sel_a, k2 * sel_b, v2 * sel_a, v2 * sel_b
    wa = jnp.exp(nt(q2, ka)).astype(BF)
    wb = jnp.exp(nt(q2, kb)).astype(BF)
    both = nn(wa, jnp.concatenate([va, ones2 * sel_a], 1)) + nn(
        wb, jnp.concatenate([vb, ones2 * sel_b], 1)
    )
    rinv = 1.0 / both[:, 128:]
    attended = both[:, :128] * rinv
    lhs = jnp.concatenate([da2, (da2.astype(F32) * attended).astype(BF)], 1)
    minus_a = jnp.broadcast_to(-sel_a, (CELLS, 128))
    minus_b = jnp.broadcast_to(-sel_b, (CELLS, 128))
    dsa = (wa.astype(F32) * nt(lhs, jnp.concatenate([va, minus_a], 1))).astype(BF)
    dsb = (wb.astype(F32) * nt(lhs, jnp.concatenate([vb, minus_b], 1))).astype(BF)
    dq = (nn(dsa, ka) + nn(dsb, kb)) * (rinv * HEAD_SCALE)
    dan = (da2.astype(F32) * rinv).astype(BF)
    qn = (q2.astype(F32) * rinv).astype(BF)
    dv = tn(wa, dan * sel_a) + tn(wb, dan * sel_b)
    dk = tn(dsa, qn * sel_a) + tn(dsb, qn * sel_b)
    return attended.astype(BF), dq.astype(BF), dk.astype(BF), dv.astype(BF)


def put(grad, keep_ref, send_ref):
    keep_ref[...] = grad[: D // 2].astype(BF)
    send_ref[...] = grad[D // 2 :].astype(BF)


def heads_group(
    hid_ref, hid_t_ref, tis_ref, live_ref, wq_ref, wk_ref, wv_ref, da_ref,
    keep_ref, send_ref, att_ref, dqkv_ref,
):
    for w in range(2):
        hidden = hid_ref[w]
        query = nn(hidden, wq_ref[...]).astype(BF) * BF(HEAD_SCALE)
        tis2 = tis_ref[w]
        tis4 = jnp.concatenate([tis2, tis2], 1)
        key = nn(hidden, wk_ref[...]).astype(BF) * tis4
        value = nn(hidden, wv_ref[...]).astype(BF) * tis4
        for p in range(2):
            s = slice(p * 128, (p + 1) * 128)
            att, dq, dk, dv = head_pair(
                query[:, s], key[:, s], value[:, s], da_ref[w, :, s], live_ref[w]
            )
            att_ref[w, :, s] = att
            dqkv_ref[0, w, :, s] = dq
            dqkv_ref[0, w, :, slice(GW + p * 128, GW + (p + 1) * 128)] = dk * tis2
            dqkv_ref[0, w, :, slice(2 * GW + p * 128, 2 * GW + (p + 1) * 128)] = dv * tis2
    put(nn(hid_t_ref[...], dqkv_ref[0].reshape(2 * CELLS, D)), keep_ref, send_ref)


def first_kernel(
    tiles_ref, below_ref, right_ref, diag_ref, tis_ref, live_ref,
    wq_ref, wk_ref, wv_ref, da_ref,
    keep_ref, send_ref, att_ref, dqkv_ref, xw_ref, hid_ref, hid_t_ref,
):
    @pl.when(pl.program_id(0) == 0)
    def _():
        own = tiles_ref[8:16].astype(F32)
        low = below_ref[...].astype(F32)
        right = right_ref[...].astype(F32)
        diag = diag_ref[...].astype(F32)
        perm = row_order("dp")
        for w in range(2):
            if w == 0:
                top, bottom = own[:, 8:24], low[:, 8:24]
            else:
                top = jnp.concatenate([own[:, 24:32], right], 1)
                bottom = jnp.concatenate([low[:, 24:32], diag], 1)
            x = jnp.concatenate([top, bottom], 0).reshape(CELLS, D)
            xw_ref[w] = x.astype(BF)
            normed, _ = moments(x)
            hidden = normed.astype(BF)
            hid_ref[w] = hidden
            hid_t_ref[:, w * CELLS : (w + 1) * CELLS] = nt(perm, hidden).astype(BF)

    heads_group(
        hid_ref, hid_t_ref, tis_ref, live_ref, wq_ref, wk_ref, wv_ref, da_ref,
        keep_ref, send_ref, att_ref, dqkv_ref,
    )


def last_kernel(
    hid_ref, tis_ref, live_ref, wq_ref, wk_ref, wv_ref, da_ref,
    keep_ref, send_ref, att_ref, dqkv_ref, hid_t_ref,
):
    perm = row_order("gy")
    for w in range(2):
        hid_t_ref[:, w * CELLS : (w + 1) * CELLS] = nt(perm, hid_ref[w]).astype(BF)
    heads_group(
        hid_ref, hid_t_ref, tis_ref, live_ref, wq_ref, wk_ref, wv_ref, da_ref,
        keep_ref, send_ref, att_ref, dqkv_ref,
    )


def columns(block, first):
    return pl.BlockSpec((D, GW), lambda g: (0, block * GROUPS + first + g))


def heads_specs(first, groups):
    inputs = [
        full((2, CELLS, 128)), full((2, CELLS, 128)),
        columns(0, first), columns(1, first), columns(2, first),
        pl.BlockSpec((2, CELLS, GW), lambda g: (0, 0, first + g)),
    ]
    half = pl.BlockSpec((D // 2, D), lambda g: (0, g))
    outputs = [
        half, half,
        pl.BlockSpec((2, CELLS, GW), lambda g: (0, 0, g)),
        pl.BlockSpec((1, 2, CELLS, D), lambda g: (g, 0, 0, 0)),
    ]
    shapes = [
        jax.ShapeDtypeStruct((D // 2, groups * D), BF),
        jax.ShapeDtypeStruct((D // 2, groups * D), BF),
        jax.ShapeDtypeStruct((2, CELLS, groups * GW), BF),
        jax.ShapeDtypeStruct((groups, 2, CELLS, D), BF),
    ]
    return inputs, outputs, shapes


def first_heads(tiles, below, right, diag, tis, live, w_qkv, da):
    inputs, outputs, shapes = heads_specs(0, 2)
    rows = jax.ShapeDtypeStruct((2, CELLS, D), BF)
    return pl.pallas_call(
        first_kernel,
        grid=(2,),
        in_specs=[full((16, 32, D)), full((8, 32, D)), full((8, 8, D)), full((8, 8, D))] + inputs,
        out_specs=outputs + [full((2, CELLS, D))] * 2,
        out_shape=shapes + [rows, rows],
        scratch_shapes=[pltpu.VMEM((D, 2 * CELLS), BF)],
        compiler_params=pltpu.CompilerParams(vmem_limit_bytes=VMEM),
        cost_estimate=cost(6e9, 10e6),
        name="first_heads",
    )(tiles, below, right, diag, tis, live, w_qkv, w_qkv, w_qkv, da)


def last_heads(hid, tis, live, w_qkv, da):
    inputs, outputs, shapes = heads_specs(2, 1)
    return pl.pallas_call(
        last_kernel,
        grid=(1,),
        in_specs=[full((2, CELLS, D))] + inputs,
        out_specs=outputs,
        out_shape=shapes,
        scratch_shapes=[pltpu.VMEM((D, 2 * CELLS), BF)],
        compiler_params=pltpu.CompilerParams(vmem_limit_bytes=VMEM),
        cost_estimate=cost(4e9, 6e6),
        name="last_heads",
    )(hid, tis, live, w_qkv, w_qkv, w_qkv, da)


def proj_kernel(att0_ref, att1_ref, db_ref, keep_ref, send_ref):
    attended = jnp.concatenate([att0_ref[...], att1_ref[...]], 2).reshape(2 * CELLS, D)
    att_t = nt(row_order("gy"), attended).astype(BF)
    put(nn(att_t, db_ref[...].reshape(2 * CELLS, D)), keep_ref, send_ref)


def proj_grad(att0, att1, db):
    shape = jax.ShapeDtypeStruct((D // 2, D), BF)
    return pl.pallas_call(
        proj_kernel,
        out_shape=[shape, shape],
        compiler_params=pltpu.CompilerParams(vmem_limit_bytes=VMEM),
        cost_estimate=cost(2e9, 4e6),
        name="proj_grad",
    )(att0, att1, db)


def outs_kernel(
    xw_ref, cot_ref, tis_ref, att0_ref, att1_ref, dqkv0_ref, dqkv1_ref,
    wq_ref, wk_ref, wv_ref, wp_ref, out_ref, grad_ref, acc_ref,
):
    step = pl.program_id(0)
    weights = jnp.concatenate([wq_ref[...], wk_ref[...], wv_ref[...]], 1)
    for w in range(2):
        dqkv = jnp.where(step < GROUPS - 1, dqkv0_ref[0, w], dqkv1_ref[0, w])
        part = nt(dqkv, weights)

        @pl.when(step == 0)
        def _():
            acc_ref[w] = part

        @pl.when(step > 0)
        def _():
            acc_ref[w] += part

    @pl.when(step == GROUPS - 1)
    def _():
        for w in range(2):
            x = xw_ref[w].astype(F32)
            tis = jnp.tile(tis_ref[w].astype(F32), (1, D // 128))
            attended = jnp.concatenate([att0_ref[w], att1_ref[w]], 1)
            out = x + tis * nn(attended, wp_ref[...])
            out_ref[:, w] = out.astype(BF).reshape(WIN, WIN, D)
            normed, inv = moments(x)
            dh = acc_ref[w]
            dnorm = inv * (
                dh
                - jnp.mean(dh, -1, keepdims=True)
                - normed * jnp.mean(dh * normed, -1, keepdims=True)
            )
            grad = cot_ref[:, w].reshape(CELLS, D).astype(F32) + dnorm
            grad_ref[:, w] = grad.astype(BF).reshape(WIN, WIN, D)


def outs(xw, cot, tis, att0, att1, dqkv0, dqkv1, w_qkv, w_proj):
    shape = jax.ShapeDtypeStruct((WIN, 2, WIN, D), BF)
    out, grad = pl.pallas_call(
        outs_kernel,
        grid=(GROUPS,),
        in_specs=[
            full((2, CELLS, D)), full((WIN, 2, WIN, D)), full((2, CELLS, 128)),
            full((2, CELLS, 2 * GW)), full((2, CELLS, GW)),
            pl.BlockSpec((1, 2, CELLS, D), lambda g: (jnp.minimum(g, 1), 0, 0, 0)),
            full((1, 2, CELLS, D)),
            columns(0, 0), columns(1, 0), columns(2, 0), full((D, D)),
        ],
        out_specs=[full((WIN, 2, WIN, D))] * 2,
        out_shape=[shape, shape],
        scratch_shapes=[pltpu.VMEM((2, CELLS, D), F32)],
        compiler_params=pltpu.CompilerParams(vmem_limit_bytes=VMEM),
        cost_estimate=cost(6e9, 12e6),
        name="outs",
    )(xw, cot, tis, att0, att1, dqkv0, dqkv1, w_qkv, w_qkv, w_qkv, w_proj)
    return out.reshape(1, WIN, 2 * WIN, D), grad.reshape(1, WIN, 2 * WIN, D)


def send(value, axis, move):
    devices = lax.axis_size(axis)
    return lax.ppermute(value, axis, [(i, move(i) % devices) for i in range(devices)])


def add(*terms):
    total = terms[0].astype(F32)
    for term in terms[1:]:
        total = total + term.astype(F32)
    return total.astype(BF)


def ring_start(low, high, axis, step):
    from_low = send(low[2], axis, lambda j: j + step)
    from_high = send(high[2], axis, lambda j: j - step)
    return from_low, from_high


def ring_pass(low, high, came, axis, step):
    up = jnp.concatenate([add(low[1], came[0]), high[1]], 1)
    down = jnp.concatenate([low[3], add(high[3], came[1])], 1)
    return send(up, axis, lambda j: j + step), send(down, axis, lambda j: j - step)


def ring_end(low, high, came):
    n = low.shape[2]
    up, down = came
    return add(low[0], up[:, :n], down[:, :n]), add(high[0], up[:, n:], down[:, n:])


def tie(*values):
    return lax.optimization_barrier(values)


def blocks(value):
    return value.reshape(4, value.shape[0] // 4, value.shape[1])


def shards(tiles, cotangent, tissue, w_qkv, w_proj):
    mine = tiles[0]
    below = send(mine[:8], "gy", lambda i: i - 1)
    right = send(mine[8:, :8], "gx", lambda i: i - 1)
    ny, nx = lax.axis_size("gy"), lax.axis_size("gx")
    diag = lax.ppermute(
        mine[:8, :8],
        ("gy", "gx"),
        [
            (a * nx + b, (a - 1) % ny * nx + (b - 1) % nx)
            for a in range(ny)
            for b in range(nx)
        ],
    )
    cot = cotangent.reshape(WIN, 2, WIN, D)
    db, da, tis, live = branch(cot, tissue[0], w_proj)
    keep0, send0, att0, dqkv0, xw, hid = first_heads(
        mine, below, right, diag, tis, live, w_qkv, da
    )
    first = add(keep0, send(send0, "gy", lambda i: i ^ 1))
    keep1, send1, att1, dqkv1 = last_heads(hid, tis, live, w_qkv, da)
    low_b = add(keep1, send(send1, "gy", lambda i: i ^ 1))
    first, att1 = tie(first, att1)
    low_a, high_a = blocks(first[:, :D]), blocks(first[:, D:])
    came_a = ring_start(low_a, high_a, "dp", 1)
    keep2, send2 = proj_grad(att0, att1, db)
    high_b = add(keep2, send(send2, "gy", lambda i: i ^ 1))
    low_b, high_b, came_a = tie(blocks(low_b), blocks(high_b), came_a)
    came_b = ring_start(low_b, high_b, "gy", 2)
    came_a = ring_pass(low_a, high_a, came_a, "dp", 1)
    came_b, xw = tie(came_b, xw)
    came_b = ring_pass(low_b, high_b, came_b, "gy", 2)
    out, grad = outs(xw, cot, tis, att0, att1, dqkv0, dqkv1, w_qkv, w_proj)
    out, came_a, came_b = tie(out, came_a, came_b)
    low_a, high_a = (blocks(v) for v in ring_end(low_a, high_a, came_a))
    low_b, high_b = (blocks(v) for v in ring_end(low_b, high_b, came_b))
    came_a = ring_start(low_a, high_a, "gy", 2)
    came_b = ring_start(low_b, high_b, "dp", 1)
    came_a = ring_pass(low_a, high_a, came_a, "gy", 2)
    came_b = ring_pass(low_b, high_b, came_b, "dp", 1)
    low_a, high_a = ring_end(low_a, high_a, came_a)
    low_b, high_b = ring_end(low_b, high_b, came_b)
    rows = jnp.concatenate([low_a, high_a, low_b, high_b], 1)
    parts = lax.all_to_all(rows.reshape(8, 3, -1), "gx", 0, 0)
    total = jnp.sum(parts.astype(F32), 0) * (1.0 / math.sqrt(512))
    grad_qkv = total[:, : 3 * D].reshape(3, GROUPS, 3, GW).transpose(0, 2, 1, 3)
    return out, grad, grad_qkv.reshape(3, 3 * D), total[:, 3 * D :]


def solution(mesh):
    block = P("dp", "gy", "gx", None)
    in_specs = (block, block, P("dp", "gy", "gx"), P(), P())
    out_specs = (block, block, P(("dp", "gy", "gx"), None), P(("dp", "gy", "gx"), None))
    return jax.shard_map(
        shards, mesh=mesh, in_specs=in_specs, out_specs=out_specs, check_vma=False
    )
```

```python
import math

import jax
import jax.numpy as jnp
from jax import lax
from jax.experimental import pallas as pl
from jax.experimental.pallas import tpu as pltpu
from jax.sharding import PartitionSpec as P

F32 = jnp.float32
BF = jnp.bfloat16
D = 768
WIN = 16
CELLS = WIN * WIN
GROUPS = 3
GW = D // GROUPS
HEAD_SCALE = 0.125
VMEM = 32 * 1024 * 1024


def nn(a, b):
    return lax.dot_general(a, b, (((1,), (0,)), ((), ())), preferred_element_type=F32)


def nt(a, b):
    return lax.dot_general(a, b, (((1,), (1,)), ((), ())), preferred_element_type=F32)


def tn(a, b):
    return lax.dot_general(a, b, (((0,), (0,)), ((), ())), preferred_element_type=F32)


def full(shape):
    return pl.BlockSpec(shape, lambda *g: (0,) * len(shape))


def cost(flops, size):
    return pl.CostEstimate(flops=int(flops), bytes_accessed=int(size), transcendentals=0)


def branch_kernel(cot_ref, tissue_ref, wp_ref, db_ref, da_ref, tis_ref, live_ref):
    grid = tissue_ref[...].astype(F32).astype(BF)
    cell = lax.broadcasted_iota(jnp.int32, (CELLS, 1), 0)
    row_of = lax.broadcasted_iota(jnp.int32, (CELLS, WIN), 1) == (cell >> 4)
    rows = nn(row_of.astype(F32).astype(BF), grid)
    lane = lax.broadcasted_iota(jnp.int32, (CELLS, 2 * WIN), 1)
    ones = jnp.ones((2 * WIN, 128), BF)
    for w in range(2):
        own = jnp.where(lane == (cell & 15) + w * WIN, rows, 0.0).astype(BF)
        tis = nn(own, ones)
        some = jnp.max(jnp.max(tis, 0, keepdims=True), 1, keepdims=True)
        tis_ref[w] = tis.astype(BF)
        live_ref[w] = jnp.maximum(tis, 1.0 - some).astype(BF)
        db = cot_ref[:, w].reshape(CELLS, D) * jnp.tile(tis.astype(BF), (1, D // 128))
        db_ref[w] = db
        da_ref[w] = nt(db, wp_ref[...]).astype(BF)


def branch(cot, tissue, w_proj):
    shape = jax.ShapeDtypeStruct((2, CELLS, D), BF)
    mask = jax.ShapeDtypeStruct((2, CELLS, 128), BF)
    return pl.pallas_call(
        branch_kernel,
        out_shape=[shape, shape, mask, mask],
        compiler_params=pltpu.CompilerParams(vmem_limit_bytes=VMEM),
        cost_estimate=cost(6e8, 4e6),
        name="branch",
    )(cot, tissue, w_proj)


def row_order(first):
    gy = lax.axis_index("gy")
    dp, y, core, gx = lax.axis_index("dp"), gy >> 1, gy & 1, lax.axis_index("gx")
    at = lax.broadcasted_iota(jnp.int32, (D, 1), 0)
    third = ((at.astype(F32) + 0.5) * (1.0 / 3)).astype(jnp.int32)
    bit = [(third >> i) & 1 for i in range(8)]
    z_of = gx ^ (bit[0] * 4 + bit[1] * 2 + bit[2])
    distance = bit[6] * 2 + bit[5]
    partner = bit[4] ^ (bit[3] * 3)
    if first == "dp":
        dp_of, y_of = (distance + dp) & 3, partner ^ y
    else:
        dp_of, y_of = partner ^ dp, (distance + y) & 3
    core_of = bit[7] ^ core
    source = ((dp_of * 8 + y_of * 2 + core_of) * 8 + z_of) * 3 + at - third * 3
    column = lax.broadcasted_iota(jnp.int32, (D, D), 1)
    return jnp.where(column == source, 1.0, 0.0).astype(BF)


def moments(x):
    mean = jnp.mean(x, -1, keepdims=True)
    centred = x - mean
    inv = lax.rsqrt(jnp.mean(centred * centred, -1, keepdims=True) + 1e-05)
    return centred * inv, inv


def head_pair(q2, k2, v2, da2, ones2):
    lane = lax.broadcasted_iota(jnp.int32, (1, 128), 1)
    sel_a = (lane < 64).astype(BF)
    sel_b = (lane >= 64).astype(BF)
    ka, kb, va, vb = k2 * sel_a, k2 * sel_b, v2 * sel_a, v2 * sel_b
    wa = jnp.exp(nt(q2, ka)).astype(BF)
    wb = jnp.exp(nt(q2, kb)).astype(BF)
    both = nn(wa, jnp.concatenate([va, ones2 * sel_a], 1)) + nn(
        wb, jnp.concatenate([vb, ones2 * sel_b], 1)
    )
    rinv = 1.0 / both[:, 128:]
    attended = both[:, :128] * rinv
    lhs = jnp.concatenate([da2, (da2.astype(F32) * attended).astype(BF)], 1)
    minus_a = jnp.broadcast_to(-sel_a, (CELLS, 128))
    minus_b = jnp.broadcast_to(-sel_b, (CELLS, 128))
    dsa = (wa.astype(F32) * nt(lhs, jnp.concatenate([va, minus_a], 1))).astype(BF)
    dsb = (wb.astype(F32) * nt(lhs, jnp.concatenate([vb, minus_b], 1))).astype(BF)
    dq = (nn(dsa, ka) + nn(dsb, kb)) * (rinv * HEAD_SCALE)
    dan = (da2.astype(F32) * rinv).astype(BF)
    qn = (q2.astype(F32) * rinv).astype(BF)
    dv = tn(wa, dan * sel_a) + tn(wb, dan * sel_b)
    dk = tn(dsa, qn * sel_a) + tn(dsb, qn * sel_b)
    return attended.astype(BF), dq.astype(BF), dk.astype(BF), dv.astype(BF)


def put(grad, keep_ref, send_ref):
    keep_ref[...] = grad[: D // 2].astype(BF)
    send_ref[...] = grad[D // 2 :].astype(BF)


def heads_group(
    hid_ref, hid_t_ref, tis_ref, live_ref, wq_ref, wk_ref, wv_ref, da_ref,
    keep_ref, send_ref, att_ref, dqkv_ref,
):
    for w in range(2):
        hidden = hid_ref[w]
        query = nn(hidden, wq_ref[...]).astype(BF) * BF(HEAD_SCALE)
        tis2 = tis_ref[w]
        tis4 = jnp.concatenate([tis2, tis2], 1)
        key = nn(hidden, wk_ref[...]).astype(BF) * tis4
        value = nn(hidden, wv_ref[...]).astype(BF) * tis4
        for p in range(2):
            s = slice(p * 128, (p + 1) * 128)
            att, dq, dk, dv = head_pair(
                query[:, s], key[:, s], value[:, s], da_ref[w, :, s], live_ref[w]
            )
            att_ref[w, :, s] = att
            dqkv_ref[0, w, :, s] = dq
            dqkv_ref[0, w, :, slice(GW + p * 128, GW + (p + 1) * 128)] = dk * tis2
            dqkv_ref[0, w, :, slice(2 * GW + p * 128, 2 * GW + (p + 1) * 128)] = dv * tis2
    put(nn(hid_t_ref[...], dqkv_ref[0].reshape(2 * CELLS, D)), keep_ref, send_ref)


def first_kernel(
    tiles_ref, below_ref, right_ref, diag_ref, tis_ref, live_ref,
    wq_ref, wk_ref, wv_ref, da_ref,
    keep_ref, send_ref, att_ref, dqkv_ref, xw_ref, hid_ref, hid_t_ref,
):
    @pl.when(pl.program_id(0) == 0)
    def _():
        own = tiles_ref[8:16].astype(F32)
        low = below_ref[...].astype(F32)
        right = right_ref[...].astype(F32)
        diag = diag_ref[...].astype(F32)
        perm = row_order("dp")
        for w in range(2):
            if w == 0:
                top, bottom = own[:, 8:24], low[:, :16]
            else:
                top = jnp.concatenate([own[:, 24:32], right], 1)
                bottom = jnp.concatenate([low[:, 16:24], diag], 1)
            x = jnp.concatenate([top, bottom], 0).reshape(CELLS, D)
            xw_ref[w] = x.astype(BF)
            normed, _ = moments(x)
            hidden = normed.astype(BF)
            hid_ref[w] = hidden
            hid_t_ref[:, w * CELLS : (w + 1) * CELLS] = nt(perm, hidden).astype(BF)

    heads_group(
        hid_ref, hid_t_ref, tis_ref, live_ref, wq_ref, wk_ref, wv_ref, da_ref,
        keep_ref, send_ref, att_ref, dqkv_ref,
    )


def last_kernel(
    hid_ref, hid_t_ref, tis_ref, live_ref, wq_ref, wk_ref, wv_ref, da_ref,
    keep_ref, send_ref, att_ref, dqkv_ref,
):
    heads_group(
        hid_ref, hid_t_ref, tis_ref, live_ref, wq_ref, wk_ref, wv_ref, da_ref,
        keep_ref, send_ref, att_ref, dqkv_ref,
    )


def turn_kernel(hid_ref, hid_t_ref):
    hid_t_ref[...] = nt(row_order("gy"), hid_ref[...].reshape(2 * CELLS, D)).astype(BF)


def turn(hid):
    return pl.pallas_call(
        turn_kernel,
        out_shape=jax.ShapeDtypeStruct((D, 2 * CELLS), BF),
        compiler_params=pltpu.CompilerParams(vmem_limit_bytes=VMEM),
        cost_estimate=cost(2e9, 2e6),
        name="turn",
    )(hid)


def columns(block, first):
    return pl.BlockSpec((D, GW), lambda g: (0, block * GROUPS + first + g))


def heads_specs(first, groups):
    inputs = [
        full((2, CELLS, 128)), full((2, CELLS, 128)),
        columns(0, first), columns(1, first), columns(2, first),
        pl.BlockSpec((2, CELLS, GW), lambda g: (0, 0, first + g)),
    ]
    half = pl.BlockSpec((D // 2, D), lambda g: (0, g))
    outputs = [
        half, half,
        pl.BlockSpec((2, CELLS, GW), lambda g: (0, 0, g)),
        pl.BlockSpec((1, 2, CELLS, D), lambda g: (g, 0, 0, 0)),
    ]
    shapes = [
        jax.ShapeDtypeStruct((D // 2, groups * D), BF),
        jax.ShapeDtypeStruct((D // 2, groups * D), BF),
        jax.ShapeDtypeStruct((2, CELLS, groups * GW), BF),
        jax.ShapeDtypeStruct((groups, 2, CELLS, D), BF),
    ]
    return inputs, outputs, shapes


def first_heads(tiles, below, right, diag, tis, live, w_qkv, da):
    inputs, outputs, shapes = heads_specs(0, 2)
    rows = jax.ShapeDtypeStruct((2, CELLS, D), BF)
    return pl.pallas_call(
        first_kernel,
        grid=(2,),
        in_specs=[full((16, 32, D)), full((8, 24, D)), full((8, 8, D)), full((8, 8, D))] + inputs,
        out_specs=outputs + [full((2, CELLS, D))] * 2,
        out_shape=shapes + [rows, rows],
        scratch_shapes=[pltpu.VMEM((D, 2 * CELLS), BF)],
        compiler_params=pltpu.CompilerParams(vmem_limit_bytes=VMEM),
        cost_estimate=cost(6e9, 10e6),
        name="first_heads",
    )(tiles, below, right, diag, tis, live, w_qkv, w_qkv, w_qkv, da)


def last_heads(hid, hid_t, tis, live, w_qkv, da):
    inputs, outputs, shapes = heads_specs(2, 1)
    return pl.pallas_call(
        last_kernel,
        grid=(1,),
        in_specs=[full((2, CELLS, D)), full((D, 2 * CELLS))] + inputs,
        out_specs=outputs,
        out_shape=shapes,
        compiler_params=pltpu.CompilerParams(vmem_limit_bytes=VMEM),
        cost_estimate=cost(4e9, 6e6),
        name="last_heads",
    )(hid, hid_t, tis, live, w_qkv, w_qkv, w_qkv, da)


def proj_kernel(att0_ref, att1_ref, db_ref, keep_ref, send_ref):
    attended = jnp.concatenate([att0_ref[...], att1_ref[...]], 2).reshape(2 * CELLS, D)
    att_t = nt(row_order("gy"), attended).astype(BF)
    put(nn(att_t, db_ref[...].reshape(2 * CELLS, D)), keep_ref, send_ref)


def proj_grad(att0, att1, db):
    shape = jax.ShapeDtypeStruct((D // 2, D), BF)
    return pl.pallas_call(
        proj_kernel,
        out_shape=[shape, shape],
        compiler_params=pltpu.CompilerParams(vmem_limit_bytes=VMEM),
        cost_estimate=cost(2e9, 4e6),
        name="proj_grad",
    )(att0, att1, db)


def out_kernel(xw_ref, tis_ref, att0_ref, att1_ref, wp_ref, out_ref):
    for w in range(2):
        tis = jnp.tile(tis_ref[w].astype(F32), (1, D // 128))
        attended = jnp.concatenate([att0_ref[w], att1_ref[w]], 1)
        out = xw_ref[w].astype(F32) + tis * nn(attended, wp_ref[...])
        out_ref[:, w] = out.astype(BF).reshape(WIN, WIN, D)


def out_part(xw, tis, att0, att1, w_proj):
    out = pl.pallas_call(
        out_kernel,
        out_shape=jax.ShapeDtypeStruct((WIN, 2, WIN, D), BF),
        compiler_params=pltpu.CompilerParams(vmem_limit_bytes=VMEM),
        cost_estimate=cost(3e9, 5e6),
        name="out_part",
    )(xw, tis, att0, att1, w_proj)
    return out.reshape(1, WIN, 2 * WIN, D)


def grad_kernel(
    xw_ref, cot_ref, dqkv0_ref, dqkv1_ref, wq_ref, wk_ref, wv_ref, grad_ref, acc_ref
):
    step = pl.program_id(0)
    weights = jnp.concatenate([wq_ref[...], wk_ref[...], wv_ref[...]], 1)
    dqkv = jnp.where(step < GROUPS - 1, dqkv0_ref[0], dqkv1_ref[0])
    part = nt(dqkv.reshape(2 * CELLS, D), weights)

    @pl.when(step == 0)
    def _():
        acc_ref[...] = part

    @pl.when((step > 0) & (step < GROUPS - 1))
    def _():
        acc_ref[...] += part

    @pl.when(step == GROUPS - 1)
    def _():
        acc_ref[...] += part
        for w in range(2):
            normed, inv = moments(xw_ref[w].astype(F32))
            dh = acc_ref[w * CELLS : (w + 1) * CELLS]
            dnorm = inv * (
                dh
                - jnp.mean(dh, -1, keepdims=True)
                - normed * jnp.mean(dh * normed, -1, keepdims=True)
            )
            grad = cot_ref[:, w].reshape(CELLS, D).astype(F32) + dnorm
            grad_ref[:, w] = grad.astype(BF).reshape(WIN, WIN, D)


def grad_part(xw, cot, dqkv0, dqkv1, w_qkv):
    grad = pl.pallas_call(
        grad_kernel,
        grid=(GROUPS,),
        in_specs=[
            full((2, CELLS, D)), full((WIN, 2, WIN, D)),
            pl.BlockSpec((1, 2, CELLS, D), lambda g: (jnp.minimum(g, 1), 0, 0, 0)),
            full((1, 2, CELLS, D)),
            columns(0, 0), columns(1, 0), columns(2, 0),
        ],
        out_specs=full((WIN, 2, WIN, D)),
        out_shape=jax.ShapeDtypeStruct((WIN, 2, WIN, D), BF),
        scratch_shapes=[pltpu.VMEM((2 * CELLS, D), F32)],
        compiler_params=pltpu.CompilerParams(vmem_limit_bytes=VMEM),
        cost_estimate=cost(6e9, 10e6),
        name="grad_part",
    )(xw, cot, dqkv0, dqkv1, w_qkv, w_qkv, w_qkv)
    return grad.reshape(1, WIN, 2 * WIN, D)


def send(value, axis, move):
    devices = lax.axis_size(axis)
    return lax.ppermute(value, axis, [(i, move(i) % devices) for i in range(devices)])


def add(*terms):
    total = terms[0].astype(F32)
    for term in terms[1:]:
        total = total + term.astype(F32)
    return total.astype(BF)


def ring_start(low, high, axis, step):
    from_low = send(low[2], axis, lambda j: j + step)
    from_high = send(high[2], axis, lambda j: j - step)
    return from_low, from_high


def ring_pass(low, high, came, axis, step):
    up = jnp.concatenate([add(low[1], came[0]), high[1]], 1)
    down = jnp.concatenate([low[3], add(high[3], came[1])], 1)
    return send(up, axis, lambda j: j + step), send(down, axis, lambda j: j - step)


def ring_end(low, high, came):
    n = low.shape[2]
    up, down = came
    low = add(low[0], up[:, :n], down[:, :n])
    high = add(high[0], up[:, n:], down[:, n:])
    return jnp.concatenate([low, high], 1)


def halve_start(rows, axis, flip):
    return send(rows[rows.shape[0] // 2 :], axis, lambda j: j ^ flip)


def halve_end(rows, came):
    return add(rows[: rows.shape[0] // 2], came)


def tie(*values):
    return lax.optimization_barrier(values)


def blocks(value):
    return value.reshape(4, value.shape[0] // 4, value.shape[1])


def shards(tiles, cotangent, tissue, w_qkv, w_proj):
    mine = tiles[0]
    below = send(mine[:8, 8:], "gy", lambda i: i - 1)
    right = send(mine[8:, :8], "gx", lambda i: i - 1)
    ny, nx = lax.axis_size("gy"), lax.axis_size("gx")
    diag = lax.ppermute(
        mine[:8, :8],
        ("gy", "gx"),
        [
            (a * nx + b, (a - 1) % ny * nx + (b - 1) % nx)
            for a in range(ny)
            for b in range(nx)
        ],
    )
    cot = cotangent.reshape(WIN, 2, WIN, D)
    db, da, tis, live = branch(cot, tissue[0], w_proj)
    keep0, send0, att0, dqkv0, xw, hid = first_heads(
        mine, below, right, diag, tis, live, w_qkv, da
    )
    came = send(send0, "gy", lambda i: i ^ 1)
    hid_t = turn(hid)
    came, hid_t = tie(came, hid_t)
    first = add(keep0, came)
    low_a, high_a = blocks(first[:, :D]), blocks(first[:, D:])
    low_a, high_a, hid_t = tie(low_a, high_a, hid_t)
    came_a = ring_start(low_a, high_a, "dp", 1)
    keep1, send1, att1, dqkv1 = last_heads(hid, hid_t, tis, live, w_qkv, da)
    came_a, send1, att1 = tie(came_a, send1, att1)
    came_a = ring_pass(low_a, high_a, came_a, "dp", 1)
    came = send(send1, "gy", lambda i: i ^ 1)
    keep2, send2 = proj_grad(att0, att1, db)
    came, send2, keep2 = tie(came, send2, keep2)
    low_b = add(keep1, came)
    high_b = add(keep2, send(send2, "gy", lambda i: i ^ 1))
    low_b, high_b, att1 = tie(blocks(low_b), blocks(high_b), att1)
    came_b = ring_start(low_b, high_b, "gy", 2)
    out = out_part(xw, tis, att0, att1, w_proj)
    came_a, came_b, out, xw = tie(came_a, came_b, out, xw)
    rows_a = ring_end(low_a, high_a, came_a)
    came_b = ring_pass(low_b, high_b, came_b, "gy", 2)
    came_a = halve_start(rows_a, "gy", 2)
    grad = grad_part(xw, cot, dqkv0, dqkv1, w_qkv)
    came_a, came_b, grad = tie(came_a, came_b, grad)
    rows_a = halve_end(rows_a, came_a)
    rows_b = ring_end(low_b, high_b, came_b)
    came_a = halve_start(rows_a, "gy", 6)
    came_b = halve_start(rows_b, "dp", 1)
    rows_b = halve_end(rows_b, came_b)
    came_b = halve_start(rows_b, "dp", 3)
    rows = jnp.concatenate([halve_end(rows_a, came_a), halve_end(rows_b, came_b)], 1)
    for flip in (1, 2):
        rows = halve_end(rows, halve_start(rows, "gx", flip))
    came = halve_start(rows, "gx", 4)
    total = (rows[:3].astype(F32) + came.astype(F32)) * (1.0 / math.sqrt(512))
    grad_qkv = total[:, : 3 * D].reshape(3, GROUPS, 3, GW).transpose(0, 2, 1, 3)
    return out, grad, grad_qkv.reshape(3, 3 * D), total[:, 3 * D :]


def solution(mesh):
    block = P("dp", "gy", "gx", None)
    in_specs = (block, block, P("dp", "gy", "gx"), P(), P())
    out_specs = (block, block, P(("dp", "gy", "gx"), None), P(("dp", "gy", "gx"), None))
    return jax.shard_map(
        shards, mesh=mesh, in_specs=in_specs, out_specs=out_specs, check_vma=False
    )
```

```python
import math

import jax
import jax.numpy as jnp
from jax import lax
from jax.experimental import pallas as pl
from jax.experimental.pallas import tpu as pltpu
from jax.sharding import PartitionSpec as P

F32 = jnp.float32
BF = jnp.bfloat16
D = 768
WIN = 16
CELLS = WIN * WIN
GROUPS = 3
GW = D // GROUPS
HEAD_SCALE = 0.125
VMEM = 32 * 1024 * 1024


def nn(a, b):
    return lax.dot_general(a, b, (((1,), (0,)), ((), ())), preferred_element_type=F32)


def nt(a, b):
    return lax.dot_general(a, b, (((1,), (1,)), ((), ())), preferred_element_type=F32)


def tn(a, b):
    return lax.dot_general(a, b, (((0,), (0,)), ((), ())), preferred_element_type=F32)


def full(shape):
    return pl.BlockSpec(shape, lambda *g: (0,) * len(shape))


def cost(flops, size):
    return pl.CostEstimate(flops=int(flops), bytes_accessed=int(size), transcendentals=0)


def branch_kernel(
    cot_hbm, tissue_hbm, wp_hbm, db_ref, da_ref, tis_ref, live_ref, cot_ref, tissue_ref, wp_ref, sem
):
    copies = [
        pltpu.make_async_copy(tissue_hbm, tissue_ref, sem.at[0]),
        pltpu.make_async_copy(cot_hbm, cot_ref, sem.at[1]),
        pltpu.make_async_copy(wp_hbm, wp_ref, sem.at[2]),
    ]
    for copy in copies:
        copy.start()
    copies[0].wait()
    grid = tissue_ref[...].astype(F32).astype(BF)
    cell = lax.broadcasted_iota(jnp.int32, (CELLS, 1), 0)
    row_of = lax.broadcasted_iota(jnp.int32, (CELLS, WIN), 1) == (cell >> 4)
    rows = nn(row_of.astype(F32).astype(BF), grid)
    lane = lax.broadcasted_iota(jnp.int32, (CELLS, 2 * WIN), 1)
    ones = jnp.ones((2 * WIN, 128), BF)
    copies[1].wait()
    copies[2].wait()
    for w in range(2):
        own = jnp.where(lane == (cell & 15) + w * WIN, rows, 0.0).astype(BF)
        tis = nn(own, ones)
        some = jnp.max(jnp.max(tis, 0, keepdims=True), 1, keepdims=True)
        tis_ref[w] = tis.astype(BF)
        live_ref[w] = jnp.maximum(tis, 1.0 - some).astype(BF)
        db = cot_ref[:, w].reshape(CELLS, D) * jnp.tile(tis.astype(BF), (1, D // 128))
        db_ref[w] = db
        da_ref[w] = nt(db, wp_ref[...]).astype(BF)


def branch(cot, tissue, w_proj):
    shape = jax.ShapeDtypeStruct((2, CELLS, D), BF)
    mask = jax.ShapeDtypeStruct((2, CELLS, 128), BF)
    return pl.pallas_call(
        branch_kernel,
        in_specs=[pl.BlockSpec(memory_space=pltpu.HBM)] * 3,
        out_shape=[shape, shape, mask, mask],
        scratch_shapes=[
            pltpu.VMEM((WIN, 2, WIN, D), BF),
            pltpu.VMEM((WIN, 2 * WIN), jnp.int32),
            pltpu.VMEM((D, D), BF),
            pltpu.SemaphoreType.DMA((3,)),
        ],
        compiler_params=pltpu.CompilerParams(vmem_limit_bytes=VMEM),
        cost_estimate=cost(2e10, 4e6),
        name="branch",
    )(cot, tissue, w_proj)


def row_order(first):
    gy = lax.axis_index("gy")
    dp, y, core, gx = lax.axis_index("dp"), gy >> 1, gy & 1, lax.axis_index("gx")
    at = lax.broadcasted_iota(jnp.int32, (D, 1), 0)
    third = ((at.astype(F32) + 0.5) * (1.0 / 3)).astype(jnp.int32)
    outer, inner, depth = (third >> 5) & 3, (third >> 3) & 3, third & 7
    if first == "dp":
        dp_of = (outer + dp) & 3
        y_of = ((inner >> 1) ^ ((inner & 1) * 3)) ^ y
        z_of = (depth + gx) & 7
    else:
        dp_of, y_of, z_of = inner, outer, depth
    core_of = (third >> 7) ^ core
    source = ((dp_of * 8 + y_of * 2 + core_of) * 8 + z_of) * 3 + at - third * 3
    column = lax.broadcasted_iota(jnp.int32, (D, D), 1)
    return jnp.where(column == source, 1.0, 0.0).astype(BF)


def moments(x):
    mean = jnp.mean(x, -1, keepdims=True)
    centred = x - mean
    inv = lax.rsqrt(jnp.mean(centred * centred, -1, keepdims=True) + 1e-05)
    return centred * inv, inv


def head_pair(q2, k2, v2, da2, ones2):
    lane = lax.broadcasted_iota(jnp.int32, (1, 128), 1)
    sel_a = (lane < 64).astype(BF)
    sel_b = (lane >= 64).astype(BF)
    ka, kb, va, vb = k2 * sel_a, k2 * sel_b, v2 * sel_a, v2 * sel_b
    wa = jnp.exp(nt(q2, ka)).astype(BF)
    wb = jnp.exp(nt(q2, kb)).astype(BF)
    both = nn(wa, jnp.concatenate([va, ones2 * sel_a], 1)) + nn(
        wb, jnp.concatenate([vb, ones2 * sel_b], 1)
    )
    rinv = 1.0 / both[:, 128:]
    attended = both[:, :128] * rinv
    lhs = jnp.concatenate([da2, (da2.astype(F32) * attended).astype(BF)], 1)
    minus_a = jnp.broadcast_to(-sel_a, (CELLS, 128))
    minus_b = jnp.broadcast_to(-sel_b, (CELLS, 128))
    dsa = (wa.astype(F32) * nt(lhs, jnp.concatenate([va, minus_a], 1))).astype(BF)
    dsb = (wb.astype(F32) * nt(lhs, jnp.concatenate([vb, minus_b], 1))).astype(BF)
    dq = (nn(dsa, ka) + nn(dsb, kb)) * (rinv * HEAD_SCALE)
    dan = (da2.astype(F32) * rinv).astype(BF)
    qn = (q2.astype(F32) * rinv).astype(BF)
    dv = tn(wa, dan * sel_a) + tn(wb, dan * sel_b)
    dk = tn(dsa, qn * sel_a) + tn(dsb, qn * sel_b)
    return attended.astype(BF), dq.astype(BF), dk.astype(BF), dv.astype(BF)


def put(grad, keep_ref, send_ref):
    keep_ref[...] = grad[: D // 2].astype(BF)
    send_ref[...] = grad[D // 2 :].astype(BF)


def heads_group(
    hid_ref, hid_t_ref, tis_ref, live_ref, wq_ref, wk_ref, wv_ref, da_ref,
    keep_ref, send_ref, att_ref, dqkv_ref,
):
    for w in range(2):
        hidden = hid_ref[w]
        query = nn(hidden, wq_ref[...]).astype(BF) * BF(HEAD_SCALE)
        tis2 = tis_ref[w]
        tis4 = jnp.concatenate([tis2, tis2], 1)
        key = nn(hidden, wk_ref[...]).astype(BF) * tis4
        value = nn(hidden, wv_ref[...]).astype(BF) * tis4
        for p in range(2):
            s = slice(p * 128, (p + 1) * 128)
            att, dq, dk, dv = head_pair(
                query[:, s], key[:, s], value[:, s], da_ref[w, :, s], live_ref[w]
            )
            att_ref[w, :, s] = att
            dqkv_ref[0, w, :, s] = dq
            dqkv_ref[0, w, :, slice(GW + p * 128, GW + (p + 1) * 128)] = dk * tis2
            dqkv_ref[0, w, :, slice(2 * GW + p * 128, 2 * GW + (p + 1) * 128)] = dv * tis2
    put(nn(hid_t_ref[...], dqkv_ref[0].reshape(2 * CELLS, D)), keep_ref, send_ref)


def first_kernel(
    tiles_ref, below_ref, right_ref, diag_ref, tis_ref, live_ref,
    wq_ref, wk_ref, wv_ref, da_ref,
    keep_ref, send_ref, att_ref, dqkv_ref, xw_ref, hid_ref, hid_t_ref,
):
    @pl.when(pl.program_id(0) == 0)
    def _():
        own = tiles_ref[8:16].astype(F32)
        low = below_ref[...].astype(F32)
        right = right_ref[...].astype(F32)
        diag = diag_ref[...].astype(F32)
        perm = row_order("dp")
        for w in range(2):
            if w == 0:
                top, bottom = own[:, 8:24], low[:, :16]
            else:
                top = jnp.concatenate([own[:, 24:32], right], 1)
                bottom = jnp.concatenate([low[:, 16:24], diag], 1)
            x = jnp.concatenate([top, bottom], 0).reshape(CELLS, D)
            xw_ref[w] = x.astype(BF)
            normed, _ = moments(x)
            hidden = normed.astype(BF)
            hid_ref[w] = hidden
            hid_t_ref[:, w * CELLS : (w + 1) * CELLS] = nt(perm, hidden).astype(BF)

    heads_group(
        hid_ref, hid_t_ref, tis_ref, live_ref, wq_ref, wk_ref, wv_ref, da_ref,
        keep_ref, send_ref, att_ref, dqkv_ref,
    )


def last_kernel(
    hid_ref, hid_t_ref, tis_ref, live_ref, wq_ref, wk_ref, wv_ref, da_ref,
    keep_ref, send_ref, att_ref, dqkv_ref,
):
    heads_group(
        hid_ref, hid_t_ref, tis_ref, live_ref, wq_ref, wk_ref, wv_ref, da_ref,
        keep_ref, send_ref, att_ref, dqkv_ref,
    )


def turn_kernel(hid_ref, hid_t_ref):
    hid_t_ref[...] = nt(row_order("gy"), hid_ref[...].reshape(2 * CELLS, D)).astype(BF)


def turn(hid):
    return pl.pallas_call(
        turn_kernel,
        out_shape=jax.ShapeDtypeStruct((D, 2 * CELLS), BF),
        compiler_params=pltpu.CompilerParams(vmem_limit_bytes=VMEM),
        cost_estimate=cost(2e9, 2e6),
        name="turn",
    )(hid)


def columns(block, first):
    return pl.BlockSpec((D, GW), lambda g: (0, block * GROUPS + first + g))


def heads_specs(first, groups):
    inputs = [
        full((2, CELLS, 128)), full((2, CELLS, 128)),
        columns(0, first), columns(1, first), columns(2, first),
        pl.BlockSpec((2, CELLS, GW), lambda g: (0, 0, first + g)),
    ]
    half = pl.BlockSpec((D // 2, D), lambda g: (0, g))
    outputs = [
        half, half,
        pl.BlockSpec((2, CELLS, GW), lambda g: (0, 0, g)),
        pl.BlockSpec((1, 2, CELLS, D), lambda g: (g, 0, 0, 0)),
    ]
    shapes = [
        jax.ShapeDtypeStruct((D // 2, groups * D), BF),
        jax.ShapeDtypeStruct((D // 2, groups * D), BF),
        jax.ShapeDtypeStruct((2, CELLS, groups * GW), BF),
        jax.ShapeDtypeStruct((groups, 2, CELLS, D), BF),
    ]
    return inputs, outputs, shapes


def first_heads(tiles, below, right, diag, tis, live, w_qkv, da):
    inputs, outputs, shapes = heads_specs(0, 2)
    rows = jax.ShapeDtypeStruct((2, CELLS, D), BF)
    return pl.pallas_call(
        first_kernel,
        grid=(2,),
        in_specs=[full((16, 32, D)), full((8, 24, D)), full((8, 8, D)), full((8, 8, D))] + inputs,
        out_specs=outputs + [full((2, CELLS, D))] * 2,
        out_shape=shapes + [rows, rows],
        scratch_shapes=[pltpu.VMEM((D, 2 * CELLS), BF)],
        compiler_params=pltpu.CompilerParams(vmem_limit_bytes=VMEM),
        cost_estimate=cost(6e9, 10e6),
        name="first_heads",
    )(tiles, below, right, diag, tis, live, w_qkv, w_qkv, w_qkv, da)


def last_heads(hid, hid_t, tis, live, w_qkv, da):
    inputs, outputs, shapes = heads_specs(2, 1)
    return pl.pallas_call(
        last_kernel,
        grid=(1,),
        in_specs=[full((2, CELLS, D)), full((D, 2 * CELLS))] + inputs,
        out_specs=outputs,
        out_shape=shapes,
        compiler_params=pltpu.CompilerParams(vmem_limit_bytes=VMEM),
        cost_estimate=cost(4e9, 6e6),
        name="last_heads",
    )(hid, hid_t, tis, live, w_qkv, w_qkv, w_qkv, da)


def proj_kernel(att0_ref, att1_ref, db_ref, keep_ref, send_ref):
    attended = jnp.concatenate([att0_ref[...], att1_ref[...]], 2).reshape(2 * CELLS, D)
    att_t = nt(row_order("gy"), attended).astype(BF)
    put(nn(att_t, db_ref[...].reshape(2 * CELLS, D)), keep_ref, send_ref)


def proj_grad(att0, att1, db):
    shape = jax.ShapeDtypeStruct((D // 2, D), BF)
    return pl.pallas_call(
        proj_kernel,
        out_shape=[shape, shape],
        compiler_params=pltpu.CompilerParams(vmem_limit_bytes=VMEM),
        cost_estimate=cost(2e9, 4e6),
        name="proj_grad",
    )(att0, att1, db)


def out_kernel(xw_ref, tis_ref, att0_ref, att1_ref, wp_ref, out_ref):
    for w in range(2):
        tis = jnp.tile(tis_ref[w].astype(F32), (1, D // 128))
        attended = jnp.concatenate([att0_ref[w], att1_ref[w]], 1)
        out = xw_ref[w].astype(F32) + tis * nn(attended, wp_ref[...])
        out_ref[:, w] = out.astype(BF).reshape(WIN, WIN, D)


def out_part(xw, tis, att0, att1, w_proj):
    out = pl.pallas_call(
        out_kernel,
        out_shape=jax.ShapeDtypeStruct((WIN, 2, WIN, D), BF),
        compiler_params=pltpu.CompilerParams(vmem_limit_bytes=VMEM),
        cost_estimate=cost(1e3, 1e3),
        name="out_part",
    )(xw, tis, att0, att1, w_proj)
    return out.reshape(1, WIN, 2 * WIN, D)


def grad_kernel(
    xw_ref, cot_ref, dqkv0_ref, dqkv1_ref, wq_ref, wk_ref, wv_ref, grad_ref, acc_ref
):
    step = pl.program_id(0)
    weights = jnp.concatenate([wq_ref[...], wk_ref[...], wv_ref[...]], 1)
    dqkv = jnp.where(step < GROUPS - 1, dqkv0_ref[0], dqkv1_ref[0])
    part = nt(dqkv.reshape(2 * CELLS, D), weights)

    @pl.when(step == 0)
    def _():
        acc_ref[...] = part

    @pl.when((step > 0) & (step < GROUPS - 1))
    def _():
        acc_ref[...] += part

    @pl.when(step == GROUPS - 1)
    def _():
        acc_ref[...] += part
        for w in range(2):
            normed, inv = moments(xw_ref[w].astype(F32))
            dh = acc_ref[w * CELLS : (w + 1) * CELLS]
            dnorm = inv * (
                dh
                - jnp.mean(dh, -1, keepdims=True)
                - normed * jnp.mean(dh * normed, -1, keepdims=True)
            )
            grad = cot_ref[:, w].reshape(CELLS, D).astype(F32) + dnorm
            grad_ref[:, w] = grad.astype(BF).reshape(WIN, WIN, D)


def grad_part(xw, cot, dqkv0, dqkv1, w_qkv):
    grad = pl.pallas_call(
        grad_kernel,
        grid=(GROUPS,),
        in_specs=[
            full((2, CELLS, D)), full((WIN, 2, WIN, D)),
            pl.BlockSpec((1, 2, CELLS, D), lambda g: (jnp.minimum(g, 1), 0, 0, 0)),
            full((1, 2, CELLS, D)),
            columns(0, 0), columns(1, 0), columns(2, 0),
        ],
        out_specs=full((WIN, 2, WIN, D)),
        out_shape=jax.ShapeDtypeStruct((WIN, 2, WIN, D), BF),
        scratch_shapes=[pltpu.VMEM((2 * CELLS, D), F32)],
        compiler_params=pltpu.CompilerParams(vmem_limit_bytes=VMEM),
        cost_estimate=cost(1e3, 1e3),
        name="grad_part",
    )(xw, cot, dqkv0, dqkv1, w_qkv, w_qkv, w_qkv)
    return grad.reshape(1, WIN, 2 * WIN, D)


def send(value, axis, move):
    devices = lax.axis_size(axis)
    return lax.ppermute(value, axis, [(i, move(i) % devices) for i in range(devices)])


def add(*terms):
    total = terms[0].astype(F32)
    for term in terms[1:]:
        total = total + term.astype(F32)
    return total.astype(BF)


def ring_start(low, high, axis, step):
    from_low = send(low[2], axis, lambda j: j + step)
    from_high = send(high[2], axis, lambda j: j - step)
    return from_low, from_high


def ring_pass(low, high, came, axis, step):
    up = jnp.concatenate([add(low[1], came[0]), high[1]], 1)
    down = jnp.concatenate([low[3], add(high[3], came[1])], 1)
    return send(up, axis, lambda j: j + step), send(down, axis, lambda j: j - step)


def ring_end(low, high, came):
    n = low.shape[2]
    up, down = came
    low = add(low[0], up[:, :n], down[:, :n])
    high = add(high[0], up[:, n:], down[:, n:])
    return jnp.concatenate([low, high], 1)


def halve_start(rows, axis, flip):
    return send(rows[rows.shape[0] // 2 :], axis, lambda j: j ^ flip)


def halve_end(rows, came):
    return add(rows[: rows.shape[0] // 2], came)


def exchange(rows, axis, groups=None):
    parts = len(groups[0]) if groups else math.prod(lax.axis_size(a) for a in axis)
    rows = rows.reshape(parts, rows.shape[0] // parts, rows.shape[1])
    return lax.all_to_all(rows, axis, 0, 0, axis_index_groups=groups)


def tie(*values):
    return lax.optimization_barrier(values)


def blocks(value):
    return value.reshape(4, value.shape[0] // 4, value.shape[1])


def shards(tiles, cotangent, tissue, w_qkv, w_proj):
    mine = tiles[0]
    below = send(mine[:8, 8:], "gy", lambda i: i - 1)
    right = send(mine[8:, :8], "gx", lambda i: i - 1)
    ny, nx = lax.axis_size("gy"), lax.axis_size("gx")
    diag = lax.ppermute(
        mine[:8, :8],
        ("gy", "gx"),
        [
            (a * nx + b, (a - 1) % ny * nx + (b - 1) % nx)
            for a in range(ny)
            for b in range(nx)
        ],
    )
    cot = cotangent.reshape(WIN, 2, WIN, D)
    db, da, tis, live = branch(cot, tissue[0], w_proj)
    keep0, send0, att0, dqkv0, xw, hid = first_heads(
        mine, below, right, diag, tis, live, w_qkv, da
    )
    came = send(send0, "gy", lambda i: i ^ 1)
    hid_t = turn(hid)
    came, hid_t = tie(came, hid_t)
    first = add(keep0, came)
    low_a, high_a = blocks(first[:, :D]), blocks(first[:, D:])
    low_a, high_a, hid_t = tie(low_a, high_a, hid_t)
    came_a = ring_start(low_a, high_a, "dp", 1)
    keep1, send1, att1, dqkv1 = last_heads(hid, hid_t, tis, live, w_qkv, da)
    came_a, send1, att1 = tie(came_a, send1, att1)
    came_a = ring_pass(low_a, high_a, came_a, "dp", 1)
    came = send(send1, "gy", lambda i: i ^ 1)
    keep2, send2 = proj_grad(att0, att1, db)
    came, send2, keep2 = tie(came, send2, keep2)
    rows_b = jnp.concatenate([add(keep1, came), add(keep2, send(send2, "gy", lambda i: i ^ 1))], 1)
    rows_b, att1 = tie(rows_b, att1)
    same_core = [[0, 2, 4, 6], [1, 3, 5, 7]]
    parts_b = exchange(rows_b, "gy", same_core)
    out = out_part(xw, tis, att0, att1, w_proj)
    rows_a = ring_end(low_a, high_a, came_a)
    came_a = halve_start(rows_a, "gy", 2)
    grad = grad_part(xw, cot, dqkv0, dqkv1, w_qkv)
    came_a, out, grad, parts_b = tie(came_a, out, grad, parts_b)
    rows_a = halve_end(rows_a, came_a)
    rows_a = halve_end(rows_a, halve_start(rows_a, "gy", 6))
    rows_b, rows_a = tie(add(*parts_b), rows_a)
    parts_b = exchange(rows_b, ("dp", "gx"))
    rows_a = rows_a.reshape(8, 3, -1)
    total_a = rows_a[0].astype(F32)
    for d in range(1, 8):
        total_a = total_a + send(rows_a[d], "gx", lambda j: j + d).astype(F32)
    scale = 1.0 / math.sqrt(512)
    total_b = jnp.sum(parts_b.astype(F32), 0) * scale
    total = jnp.concatenate([total_a * scale, total_b[:, :D]], 1)
    grad_qkv = total.reshape(3, GROUPS, 3, GW).transpose(0, 2, 1, 3)
    return out, grad, grad_qkv.reshape(3, 3 * D), total_b[:, D:]


def solution(mesh):
    block = P("dp", "gy", "gx", None)
    in_specs = (block, block, P("dp", "gy", "gx"), P(), P())
    out_specs = (block, block, P(("dp", "gy", "gx"), None), P(("dp", "gy", "gx"), None))
    return jax.shard_map(
        shards, mesh=mesh, in_specs=in_specs, out_specs=out_specs, check_vma=False
    )
```

```python
import math

import jax
import jax.numpy as jnp
from jax import lax
from jax.experimental import pallas as pl
from jax.experimental.pallas import tpu as pltpu
from jax.sharding import PartitionSpec as P

F32 = jnp.float32
BF = jnp.bfloat16
D = 768
WIN = 16
CELLS = WIN * WIN
GROUPS = 3
GW = D // GROUPS
HEAD_SCALE = 0.125
VMEM = 32 * 1024 * 1024


def nn(a, b):
    return lax.dot_general(a, b, (((1,), (0,)), ((), ())), preferred_element_type=F32)


def nt(a, b):
    return lax.dot_general(a, b, (((1,), (1,)), ((), ())), preferred_element_type=F32)


def tn(a, b):
    return lax.dot_general(a, b, (((0,), (0,)), ((), ())), preferred_element_type=F32)


def full(shape):
    return pl.BlockSpec(shape, lambda *g: (0,) * len(shape))


def cost(flops, size):
    return pl.CostEstimate(flops=int(flops), bytes_accessed=int(size), transcendentals=0)


def edges_kernel(tiles, above, left, corner, sem):
    copies = [
        pltpu.make_async_copy(tiles.at[0:8, 8:32], above, sem.at[0]),
        pltpu.make_async_copy(tiles.at[8:16, 0:8], left, sem.at[1]),
        pltpu.make_async_copy(tiles.at[0:8, 0:8], corner, sem.at[2]),
    ]
    for copy in copies:
        copy.start()
    for copy in copies:
        copy.wait()


def edges(tiles):
    small = jax.ShapeDtypeStruct((8, 8, D), BF)
    return pl.pallas_call(
        edges_kernel,
        in_specs=[pl.BlockSpec(memory_space=pl.ANY)],
        out_specs=[pl.BlockSpec(memory_space=pl.ANY)] * 3,
        out_shape=[jax.ShapeDtypeStruct((8, 24, D), BF), small, small],
        scratch_shapes=[pltpu.SemaphoreType.DMA((3,))],
        compiler_params=pltpu.CompilerParams(vmem_limit_bytes=VMEM),
        cost_estimate=cost(3e10, 1e6),
        name="edges",
    )(tiles)


def branch_kernel(
    cot_hbm, tissue_hbm, wp_hbm, db_ref, da_ref, tis_ref, live_ref, cot_ref, tissue_ref, wp_ref, sem
):
    copies = [
        pltpu.make_async_copy(tissue_hbm, tissue_ref, sem.at[0]),
        pltpu.make_async_copy(cot_hbm, cot_ref, sem.at[1]),
        pltpu.make_async_copy(wp_hbm, wp_ref, sem.at[2]),
    ]
    for copy in copies:
        copy.start()
    copies[0].wait()
    grid = tissue_ref[...].astype(F32).astype(BF)
    cell = lax.broadcasted_iota(jnp.int32, (CELLS, 1), 0)
    row_of = lax.broadcasted_iota(jnp.int32, (CELLS, WIN), 1) == (cell >> 4)
    rows = nn(row_of.astype(F32).astype(BF), grid)
    lane = lax.broadcasted_iota(jnp.int32, (CELLS, 2 * WIN), 1)
    ones = jnp.ones((2 * WIN, 128), BF)
    copies[1].wait()
    copies[2].wait()
    for w in range(2):
        own = jnp.where(lane == (cell & 15) + w * WIN, rows, 0.0).astype(BF)
        tis = nn(own, ones)
        some = jnp.max(jnp.max(tis, 0, keepdims=True), 1, keepdims=True)
        tis_ref[w] = tis.astype(BF)
        live_ref[w] = jnp.maximum(tis, 1.0 - some).astype(BF)
        db = cot_ref[:, w].reshape(CELLS, D) * jnp.tile(tis.astype(BF), (1, D // 128))
        db_ref[w] = db
        da_ref[w] = nt(db, wp_ref[...]).astype(BF)


def branch(cot, tissue, w_proj):
    shape = jax.ShapeDtypeStruct((2, CELLS, D), BF)
    mask = jax.ShapeDtypeStruct((2, CELLS, 128), BF)
    return pl.pallas_call(
        branch_kernel,
        in_specs=[pl.BlockSpec(memory_space=pltpu.HBM)] * 3,
        out_shape=[shape, shape, mask, mask],
        scratch_shapes=[
            pltpu.VMEM((WIN, 2, WIN, D), BF),
            pltpu.VMEM((WIN, 2 * WIN), jnp.int32),
            pltpu.VMEM((D, D), BF),
            pltpu.SemaphoreType.DMA((3,)),
        ],
        compiler_params=pltpu.CompilerParams(vmem_limit_bytes=VMEM),
        cost_estimate=cost(2e10, 4e6),
        name="branch",
    )(cot, tissue, w_proj)


def row_order(permutes):
    gy = lax.axis_index("gy")
    dp, y, core = lax.axis_index("dp"), gy >> 1, gy & 1
    at = lax.broadcasted_iota(jnp.int32, (D, 1), 0)
    third = ((at.astype(F32) + 0.5) * (1.0 / 3)).astype(jnp.int32)
    outer, inner, depth = (third >> 5) & 3, (third >> 3) & 3, third & 7
    if permutes:
        dp_of = (outer + dp) & 3
        y_of = ((inner >> 1) ^ ((inner & 1) * 3)) ^ y
    else:
        dp_of, y_of = outer, inner
    core_of = (third >> 7) ^ core
    source = ((dp_of * 8 + y_of * 2 + core_of) * 8 + depth) * 3 + at - third * 3
    column = lax.broadcasted_iota(jnp.int32, (D, D), 1)
    return jnp.where(column == source, 1.0, 0.0).astype(BF)


def moments(x):
    mean = jnp.mean(x, -1, keepdims=True)
    centred = x - mean
    inv = lax.rsqrt(jnp.mean(centred * centred, -1, keepdims=True) + 1e-05)
    return centred * inv, inv


def head_pair(q2, k2, v2, da2, ones2):
    lane = lax.broadcasted_iota(jnp.int32, (1, 128), 1)
    sel_a = (lane < 64).astype(BF)
    sel_b = (lane >= 64).astype(BF)
    ka, kb, va, vb = k2 * sel_a, k2 * sel_b, v2 * sel_a, v2 * sel_b
    wa = jnp.exp(nt(q2, ka)).astype(BF)
    wb = jnp.exp(nt(q2, kb)).astype(BF)
    both = nn(wa, jnp.concatenate([va, ones2 * sel_a], 1)) + nn(
        wb, jnp.concatenate([vb, ones2 * sel_b], 1)
    )
    rinv = 1.0 / both[:, 128:]
    attended = both[:, :128] * rinv
    lhs = jnp.concatenate([da2, (da2.astype(F32) * attended).astype(BF)], 1)
    minus_a = jnp.broadcast_to(-sel_a, (CELLS, 128))
    minus_b = jnp.broadcast_to(-sel_b, (CELLS, 128))
    dsa = (wa.astype(F32) * nt(lhs, jnp.concatenate([va, minus_a], 1))).astype(BF)
    dsb = (wb.astype(F32) * nt(lhs, jnp.concatenate([vb, minus_b], 1))).astype(BF)
    dq = (nn(dsa, ka) + nn(dsb, kb)) * (rinv * HEAD_SCALE)
    dan = (da2.astype(F32) * rinv).astype(BF)
    qn = (q2.astype(F32) * rinv).astype(BF)
    dv = tn(wa, dan * sel_a) + tn(wb, dan * sel_b)
    dk = tn(dsa, qn * sel_a) + tn(dsb, qn * sel_b)
    return attended.astype(BF), dq.astype(BF), dk.astype(BF), dv.astype(BF)


def put(grad, keep_ref, send_ref):
    keep_ref[...] = grad[: D // 2].astype(BF)
    send_ref[...] = grad[D // 2 :].astype(BF)


def heads_group(
    hid_ref, hid_t_ref, tis_ref, live_ref, wq_ref, wk_ref, wv_ref, da_ref,
    keep_ref, send_ref, att_ref, dqkv_ref,
):
    for w in range(2):
        hidden = hid_ref[w]
        query = nn(hidden, wq_ref[...]).astype(BF) * BF(HEAD_SCALE)
        tis2 = tis_ref[w]
        tis4 = jnp.concatenate([tis2, tis2], 1)
        key = nn(hidden, wk_ref[...]).astype(BF) * tis4
        value = nn(hidden, wv_ref[...]).astype(BF) * tis4
        for p in range(2):
            s = slice(p * 128, (p + 1) * 128)
            att, dq, dk, dv = head_pair(
                query[:, s], key[:, s], value[:, s], da_ref[w, :, s], live_ref[w]
            )
            att_ref[w, :, s] = att
            dqkv_ref[0, w, :, s] = dq
            dqkv_ref[0, w, :, slice(GW + p * 128, GW + (p + 1) * 128)] = dk * tis2
            dqkv_ref[0, w, :, slice(2 * GW + p * 128, 2 * GW + (p + 1) * 128)] = dv * tis2
    put(nn(hid_t_ref[...], dqkv_ref[0].reshape(2 * CELLS, D)), keep_ref, send_ref)


def first_kernel(
    tiles_ref, below_ref, right_ref, diag_ref, tis_ref, live_ref,
    wq_ref, wk_ref, wv_ref, da_ref,
    keep_ref, send_ref, att_ref, dqkv_ref, xw_ref, hid_ref, hid_t_ref,
):
    @pl.when(pl.program_id(0) == 0)
    def _():
        own = tiles_ref[8:16].astype(F32)
        low = below_ref[...].astype(F32)
        right = right_ref[...].astype(F32)
        diag = diag_ref[...].astype(F32)
        perm = row_order(True)
        for w in range(2):
            if w == 0:
                top, bottom = own[:, 8:24], low[:, :16]
            else:
                top = jnp.concatenate([own[:, 24:32], right], 1)
                bottom = jnp.concatenate([low[:, 16:24], diag], 1)
            x = jnp.concatenate([top, bottom], 0).reshape(CELLS, D)
            xw_ref[w] = x.astype(BF)
            normed, _ = moments(x)
            hidden = normed.astype(BF)
            hid_ref[w] = hidden
            hid_t_ref[:, w * CELLS : (w + 1) * CELLS] = nt(perm, hidden).astype(BF)

    heads_group(
        hid_ref, hid_t_ref, tis_ref, live_ref, wq_ref, wk_ref, wv_ref, da_ref,
        keep_ref, send_ref, att_ref, dqkv_ref,
    )


def last_kernel(
    hid_ref, hid_t_ref, tis_ref, live_ref, wq_ref, wk_ref, wv_ref, da_ref,
    keep_ref, send_ref, att_ref, dqkv_ref,
):
    heads_group(
        hid_ref, hid_t_ref, tis_ref, live_ref, wq_ref, wk_ref, wv_ref, da_ref,
        keep_ref, send_ref, att_ref, dqkv_ref,
    )


def turn_kernel(hid_ref, hid_t_ref):
    hid_t_ref[...] = nt(row_order(False), hid_ref[...].reshape(2 * CELLS, D)).astype(BF)


def turn(hid):
    return pl.pallas_call(
        turn_kernel,
        out_shape=jax.ShapeDtypeStruct((D, 2 * CELLS), BF),
        compiler_params=pltpu.CompilerParams(vmem_limit_bytes=VMEM),
        cost_estimate=cost(2e9, 2e6),
        name="turn",
    )(hid)


def columns(block, first):
    return pl.BlockSpec((D, GW), lambda g: (0, block * GROUPS + first + g))


def heads_specs(first, groups):
    inputs = [
        full((2, CELLS, 128)), full((2, CELLS, 128)),
        columns(0, first), columns(1, first), columns(2, first),
        pl.BlockSpec((2, CELLS, GW), lambda g: (0, 0, first + g)),
    ]
    half = pl.BlockSpec((D // 2, D), lambda g: (0, g))
    outputs = [
        half, half,
        pl.BlockSpec((2, CELLS, GW), lambda g: (0, 0, g)),
        pl.BlockSpec((1, 2, CELLS, D), lambda g: (g, 0, 0, 0)),
    ]
    shapes = [
        jax.ShapeDtypeStruct((D // 2, groups * D), BF),
        jax.ShapeDtypeStruct((D // 2, groups * D), BF),
        jax.ShapeDtypeStruct((2, CELLS, groups * GW), BF),
        jax.ShapeDtypeStruct((groups, 2, CELLS, D), BF),
    ]
    return inputs, outputs, shapes


def first_heads(tiles, below, right, diag, tis, live, w_qkv, da):
    inputs, outputs, shapes = heads_specs(0, 2)
    rows = jax.ShapeDtypeStruct((2, CELLS, D), BF)
    return pl.pallas_call(
        first_kernel,
        grid=(2,),
        in_specs=[full((16, 32, D)), full((8, 24, D)), full((8, 8, D)), full((8, 8, D))] + inputs,
        out_specs=outputs + [full((2, CELLS, D))] * 2,
        out_shape=shapes + [rows, rows],
        scratch_shapes=[pltpu.VMEM((D, 2 * CELLS), BF)],
        compiler_params=pltpu.CompilerParams(vmem_limit_bytes=VMEM),
        cost_estimate=cost(6e9, 10e6),
        name="first_heads",
    )(tiles, below, right, diag, tis, live, w_qkv, w_qkv, w_qkv, da)


def last_heads(hid, hid_t, tis, live, w_qkv, da):
    inputs, outputs, shapes = heads_specs(2, 1)
    return pl.pallas_call(
        last_kernel,
        grid=(1,),
        in_specs=[full((2, CELLS, D)), full((D, 2 * CELLS))] + inputs,
        out_specs=outputs,
        out_shape=shapes,
        compiler_params=pltpu.CompilerParams(vmem_limit_bytes=VMEM),
        cost_estimate=cost(4e9, 6e6),
        name="last_heads",
    )(hid, hid_t, tis, live, w_qkv, w_qkv, w_qkv, da)


def proj_kernel(att0_ref, att1_ref, db_ref, keep_ref, send_ref):
    attended = jnp.concatenate([att0_ref[...], att1_ref[...]], 2).reshape(2 * CELLS, D)
    att_t = nt(row_order(False), attended).astype(BF)
    put(nn(att_t, db_ref[...].reshape(2 * CELLS, D)), keep_ref, send_ref)


def proj_grad(att0, att1, db):
    shape = jax.ShapeDtypeStruct((D // 2, D), BF)
    return pl.pallas_call(
        proj_kernel,
        out_shape=[shape, shape],
        compiler_params=pltpu.CompilerParams(vmem_limit_bytes=VMEM),
        cost_estimate=cost(2e9, 4e6),
        name="proj_grad",
    )(att0, att1, db)


def out_kernel(xw_ref, tis_ref, att0_ref, att1_ref, wp_ref, out_ref):
    for w in range(2):
        tis = jnp.tile(tis_ref[w].astype(F32), (1, D // 128))
        attended = jnp.concatenate([att0_ref[w], att1_ref[w]], 1)
        out = xw_ref[w].astype(F32) + tis * nn(attended, wp_ref[...])
        out_ref[:, w] = out.astype(BF).reshape(WIN, WIN, D)


def out_part(xw, tis, att0, att1, w_proj):
    out = pl.pallas_call(
        out_kernel,
        out_shape=jax.ShapeDtypeStruct((WIN, 2, WIN, D), BF),
        compiler_params=pltpu.CompilerParams(vmem_limit_bytes=VMEM),
        cost_estimate=cost(1e3, 1e3),
        name="out_part",
    )(xw, tis, att0, att1, w_proj)
    return out.reshape(1, WIN, 2 * WIN, D)


def grad_kernel(
    xw_ref, cot_ref, dqkv0_ref, dqkv1_ref, wq_ref, wk_ref, wv_ref, grad_ref, acc_ref
):
    step = pl.program_id(0)
    weights = jnp.concatenate([wq_ref[...], wk_ref[...], wv_ref[...]], 1)
    dqkv = jnp.where(step < GROUPS - 1, dqkv0_ref[0], dqkv1_ref[0])
    part = nt(dqkv.reshape(2 * CELLS, D), weights)

    @pl.when(step == 0)
    def _():
        acc_ref[...] = part

    @pl.when((step > 0) & (step < GROUPS - 1))
    def _():
        acc_ref[...] += part

    @pl.when(step == GROUPS - 1)
    def _():
        acc_ref[...] += part
        for w in range(2):
            normed, inv = moments(xw_ref[w].astype(F32))
            dh = acc_ref[w * CELLS : (w + 1) * CELLS]
            dnorm = inv * (
                dh
                - jnp.mean(dh, -1, keepdims=True)
                - normed * jnp.mean(dh * normed, -1, keepdims=True)
            )
            grad = cot_ref[:, w].reshape(CELLS, D).astype(F32) + dnorm
            grad_ref[:, w] = grad.astype(BF).reshape(WIN, WIN, D)


def grad_part(xw, cot, dqkv0, dqkv1, w_qkv):
    grad = pl.pallas_call(
        grad_kernel,
        grid=(GROUPS,),
        in_specs=[
            full((2, CELLS, D)), full((WIN, 2, WIN, D)),
            pl.BlockSpec((1, 2, CELLS, D), lambda g: (jnp.minimum(g, 1), 0, 0, 0)),
            full((1, 2, CELLS, D)),
            columns(0, 0), columns(1, 0), columns(2, 0),
        ],
        out_specs=full((WIN, 2, WIN, D)),
        out_shape=jax.ShapeDtypeStruct((WIN, 2, WIN, D), BF),
        scratch_shapes=[pltpu.VMEM((2 * CELLS, D), F32)],
        compiler_params=pltpu.CompilerParams(vmem_limit_bytes=VMEM),
        cost_estimate=cost(1e3, 1e3),
        name="grad_part",
    )(xw, cot, dqkv0, dqkv1, w_qkv, w_qkv, w_qkv)
    return grad.reshape(1, WIN, 2 * WIN, D)


def send(value, axis, move):
    devices = lax.axis_size(axis)
    return lax.ppermute(value, axis, [(i, move(i) % devices) for i in range(devices)])


def add(*terms):
    total = terms[0].astype(F32)
    for term in terms[1:]:
        total = total + term.astype(F32)
    return total.astype(BF)


def ring_start(low, high, axis, step):
    from_low = send(low[2], axis, lambda j: j + step)
    from_high = send(high[2], axis, lambda j: j - step)
    return from_low, from_high


def ring_pass(low, high, came, axis, step):
    up = jnp.concatenate([add(low[1], came[0]), high[1]], 1)
    down = jnp.concatenate([low[3], add(high[3], came[1])], 1)
    return send(up, axis, lambda j: j + step), send(down, axis, lambda j: j - step)


def ring_end(low, high, came):
    n = low.shape[2]
    up, down = came
    low = add(low[0], up[:, :n], down[:, :n])
    high = add(high[0], up[:, n:], down[:, n:])
    return jnp.concatenate([low, high], 1)


def halve_start(rows, axis, flip):
    return send(rows[rows.shape[0] // 2 :], axis, lambda j: j ^ flip)


def halve_end(rows, came):
    return add(rows[: rows.shape[0] // 2], came)


def exchange(rows, axis, groups=None):
    parts = len(groups[0]) if groups else math.prod(lax.axis_size(a) for a in axis)
    rows = rows.reshape(parts, rows.shape[0] // parts, rows.shape[1])
    return lax.all_to_all(rows, axis, 0, 0, axis_index_groups=groups)


def tie(*values):
    return lax.optimization_barrier(values)


def blocks(value):
    return value.reshape(4, value.shape[0] // 4, value.shape[1])


def shards(tiles, cotangent, tissue, w_qkv, w_proj):
    mine = tiles[0]
    above, left, corner = edges(mine)
    below = send(above, "gy", lambda i: i - 1)
    right = send(left, "gx", lambda i: i - 1)
    ny, nx = lax.axis_size("gy"), lax.axis_size("gx")
    diag = lax.ppermute(
        corner,
        ("gy", "gx"),
        [
            (a * nx + b, (a - 1) % ny * nx + (b - 1) % nx)
            for a in range(ny)
            for b in range(nx)
        ],
    )
    cot = cotangent.reshape(WIN, 2, WIN, D)
    db, da, tis, live = branch(cot, tissue[0], w_proj)
    keep0, send0, att0, dqkv0, xw, hid = first_heads(
        mine, below, right, diag, tis, live, w_qkv, da
    )
    came = send(send0, "gy", lambda i: i ^ 1)
    hid_t = turn(hid)
    came, hid_t = tie(came, hid_t)
    first = add(keep0, came)
    low_a, high_a = blocks(first[:, :D]), blocks(first[:, D:])
    low_a, high_a, hid_t = tie(low_a, high_a, hid_t)
    came_a = ring_start(low_a, high_a, "dp", 1)
    keep1, send1, att1, dqkv1 = last_heads(hid, hid_t, tis, live, w_qkv, da)
    came_a, send1, att1 = tie(came_a, send1, att1)
    came_a = ring_pass(low_a, high_a, came_a, "dp", 1)
    came = send(send1, "gy", lambda i: i ^ 1)
    keep2, send2 = proj_grad(att0, att1, db)
    came, send2, keep2 = tie(came, send2, keep2)
    rows_b = jnp.concatenate([add(keep1, came), add(keep2, send(send2, "gy", lambda i: i ^ 1))], 1)
    rows_b, att1 = tie(rows_b, att1)
    same_core = [[d * 8 + y * 2 + c for d in range(4) for y in range(4)] for c in range(2)]
    parts_b = exchange(rows_b, ("dp", "gy"), same_core)
    rows_a, att1 = tie(ring_end(low_a, high_a, came_a), att1)
    came_a = halve_start(rows_a, "gy", 2)
    out = out_part(xw, tis, att0, att1, w_proj)
    came_a, out, xw = tie(came_a, out, xw)
    rows_a = halve_end(rows_a, came_a)
    came_a = halve_start(rows_a, "gy", 6)
    grad = grad_part(xw, cot, dqkv0, dqkv1, w_qkv)
    came_a, grad, parts_b = tie(came_a, grad, parts_b)
    rows = jnp.concatenate([halve_end(rows_a, came_a), add(*parts_b)], 1)
    parts = exchange(rows, ("gx",))
    total = jnp.sum(parts.astype(F32), 0) * (1.0 / math.sqrt(512))
    grad_qkv = total[:, : 3 * D].reshape(3, GROUPS, 3, GW).transpose(0, 2, 1, 3)
    return out, grad, grad_qkv.reshape(3, 3 * D), total[:, 3 * D :]


def solution(mesh):
    block = P("dp", "gy", "gx", None)
    in_specs = (block, block, P("dp", "gy", "gx"), P(), P())
    out_specs = (block, block, P(("dp", "gy", "gx"), None), P(("dp", "gy", "gx"), None))
    return jax.shard_map(
        shards, mesh=mesh, in_specs=in_specs, out_specs=out_specs, check_vma=False
    )
```

```python
import math

import jax
import jax.numpy as jnp
from jax import lax
from jax.experimental import pallas as pl
from jax.experimental.pallas import tpu as pltpu
from jax.sharding import PartitionSpec as P

F32 = jnp.float32
BF = jnp.bfloat16
D = 768
WIN = 16
CELLS = WIN * WIN
GROUPS = 3
GW = D // GROUPS
HEAD_SCALE = 0.125
VMEM = 32 * 1024 * 1024


def nn(a, b):
    return lax.dot_general(a, b, (((1,), (0,)), ((), ())), preferred_element_type=F32)


def nt(a, b):
    return lax.dot_general(a, b, (((1,), (1,)), ((), ())), preferred_element_type=F32)


def tn(a, b):
    return lax.dot_general(a, b, (((0,), (0,)), ((), ())), preferred_element_type=F32)


def full(shape):
    return pl.BlockSpec(shape, lambda *g: (0,) * len(shape))


def cost(flops, size):
    return pl.CostEstimate(flops=int(flops), bytes_accessed=int(size), transcendentals=0)


def edges_kernel(tiles, above, left, corner, sem):
    copies = [
        pltpu.make_async_copy(tiles.at[0:8, 8:32], above, sem.at[0]),
        pltpu.make_async_copy(tiles.at[8:16, 0:8], left, sem.at[1]),
        pltpu.make_async_copy(tiles.at[0:8, 0:8], corner, sem.at[2]),
    ]
    for copy in copies:
        copy.start()
    for copy in copies:
        copy.wait()


def edges(tiles):
    small = jax.ShapeDtypeStruct((8, 8, D), BF)
    return pl.pallas_call(
        edges_kernel,
        in_specs=[pl.BlockSpec(memory_space=pl.ANY)],
        out_specs=[pl.BlockSpec(memory_space=pl.ANY)] * 3,
        out_shape=[jax.ShapeDtypeStruct((8, 24, D), BF), small, small],
        scratch_shapes=[pltpu.SemaphoreType.DMA((3,))],
        compiler_params=pltpu.CompilerParams(vmem_limit_bytes=VMEM),
        cost_estimate=cost(3e10, 1e6),
        name="edges",
    )(tiles)


def branch_kernel(
    cot_hbm, tissue_hbm, wp_hbm, db_ref, da_ref, tis_ref, live_ref, cot_ref, tissue_ref, wp_ref, sem
):
    copies = [
        pltpu.make_async_copy(tissue_hbm, tissue_ref, sem.at[0]),
        pltpu.make_async_copy(cot_hbm, cot_ref, sem.at[1]),
        pltpu.make_async_copy(wp_hbm, wp_ref, sem.at[2]),
    ]
    for copy in copies:
        copy.start()
    copies[0].wait()
    grid = tissue_ref[...].astype(F32).astype(BF)
    cell = lax.broadcasted_iota(jnp.int32, (CELLS, 1), 0)
    row_of = lax.broadcasted_iota(jnp.int32, (CELLS, WIN), 1) == (cell >> 4)
    rows = nn(row_of.astype(F32).astype(BF), grid)
    lane = lax.broadcasted_iota(jnp.int32, (CELLS, 2 * WIN), 1)
    ones = jnp.ones((2 * WIN, 128), BF)
    copies[1].wait()
    copies[2].wait()
    for w in range(2):
        own = jnp.where(lane == (cell & 15) + w * WIN, rows, 0.0).astype(BF)
        tis = nn(own, ones)
        some = jnp.max(jnp.max(tis, 0, keepdims=True), 1, keepdims=True)
        tis_ref[w] = tis.astype(BF)
        live_ref[w] = jnp.maximum(tis, 1.0 - some).astype(BF)
        db = cot_ref[:, w].reshape(CELLS, D) * jnp.tile(tis.astype(BF), (1, D // 128))
        db_ref[w] = db
        da_ref[w] = nt(db, wp_ref[...]).astype(BF)


def branch(cot, tissue, w_proj):
    shape = jax.ShapeDtypeStruct((2, CELLS, D), BF)
    mask = jax.ShapeDtypeStruct((2, CELLS, 128), BF)
    return pl.pallas_call(
        branch_kernel,
        in_specs=[pl.BlockSpec(memory_space=pltpu.HBM)] * 3,
        out_shape=[shape, shape, mask, mask],
        scratch_shapes=[
            pltpu.VMEM((WIN, 2, WIN, D), BF),
            pltpu.VMEM((WIN, 2 * WIN), jnp.int32),
            pltpu.VMEM((D, D), BF),
            pltpu.SemaphoreType.DMA((3,)),
        ],
        compiler_params=pltpu.CompilerParams(vmem_limit_bytes=VMEM),
        cost_estimate=cost(2e10, 4e6),
        name="branch",
    )(cot, tissue, w_proj)


def row_order(first):
    gy = lax.axis_index("gy")
    dp, y, core = lax.axis_index("dp"), gy >> 1, gy & 1
    at = lax.broadcasted_iota(jnp.int32, (D, 1), 0)
    third = ((at.astype(F32) + 0.5) * (1.0 / 3)).astype(jnp.int32)
    distance, depth = (third >> 5) & 3, third & 7
    partner = ((third >> 4) & 1) ^ (((third >> 3) & 1) * 3)
    if first == "dp":
        dp_of, y_of = (distance + dp) & 3, partner ^ y
    else:
        dp_of, y_of = partner ^ dp, (distance + y) & 3
    core_of = (third >> 7) ^ core
    source = ((dp_of * 8 + y_of * 2 + core_of) * 8 + depth) * 3 + at - third * 3
    column = lax.broadcasted_iota(jnp.int32, (D, D), 1)
    return jnp.where(column == source, 1.0, 0.0).astype(BF)


def moments(x):
    mean = jnp.mean(x, -1, keepdims=True)
    centred = x - mean
    inv = lax.rsqrt(jnp.mean(centred * centred, -1, keepdims=True) + 1e-05)
    return centred * inv, inv


def head_pair(q2, k2, v2, da2, ones2):
    lane = lax.broadcasted_iota(jnp.int32, (1, 128), 1)
    sel_a = (lane < 64).astype(BF)
    sel_b = (lane >= 64).astype(BF)
    ka, kb, va, vb = k2 * sel_a, k2 * sel_b, v2 * sel_a, v2 * sel_b
    wa = jnp.exp(nt(q2, ka)).astype(BF)
    wb = jnp.exp(nt(q2, kb)).astype(BF)
    both = nn(wa, jnp.concatenate([va, ones2 * sel_a], 1)) + nn(
        wb, jnp.concatenate([vb, ones2 * sel_b], 1)
    )
    rinv = 1.0 / both[:, 128:]
    attended = both[:, :128] * rinv
    lhs = jnp.concatenate([da2, (da2.astype(F32) * attended).astype(BF)], 1)
    minus_a = jnp.broadcast_to(-sel_a, (CELLS, 128))
    minus_b = jnp.broadcast_to(-sel_b, (CELLS, 128))
    dsa = (wa.astype(F32) * nt(lhs, jnp.concatenate([va, minus_a], 1))).astype(BF)
    dsb = (wb.astype(F32) * nt(lhs, jnp.concatenate([vb, minus_b], 1))).astype(BF)
    dq = (nn(dsa, ka) + nn(dsb, kb)) * (rinv * HEAD_SCALE)
    dan = (da2.astype(F32) * rinv).astype(BF)
    qn = (q2.astype(F32) * rinv).astype(BF)
    dv = tn(wa, dan * sel_a) + tn(wb, dan * sel_b)
    dk = tn(dsa, qn * sel_a) + tn(dsb, qn * sel_b)
    return attended.astype(BF), dq.astype(BF), dk.astype(BF), dv.astype(BF)


def put(grad, keep_ref, send_ref):
    keep_ref[...] = grad[: D // 2].astype(BF)
    send_ref[...] = grad[D // 2 :].astype(BF)


def heads_group(
    hid_ref, hid_t_ref, tis_ref, live_ref, wq_ref, wk_ref, wv_ref, da_ref,
    keep_ref, send_ref, att_ref, dqkv_ref,
):
    for w in range(2):
        hidden = hid_ref[w]
        query = nn(hidden, wq_ref[...]).astype(BF) * BF(HEAD_SCALE)
        tis2 = tis_ref[w]
        tis4 = jnp.concatenate([tis2, tis2], 1)
        key = nn(hidden, wk_ref[...]).astype(BF) * tis4
        value = nn(hidden, wv_ref[...]).astype(BF) * tis4
        for p in range(2):
            s = slice(p * 128, (p + 1) * 128)
            att, dq, dk, dv = head_pair(
                query[:, s], key[:, s], value[:, s], da_ref[w, :, s], live_ref[w]
            )
            att_ref[w, :, s] = att
            dqkv_ref[0, w, :, s] = dq
            dqkv_ref[0, w, :, slice(GW + p * 128, GW + (p + 1) * 128)] = dk * tis2
            dqkv_ref[0, w, :, slice(2 * GW + p * 128, 2 * GW + (p + 1) * 128)] = dv * tis2
    put(nn(hid_t_ref[...], dqkv_ref[0].reshape(2 * CELLS, D)), keep_ref, send_ref)


def first_kernel(
    tiles_ref, below_ref, right_ref, diag_ref, tis_ref, live_ref,
    wq_ref, wk_ref, wv_ref, da_ref,
    keep_ref, send_ref, att_ref, dqkv_ref, xw_ref, hid_ref, hid_t_ref,
):
    @pl.when(pl.program_id(0) == 0)
    def _():
        own = tiles_ref[8:16].astype(F32)
        low = below_ref[...].astype(F32)
        right = right_ref[...].astype(F32)
        diag = diag_ref[...].astype(F32)
        perm = row_order("dp")
        for w in range(2):
            if w == 0:
                top, bottom = own[:, 8:24], low[:, :16]
            else:
                top = jnp.concatenate([own[:, 24:32], right], 1)
                bottom = jnp.concatenate([low[:, 16:24], diag], 1)
            x = jnp.concatenate([top, bottom], 0).reshape(CELLS, D)
            xw_ref[w] = x.astype(BF)
            normed, _ = moments(x)
            hidden = normed.astype(BF)
            hid_ref[w] = hidden
            hid_t_ref[:, w * CELLS : (w + 1) * CELLS] = nt(perm, hidden).astype(BF)

    heads_group(
        hid_ref, hid_t_ref, tis_ref, live_ref, wq_ref, wk_ref, wv_ref, da_ref,
        keep_ref, send_ref, att_ref, dqkv_ref,
    )


def last_kernel(
    hid_ref, hid_t_ref, tis_ref, live_ref, wq_ref, wk_ref, wv_ref, da_ref,
    keep_ref, send_ref, att_ref, dqkv_ref,
):
    heads_group(
        hid_ref, hid_t_ref, tis_ref, live_ref, wq_ref, wk_ref, wv_ref, da_ref,
        keep_ref, send_ref, att_ref, dqkv_ref,
    )


def turn_kernel(hid_ref, hid_t_ref):
    hid_t_ref[...] = nt(row_order("gy"), hid_ref[...].reshape(2 * CELLS, D)).astype(BF)


def turn(hid):
    return pl.pallas_call(
        turn_kernel,
        out_shape=jax.ShapeDtypeStruct((D, 2 * CELLS), BF),
        compiler_params=pltpu.CompilerParams(vmem_limit_bytes=VMEM),
        cost_estimate=cost(2e9, 2e6),
        name="turn",
    )(hid)


def columns(block, first):
    return pl.BlockSpec((D, GW), lambda g: (0, block * GROUPS + first + g))


def heads_specs(first, groups):
    inputs = [
        full((2, CELLS, 128)), full((2, CELLS, 128)),
        columns(0, first), columns(1, first), columns(2, first),
        pl.BlockSpec((2, CELLS, GW), lambda g: (0, 0, first + g)),
    ]
    half = pl.BlockSpec((D // 2, D), lambda g: (0, g))
    outputs = [
        half, half,
        pl.BlockSpec((2, CELLS, GW), lambda g: (0, 0, g)),
        pl.BlockSpec((1, 2, CELLS, D), lambda g: (g, 0, 0, 0)),
    ]
    shapes = [
        jax.ShapeDtypeStruct((D // 2, groups * D), BF),
        jax.ShapeDtypeStruct((D // 2, groups * D), BF),
        jax.ShapeDtypeStruct((2, CELLS, groups * GW), BF),
        jax.ShapeDtypeStruct((groups, 2, CELLS, D), BF),
    ]
    return inputs, outputs, shapes


def first_heads(tiles, below, right, diag, tis, live, w_qkv, da):
    inputs, outputs, shapes = heads_specs(0, 2)
    rows = jax.ShapeDtypeStruct((2, CELLS, D), BF)
    return pl.pallas_call(
        first_kernel,
        grid=(2,),
        in_specs=[full((16, 32, D)), full((8, 24, D)), full((8, 8, D)), full((8, 8, D))] + inputs,
        out_specs=outputs + [full((2, CELLS, D))] * 2,
        out_shape=shapes + [rows, rows],
        scratch_shapes=[pltpu.VMEM((D, 2 * CELLS), BF)],
        compiler_params=pltpu.CompilerParams(vmem_limit_bytes=VMEM),
        cost_estimate=cost(6e9, 10e6),
        name="first_heads",
    )(tiles, below, right, diag, tis, live, w_qkv, w_qkv, w_qkv, da)


def last_heads(hid, hid_t, tis, live, w_qkv, da):
    inputs, outputs, shapes = heads_specs(2, 1)
    return pl.pallas_call(
        last_kernel,
        grid=(1,),
        in_specs=[full((2, CELLS, D)), full((D, 2 * CELLS))] + inputs,
        out_specs=outputs,
        out_shape=shapes,
        compiler_params=pltpu.CompilerParams(vmem_limit_bytes=VMEM),
        cost_estimate=cost(4e9, 6e6),
        name="last_heads",
    )(hid, hid_t, tis, live, w_qkv, w_qkv, w_qkv, da)


def proj_kernel(att0_ref, att1_ref, db_ref, keep_ref, send_ref):
    attended = jnp.concatenate([att0_ref[...], att1_ref[...]], 2).reshape(2 * CELLS, D)
    att_t = nt(row_order("gy"), attended).astype(BF)
    put(nn(att_t, db_ref[...].reshape(2 * CELLS, D)), keep_ref, send_ref)


def proj_grad(att0, att1, db):
    shape = jax.ShapeDtypeStruct((D // 2, D), BF)
    return pl.pallas_call(
        proj_kernel,
        out_shape=[shape, shape],
        compiler_params=pltpu.CompilerParams(vmem_limit_bytes=VMEM),
        cost_estimate=cost(2e9, 4e6),
        name="proj_grad",
    )(att0, att1, db)


def out_kernel(xw_ref, tis_ref, att0_ref, att1_ref, wp_ref, out_ref):
    for w in range(2):
        tis = jnp.tile(tis_ref[w].astype(F32), (1, D // 128))
        attended = jnp.concatenate([att0_ref[w], att1_ref[w]], 1)
        out = xw_ref[w].astype(F32) + tis * nn(attended, wp_ref[...])
        out_ref[:, w] = out.astype(BF).reshape(WIN, WIN, D)


def out_part(xw, tis, att0, att1, w_proj):
    out = pl.pallas_call(
        out_kernel,
        out_shape=jax.ShapeDtypeStruct((WIN, 2, WIN, D), BF),
        compiler_params=pltpu.CompilerParams(vmem_limit_bytes=VMEM),
        cost_estimate=cost(1e3, 1e3),
        name="out_part",
    )(xw, tis, att0, att1, w_proj)
    return out.reshape(1, WIN, 2 * WIN, D)


def grad_kernel(
    xw_ref, cot_ref, dqkv0_ref, dqkv1_ref, wq_ref, wk_ref, wv_ref, grad_ref, acc_ref
):
    step = pl.program_id(0)
    weights = jnp.concatenate([wq_ref[...], wk_ref[...], wv_ref[...]], 1)
    dqkv = jnp.where(step < GROUPS - 1, dqkv0_ref[0], dqkv1_ref[0])
    part = nt(dqkv.reshape(2 * CELLS, D), weights)

    @pl.when(step == 0)
    def _():
        acc_ref[...] = part

    @pl.when((step > 0) & (step < GROUPS - 1))
    def _():
        acc_ref[...] += part

    @pl.when(step == GROUPS - 1)
    def _():
        acc_ref[...] += part
        for w in range(2):
            normed, inv = moments(xw_ref[w].astype(F32))
            dh = acc_ref[w * CELLS : (w + 1) * CELLS]
            dnorm = inv * (
                dh
                - jnp.mean(dh, -1, keepdims=True)
                - normed * jnp.mean(dh * normed, -1, keepdims=True)
            )
            grad = cot_ref[:, w].reshape(CELLS, D).astype(F32) + dnorm
            grad_ref[:, w] = grad.astype(BF).reshape(WIN, WIN, D)


def grad_part(xw, cot, dqkv0, dqkv1, w_qkv):
    grad = pl.pallas_call(
        grad_kernel,
        grid=(GROUPS,),
        in_specs=[
            full((2, CELLS, D)), full((WIN, 2, WIN, D)),
            pl.BlockSpec((1, 2, CELLS, D), lambda g: (jnp.minimum(g, 1), 0, 0, 0)),
            full((1, 2, CELLS, D)),
            columns(0, 0), columns(1, 0), columns(2, 0),
        ],
        out_specs=full((WIN, 2, WIN, D)),
        out_shape=jax.ShapeDtypeStruct((WIN, 2, WIN, D), BF),
        scratch_shapes=[pltpu.VMEM((2 * CELLS, D), F32)],
        compiler_params=pltpu.CompilerParams(vmem_limit_bytes=VMEM),
        cost_estimate=cost(1e3, 1e3),
        name="grad_part",
    )(xw, cot, dqkv0, dqkv1, w_qkv, w_qkv, w_qkv)
    return grad.reshape(1, WIN, 2 * WIN, D)


def send(value, axis, move):
    devices = lax.axis_size(axis)
    return lax.ppermute(value, axis, [(i, move(i) % devices) for i in range(devices)])


def add(*terms):
    total = terms[0].astype(F32)
    for term in terms[1:]:
        total = total + term.astype(F32)
    return total.astype(BF)


def ring_start(low, high, axis, step):
    from_low = send(low[2], axis, lambda j: j + step)
    from_high = send(high[2], axis, lambda j: j - step)
    return from_low, from_high


def ring_pass(low, high, came, axis, step):
    up = jnp.concatenate([add(low[1], came[0]), high[1]], 1)
    down = jnp.concatenate([low[3], add(high[3], came[1])], 1)
    return send(up, axis, lambda j: j + step), send(down, axis, lambda j: j - step)


def ring_end(low, high, came):
    n = low.shape[2]
    up, down = came
    low = add(low[0], up[:, :n], down[:, :n])
    high = add(high[0], up[:, n:], down[:, n:])
    return jnp.concatenate([low, high], 1)


def halve_start(rows, axis, flip):
    return send(rows[rows.shape[0] // 2 :], axis, lambda j: j ^ flip)


def halve_end(rows, came):
    return add(rows[: rows.shape[0] // 2], came)


def exchange(rows, axis, groups=None):
    parts = len(groups[0]) if groups else math.prod(lax.axis_size(a) for a in axis)
    rows = rows.reshape(parts, rows.shape[0] // parts, rows.shape[1])
    return lax.all_to_all(rows, axis, 0, 0, axis_index_groups=groups)


def tie(*values):
    return lax.optimization_barrier(values)


def blocks(value):
    return value.reshape(4, value.shape[0] // 4, value.shape[1])


def shards(tiles, cotangent, tissue, w_qkv, w_proj):
    mine = tiles[0]
    above, left, corner = edges(mine)
    below = send(above, "gy", lambda i: i - 1)
    right = send(left, "gx", lambda i: i - 1)
    ny, nx = lax.axis_size("gy"), lax.axis_size("gx")
    diag = lax.ppermute(
        corner,
        ("gy", "gx"),
        [
            (a * nx + b, (a - 1) % ny * nx + (b - 1) % nx)
            for a in range(ny)
            for b in range(nx)
        ],
    )
    cot = cotangent.reshape(WIN, 2, WIN, D)
    db, da, tis, live = branch(cot, tissue[0], w_proj)
    keep0, send0, att0, dqkv0, xw, hid = first_heads(
        mine, below, right, diag, tis, live, w_qkv, da
    )
    came = send(send0, "gy", lambda i: i ^ 1)
    hid_t = turn(hid)
    came, hid_t = tie(came, hid_t)
    first = add(keep0, came)
    low_a, high_a = blocks(first[:, :D]), blocks(first[:, D:])
    low_a, high_a, hid_t = tie(low_a, high_a, hid_t)
    came_a = ring_start(low_a, high_a, "dp", 1)
    keep1, send1, att1, dqkv1 = last_heads(hid, hid_t, tis, live, w_qkv, da)
    came_a, send1, att1 = tie(came_a, send1, att1)
    came_a = ring_pass(low_a, high_a, came_a, "dp", 1)
    came = send(send1, "gy", lambda i: i ^ 1)
    keep2, send2 = proj_grad(att0, att1, db)
    came, send2, keep2 = tie(came, send2, keep2)
    low_b = add(keep1, came)
    high_b = add(keep2, send(send2, "gy", lambda i: i ^ 1))
    low_b, high_b, att1 = tie(blocks(low_b), blocks(high_b), att1)
    came_b = ring_start(low_b, high_b, "gy", 2)
    out = out_part(xw, tis, att0, att1, w_proj)
    came_b, out, xw, low_a, high_a = tie(came_b, out, xw, low_a, high_a)
    came_b = ring_pass(low_b, high_b, came_b, "gy", 2)
    rows_a = ring_end(low_a, high_a, came_a)
    came_a = halve_start(rows_a, "gy", 2)
    grad = grad_part(xw, cot, dqkv0, dqkv1, w_qkv)
    came_a, came_b, grad = tie(came_a, came_b, grad)
    rows_a = halve_end(rows_a, came_a)
    rows_b = ring_end(low_b, high_b, came_b)
    came_a = halve_start(rows_a, "gy", 6)
    came_b = halve_start(rows_b, "dp", 1)
    rows_b = halve_end(rows_b, came_b)
    came_b = halve_start(rows_b, "dp", 3)
    rows = jnp.concatenate([halve_end(rows_a, came_a), halve_end(rows_b, came_b)], 1)
    parts = exchange(rows, ("gx",))
    total = jnp.sum(parts.astype(F32), 0) * (1.0 / math.sqrt(512))
    grad_qkv = total[:, : 3 * D].reshape(3, GROUPS, 3, GW).transpose(0, 2, 1, 3)
    return out, grad, grad_qkv.reshape(3, 3 * D), total[:, 3 * D :]


def solution(mesh):
    block = P("dp", "gy", "gx", None)
    in_specs = (block, block, P("dp", "gy", "gx"), P(), P())
    out_specs = (block, block, P(("dp", "gy", "gx"), None), P(("dp", "gy", "gx"), None))
    return jax.shard_map(
        shards, mesh=mesh, in_specs=in_specs, out_specs=out_specs, check_vma=False
    )
```

```python
import math

import jax
import jax.numpy as jnp
from jax import lax
from jax.experimental import pallas as pl
from jax.experimental.pallas import tpu as pltpu
from jax.sharding import PartitionSpec as P

F32 = jnp.float32
BF = jnp.bfloat16
D = 768
WIN = 16
CELLS = WIN * WIN
GROUPS = 3
GW = D // GROUPS
HEAD_SCALE = 0.125
VMEM = 32 * 1024 * 1024


def nn(a, b):
    return lax.dot_general(a, b, (((1,), (0,)), ((), ())), preferred_element_type=F32)


def nt(a, b):
    return lax.dot_general(a, b, (((1,), (1,)), ((), ())), preferred_element_type=F32)


def tn(a, b):
    return lax.dot_general(a, b, (((0,), (0,)), ((), ())), preferred_element_type=F32)


def full(shape):
    return pl.BlockSpec(shape, lambda *g: (0,) * len(shape))


def cost(flops, size):
    return pl.CostEstimate(flops=int(flops), bytes_accessed=int(size), transcendentals=0)


def above_kernel(tiles_ref, above_ref):
    above_ref[...] = tiles_ref[...].astype(F32)[:, 8:].astype(BF)


def left_kernel(tiles_ref, after_ref, left_ref, corner_ref):
    tiles = tiles_ref[...].astype(F32)[:, :8].astype(BF)
    corner_ref[...] = tiles[:8]
    left_ref[...] = tiles[8:]


def edges(tiles):
    small = jax.ShapeDtypeStruct((8, 8, D), BF)
    above = pl.pallas_call(
        above_kernel,
        grid=(1,),
        in_specs=[pl.BlockSpec((8, 32, D), lambda g: (0, 0, 0))],
        out_specs=full((8, 24, D)),
        out_shape=jax.ShapeDtypeStruct((8, 24, D), BF),
        compiler_params=pltpu.CompilerParams(vmem_limit_bytes=VMEM),
        cost_estimate=cost(3e10, 1e6),
        name="above",
    )(tiles)
    left, corner = pl.pallas_call(
        left_kernel,
        grid=(1,),
        in_specs=[
            pl.BlockSpec((16, 16, D), lambda g: (0, 0, 0)),
            pl.BlockSpec(memory_space=pl.ANY),
        ],
        out_specs=[full((8, 8, D))] * 2,
        out_shape=[small, small],
        compiler_params=pltpu.CompilerParams(vmem_limit_bytes=VMEM),
        cost_estimate=cost(1e3, 1e3),
        name="left",
    )(tiles, above)
    return above, left, corner


def branch_kernel(
    cot_hbm, tissue_hbm, wp_hbm, db_ref, da_ref, tis_ref, live_ref, cot_ref, tissue_ref, wp_ref, sem
):
    copies = [
        pltpu.make_async_copy(tissue_hbm, tissue_ref, sem.at[0]),
        pltpu.make_async_copy(cot_hbm, cot_ref, sem.at[1]),
        pltpu.make_async_copy(wp_hbm, wp_ref, sem.at[2]),
    ]
    for copy in copies:
        copy.start()
    copies[0].wait()
    grid = tissue_ref[...].astype(F32).astype(BF)
    cell = lax.broadcasted_iota(jnp.int32, (CELLS, 1), 0)
    row_of = lax.broadcasted_iota(jnp.int32, (CELLS, WIN), 1) == (cell >> 4)
    rows = nn(row_of.astype(F32).astype(BF), grid)
    lane = lax.broadcasted_iota(jnp.int32, (CELLS, 2 * WIN), 1)
    ones = jnp.ones((2 * WIN, 128), BF)
    copies[1].wait()
    copies[2].wait()
    for w in range(2):
        own = jnp.where(lane == (cell & 15) + w * WIN, rows, 0.0).astype(BF)
        tis = nn(own, ones)
        some = jnp.max(jnp.max(tis, 0, keepdims=True), 1, keepdims=True)
        tis_ref[w] = tis.astype(BF)
        live_ref[w] = jnp.maximum(tis, 1.0 - some).astype(BF)
        db = cot_ref[:, w].reshape(CELLS, D) * jnp.tile(tis.astype(BF), (1, D // 128))
        db_ref[w] = db
        da_ref[w] = nt(db, wp_ref[...]).astype(BF)


def branch(cot, tissue, w_proj):
    shape = jax.ShapeDtypeStruct((2, CELLS, D), BF)
    mask = jax.ShapeDtypeStruct((2, CELLS, 128), BF)
    return pl.pallas_call(
        branch_kernel,
        in_specs=[pl.BlockSpec(memory_space=pltpu.HBM)] * 3,
        out_shape=[shape, shape, mask, mask],
        scratch_shapes=[
            pltpu.VMEM((WIN, 2, WIN, D), BF),
            pltpu.VMEM((WIN, 2 * WIN), jnp.int32),
            pltpu.VMEM((D, D), BF),
            pltpu.SemaphoreType.DMA((3,)),
        ],
        compiler_params=pltpu.CompilerParams(vmem_limit_bytes=VMEM),
        cost_estimate=cost(2e10, 4e6),
        name="branch",
    )(cot, tissue, w_proj)


def row_order(first):
    gy = lax.axis_index("gy")
    dp, y, core = lax.axis_index("dp"), gy >> 1, gy & 1
    at = lax.broadcasted_iota(jnp.int32, (D, 1), 0)
    third = ((at.astype(F32) + 0.5) * (1.0 / 3)).astype(jnp.int32)
    distance, depth = (third >> 5) & 3, third & 7
    partner = ((third >> 4) & 1) ^ (((third >> 3) & 1) * 3)
    if first == "dp":
        dp_of, y_of = (distance + dp) & 3, partner ^ y
    else:
        dp_of, y_of = partner ^ dp, (distance + y) & 3
    core_of = (third >> 7) ^ core
    source = ((dp_of * 8 + y_of * 2 + core_of) * 8 + depth) * 3 + at - third * 3
    column = lax.broadcasted_iota(jnp.int32, (D, D), 1)
    return jnp.where(column == source, 1.0, 0.0).astype(BF)


def moments(x):
    mean = jnp.mean(x, -1, keepdims=True)
    centred = x - mean
    inv = lax.rsqrt(jnp.mean(centred * centred, -1, keepdims=True) + 1e-05)
    return centred * inv, inv


def put(grad, keep_ref, send_ref):
    keep_ref[...] = grad[: D // 2].astype(BF)
    send_ref[...] = grad[D // 2 :].astype(BF)


def heads_group(
    hid_ref, hid_t_ref, tis_ref, live_ref, wq_ref, wk_ref, wv_ref, da_ref,
    keep_ref, send_ref, att_ref, dqkv_ref,
):
    hidden = hid_ref[...].reshape(2 * CELLS, D)
    query = nn(hidden, wq_ref[...]).astype(BF) * BF(HEAD_SCALE)
    key = nn(hidden, wk_ref[...]).astype(BF)
    value = nn(hidden, wv_ref[...]).astype(BF)
    lane = lax.broadcasted_iota(jnp.int32, (1, 128), 1)
    sel = [(lane < 64).astype(BF), (lane >= 64).astype(BF)]
    units = [(w, p) for w in range(2) for p in range(2)]
    q, k, v, da, weight, ds, rinv, att = {}, {}, {}, {}, {}, {}, {}, {}
    for u in units:
        w, p = u
        rows, lanes = slice(w * CELLS, (w + 1) * CELLS), slice(p * 128, (p + 1) * 128)
        q[u] = query[rows, lanes]
        k[u] = key[rows, lanes] * tis_ref[w]
        v[u] = value[rows, lanes] * tis_ref[w]
        da[u] = da_ref[w, :, lanes]
    for u in units:
        for h in range(2):
            weight[u, h] = jnp.exp(nt(q[u], k[u] * sel[h])).astype(BF)
    for u in units:
        live = live_ref[u[0]]
        both = nn(weight[u, 0], jnp.concatenate([v[u] * sel[0], live * sel[0]], 1)) + nn(
            weight[u, 1], jnp.concatenate([v[u] * sel[1], live * sel[1]], 1)
        )
        rinv[u] = 1.0 / both[:, 128:]
        att[u] = both[:, :128] * rinv[u]
        att_ref[u[0], :, u[1] * 128 : (u[1] + 1) * 128] = att[u].astype(BF)
    for u in units:
        terms = da[u].astype(F32) * att[u]
        for h in range(2):
            delta = jnp.sum(terms * sel[h].astype(F32), 1, keepdims=True)
            dprobs = nt(da[u], v[u] * sel[h]) - delta
            ds[u, h] = (weight[u, h].astype(F32) * dprobs).astype(BF)
    for u in units:
        w, p = u
        dq = (nn(ds[u, 0], k[u] * sel[0]) + nn(ds[u, 1], k[u] * sel[1])) * (rinv[u] * HEAD_SCALE)
        dan = (da[u].astype(F32) * rinv[u]).astype(BF)
        qn = (q[u].astype(F32) * rinv[u]).astype(BF)
        dv = tn(weight[u, 0], dan * sel[0]) + tn(weight[u, 1], dan * sel[1])
        dk = tn(ds[u, 0], qn * sel[0]) + tn(ds[u, 1], qn * sel[1])
        for i, grad in enumerate((dq, dk, dv)):
            at = i * GW + p * 128
            dqkv_ref[0, w, :, at : at + 128] = grad.astype(BF)
    put(nn(hid_t_ref[...], dqkv_ref[0].reshape(2 * CELLS, D)), keep_ref, send_ref)


def first_kernel(
    tiles_ref, below_ref, right_ref, diag_ref, tis_ref, live_ref,
    wq_ref, wk_ref, wv_ref, da_ref,
    keep_ref, send_ref, att_ref, dqkv_ref, xw_ref, hid_ref, hid_t_ref,
):
    @pl.when(pl.program_id(0) == 0)
    def _():
        own = tiles_ref[8:16].astype(F32)
        low = below_ref[...].astype(F32)
        right = right_ref[...].astype(F32)
        diag = diag_ref[...].astype(F32)
        perm = row_order("dp")
        for w in range(2):
            if w == 0:
                top, bottom = own[:, 8:24], low[:, :16]
            else:
                top = jnp.concatenate([own[:, 24:32], right], 1)
                bottom = jnp.concatenate([low[:, 16:24], diag], 1)
            x = jnp.concatenate([top, bottom], 0).reshape(CELLS, D)
            xw_ref[w] = x.astype(BF)
            normed, _ = moments(x)
            hidden = normed.astype(BF)
            hid_ref[w] = hidden
            masked = hidden * jnp.tile(tis_ref[w], (1, D // 128))
            hid_t_ref[:, w * CELLS : (w + 1) * CELLS] = nt(perm, masked).astype(BF)

    heads_group(
        hid_ref, hid_t_ref, tis_ref, live_ref, wq_ref, wk_ref, wv_ref, da_ref,
        keep_ref, send_ref, att_ref, dqkv_ref,
    )


def last_kernel(
    hid_ref, hid_t_ref, tis_ref, live_ref, wq_ref, wk_ref, wv_ref, da_ref,
    keep_ref, send_ref, att_ref, dqkv_ref,
):
    heads_group(
        hid_ref, hid_t_ref, tis_ref, live_ref, wq_ref, wk_ref, wv_ref, da_ref,
        keep_ref, send_ref, att_ref, dqkv_ref,
    )


def turn_kernel(hid_ref, tis_ref, hid_t_ref):
    perm = row_order("gy")
    for w in range(2):
        masked = hid_ref[w] * jnp.tile(tis_ref[w], (1, D // 128))
        hid_t_ref[:, w * CELLS : (w + 1) * CELLS] = nt(perm, masked).astype(BF)


def turn(hid, tis):
    return pl.pallas_call(
        turn_kernel,
        out_shape=jax.ShapeDtypeStruct((D, 2 * CELLS), BF),
        compiler_params=pltpu.CompilerParams(vmem_limit_bytes=VMEM),
        cost_estimate=cost(2e9, 2e6),
        name="turn",
    )(hid, tis)


def columns(block, first):
    return pl.BlockSpec((D, GW), lambda g: (0, block * GROUPS + first + g))


def heads_specs(first, groups):
    inputs = [
        full((2, CELLS, 128)), full((2, CELLS, 128)),
        columns(0, first), columns(1, first), columns(2, first),
        pl.BlockSpec((2, CELLS, GW), lambda g: (0, 0, first + g)),
    ]
    half = pl.BlockSpec((D // 2, D), lambda g: (0, g))
    outputs = [
        half, half,
        pl.BlockSpec((2, CELLS, GW), lambda g: (0, 0, g)),
        pl.BlockSpec((1, 2, CELLS, D), lambda g: (g, 0, 0, 0)),
    ]
    shapes = [
        jax.ShapeDtypeStruct((D // 2, groups * D), BF),
        jax.ShapeDtypeStruct((D // 2, groups * D), BF),
        jax.ShapeDtypeStruct((2, CELLS, groups * GW), BF),
        jax.ShapeDtypeStruct((groups, 2, CELLS, D), BF),
    ]
    return inputs, outputs, shapes


def first_heads(tiles, below, right, diag, tis, live, w_qkv, da):
    inputs, outputs, shapes = heads_specs(0, 2)
    rows = jax.ShapeDtypeStruct((2, CELLS, D), BF)
    return pl.pallas_call(
        first_kernel,
        grid=(2,),
        in_specs=[full((16, 32, D)), full((8, 24, D)), full((8, 8, D)), full((8, 8, D))] + inputs,
        out_specs=outputs + [full((2, CELLS, D))] * 2,
        out_shape=shapes + [rows, rows],
        scratch_shapes=[pltpu.VMEM((D, 2 * CELLS), BF)],
        compiler_params=pltpu.CompilerParams(vmem_limit_bytes=VMEM),
        cost_estimate=cost(6e9, 10e6),
        name="first_heads",
    )(tiles, below, right, diag, tis, live, w_qkv, w_qkv, w_qkv, da)


def last_heads(hid, hid_t, tis, live, w_qkv, da):
    inputs, outputs, shapes = heads_specs(2, 1)
    return pl.pallas_call(
        last_kernel,
        grid=(1,),
        in_specs=[full((2, CELLS, D)), full((D, 2 * CELLS))] + inputs,
        out_specs=outputs,
        out_shape=shapes,
        compiler_params=pltpu.CompilerParams(vmem_limit_bytes=VMEM),
        cost_estimate=cost(4e9, 6e6),
        name="last_heads",
    )(hid, hid_t, tis, live, w_qkv, w_qkv, w_qkv, da)


def proj_kernel(att0_ref, att1_ref, db_ref, keep_ref, send_ref):
    attended = jnp.concatenate([att0_ref[...], att1_ref[...]], 2).reshape(2 * CELLS, D)
    att_t = nt(row_order("gy"), attended).astype(BF)
    put(nn(att_t, db_ref[...].reshape(2 * CELLS, D)), keep_ref, send_ref)


def proj_grad(att0, att1, db):
    shape = jax.ShapeDtypeStruct((D // 2, D), BF)
    return pl.pallas_call(
        proj_kernel,
        out_shape=[shape, shape],
        compiler_params=pltpu.CompilerParams(vmem_limit_bytes=VMEM),
        cost_estimate=cost(2e9, 4e6),
        name="proj_grad",
    )(att0, att1, db)


def out_kernel(xw_ref, tis_ref, att0_ref, att1_ref, wp_ref, out_ref):
    for w in range(2):
        tis = jnp.tile(tis_ref[w].astype(F32), (1, D // 128))
        attended = jnp.concatenate([att0_ref[w], att1_ref[w]], 1)
        out = xw_ref[w].astype(F32) + tis * nn(attended, wp_ref[...])
        out_ref[:, w] = out.astype(BF).reshape(WIN, WIN, D)


def out_part(xw, tis, att0, att1, w_proj):
    out = pl.pallas_call(
        out_kernel,
        out_shape=jax.ShapeDtypeStruct((WIN, 2, WIN, D), BF),
        compiler_params=pltpu.CompilerParams(vmem_limit_bytes=VMEM),
        cost_estimate=cost(1e3, 1e3),
        name="out_part",
    )(xw, tis, att0, att1, w_proj)
    return out.reshape(1, WIN, 2 * WIN, D)


def grad_kernel(
    xw_ref, cot_ref, tis_ref, dqkv0_ref, dqkv1_ref, wq_ref, wk_ref, wv_ref, grad_ref, acc_ref
):
    step = pl.program_id(0)
    weights = jnp.concatenate([wq_ref[...], wk_ref[...], wv_ref[...]], 1)
    dqkv = jnp.where(step < GROUPS - 1, dqkv0_ref[0], dqkv1_ref[0])
    part = nt(dqkv.reshape(2 * CELLS, D), weights)

    @pl.when(step == 0)
    def _():
        acc_ref[...] = part

    @pl.when((step > 0) & (step < GROUPS - 1))
    def _():
        acc_ref[...] += part

    @pl.when(step == GROUPS - 1)
    def _():
        acc_ref[...] += part
        for w in range(2):
            normed, inv = moments(xw_ref[w].astype(F32))
            tis = jnp.tile(tis_ref[w].astype(F32), (1, D // 128))
            dh = acc_ref[w * CELLS : (w + 1) * CELLS] * tis
            dnorm = inv * (
                dh
                - jnp.mean(dh, -1, keepdims=True)
                - normed * jnp.mean(dh * normed, -1, keepdims=True)
            )
            grad = cot_ref[:, w].reshape(CELLS, D).astype(F32) + dnorm
            grad_ref[:, w] = grad.astype(BF).reshape(WIN, WIN, D)


def grad_part(xw, cot, tis, dqkv0, dqkv1, w_qkv):
    grad = pl.pallas_call(
        grad_kernel,
        grid=(GROUPS,),
        in_specs=[
            full((2, CELLS, D)), full((WIN, 2, WIN, D)), full((2, CELLS, 128)),
            pl.BlockSpec((1, 2, CELLS, D), lambda g: (jnp.minimum(g, 1), 0, 0, 0)),
            full((1, 2, CELLS, D)),
            columns(0, 0), columns(1, 0), columns(2, 0),
        ],
        out_specs=full((WIN, 2, WIN, D)),
        out_shape=jax.ShapeDtypeStruct((WIN, 2, WIN, D), BF),
        scratch_shapes=[pltpu.VMEM((2 * CELLS, D), F32)],
        compiler_params=pltpu.CompilerParams(vmem_limit_bytes=VMEM),
        cost_estimate=cost(1e3, 1e3),
        name="grad_part",
    )(xw, cot, tis, dqkv0, dqkv1, w_qkv, w_qkv, w_qkv)
    return grad.reshape(1, WIN, 2 * WIN, D)


def finish_kernel(parts_ref, qkv_ref, proj_ref):
    total = parts_ref[0].astype(F32)
    for part in range(1, parts_ref.shape[0]):
        total = total + parts_ref[part].astype(F32)
    total = total * (1.0 / math.sqrt(512))
    for i in range(3):
        for g in range(GROUPS):
            at = g * D + i * GW
            qkv_ref[:, i * D + g * GW : i * D + (g + 1) * GW] = total[:, at : at + GW]
    proj_ref[...] = total[:, 3 * D :]


def finish(parts):
    rows = parts.shape[1]
    return pl.pallas_call(
        finish_kernel,
        out_shape=[
            jax.ShapeDtypeStruct((rows, 3 * D), F32),
            jax.ShapeDtypeStruct((rows, D), F32),
        ],
        compiler_params=pltpu.CompilerParams(vmem_limit_bytes=VMEM),
        name="finish",
    )(parts)


def send(value, axis, move):
    devices = lax.axis_size(axis)
    return lax.ppermute(value, axis, [(i, move(i) % devices) for i in range(devices)])


def add(*terms):
    total = terms[0].astype(F32)
    for term in terms[1:]:
        total = total + term.astype(F32)
    return total.astype(BF)


def ring_start(low, high, axis, step):
    from_low = send(low[2], axis, lambda j: j + step)
    from_high = send(high[2], axis, lambda j: j - step)
    return from_low, from_high


def ring_pass(low, high, came, axis, step):
    up = jnp.concatenate([add(low[1], came[0]), high[1]], 1)
    down = jnp.concatenate([low[3], add(high[3], came[1])], 1)
    return send(up, axis, lambda j: j + step), send(down, axis, lambda j: j - step)


def ring_end(low, high, came):
    n = low.shape[2]
    up, down = came
    low = add(low[0], up[:, :n], down[:, :n])
    high = add(high[0], up[:, n:], down[:, n:])
    return jnp.concatenate([low, high], 1)


def halve_start(rows, axis, flip):
    return send(rows[rows.shape[0] // 2 :], axis, lambda j: j ^ flip)


def halve_end(rows, came):
    return add(rows[: rows.shape[0] // 2], came)


def exchange(rows, axis, groups=None):
    parts = len(groups[0]) if groups else math.prod(lax.axis_size(a) for a in axis)
    rows = rows.reshape(parts, rows.shape[0] // parts, rows.shape[1])
    return lax.all_to_all(rows, axis, 0, 0, axis_index_groups=groups)


def tie(*values):
    return lax.optimization_barrier(values)


def blocks(value):
    return value.reshape(4, value.shape[0] // 4, value.shape[1])


def shards(tiles, cotangent, tissue, w_qkv, w_proj):
    mine = tiles[0]
    above, left, corner = edges(mine)
    below = send(above, "gy", lambda i: i - 1)
    right = send(left, "gx", lambda i: i - 1)
    ny, nx = lax.axis_size("gy"), lax.axis_size("gx")
    diag = lax.ppermute(
        corner,
        ("gy", "gx"),
        [
            (a * nx + b, (a - 1) % ny * nx + (b - 1) % nx)
            for a in range(ny)
            for b in range(nx)
        ],
    )
    cot = cotangent.reshape(WIN, 2, WIN, D)
    db, da, tis, live = branch(cot, tissue[0], w_proj)
    keep0, send0, att0, dqkv0, xw, hid = first_heads(
        mine, below, right, diag, tis, live, w_qkv, da
    )
    came = send(send0, "gy", lambda i: i ^ 1)
    hid_t = turn(hid, tis)
    came, hid_t = tie(came, hid_t)
    first = add(keep0, came)
    low_a, high_a = blocks(first[:, :D]), blocks(first[:, D:])
    low_a, high_a, hid_t = tie(low_a, high_a, hid_t)
    came_a = ring_start(low_a, high_a, "dp", 1)
    keep1, send1, att1, dqkv1 = last_heads(hid, hid_t, tis, live, w_qkv, da)
    came_a, send1, att1 = tie(came_a, send1, att1)
    came_a = ring_pass(low_a, high_a, came_a, "dp", 1)
    came = send(send1, "gy", lambda i: i ^ 1)
    keep2, send2 = proj_grad(att0, att1, db)
    came, send2, keep2 = tie(came, send2, keep2)
    low_b = add(keep1, came)
    high_b = add(keep2, send(send2, "gy", lambda i: i ^ 1))
    low_b, high_b, att1 = tie(blocks(low_b), blocks(high_b), att1)
    came_b = ring_start(low_b, high_b, "gy", 2)
    out = out_part(xw, tis, att0, att1, w_proj)
    came_b, out, xw, low_a, high_a = tie(came_b, out, xw, low_a, high_a)
    came_b = ring_pass(low_b, high_b, came_b, "gy", 2)
    rows_a = ring_end(low_a, high_a, came_a)
    came_a = halve_start(rows_a, "gy", 2)
    grad = grad_part(xw, cot, tis, dqkv0, dqkv1, w_qkv)
    came_a, came_b, grad = tie(came_a, came_b, grad)
    rows_a = halve_end(rows_a, came_a)
    rows_b = ring_end(low_b, high_b, came_b)
    came_a = halve_start(rows_a, "gy", 6)
    came_b = halve_start(rows_b, "dp", 1)
    rows_b = halve_end(rows_b, came_b)
    came_b = halve_start(rows_b, "dp", 3)
    rows = jnp.concatenate([halve_end(rows_a, came_a), halve_end(rows_b, came_b)], 1)
    grad_qkv, grad_proj = finish(exchange(rows, ("gx",)))
    return out, grad, grad_qkv, grad_proj


def solution(mesh):
    block = P("dp", "gy", "gx", None)
    in_specs = (block, block, P("dp", "gy", "gx"), P(), P())
    out_specs = (block, block, P(("dp", "gy", "gx"), None), P(("dp", "gy", "gx"), None))
    return jax.shard_map(
        shards, mesh=mesh, in_specs=in_specs, out_specs=out_specs, check_vma=False
    )
```

```python
import math

import jax
import jax.numpy as jnp
from jax import lax
from jax.experimental import pallas as pl
from jax.experimental.pallas import tpu as pltpu
from jax.sharding import PartitionSpec as P

F32 = jnp.float32
BF = jnp.bfloat16
D = 768
WIN = 16
CELLS = WIN * WIN
GROUPS = 3
GW = D // GROUPS
HEAD_SCALE = 0.125
VMEM = 32 * 1024 * 1024


def nn(a, b):
    return lax.dot_general(a, b, (((1,), (0,)), ((), ())), preferred_element_type=F32)


def nt(a, b):
    return lax.dot_general(a, b, (((1,), (1,)), ((), ())), preferred_element_type=F32)


def tn(a, b):
    return lax.dot_general(a, b, (((0,), (0,)), ((), ())), preferred_element_type=F32)


def full(shape):
    return pl.BlockSpec(shape, lambda *g: (0,) * len(shape))


def cost(flops, size):
    return pl.CostEstimate(flops=int(flops), bytes_accessed=int(size), transcendentals=0)


def above_kernel(tiles_ref, above_ref):
    above_ref[...] = tiles_ref[...].astype(F32)[:, 8:].astype(BF)


def left_kernel(tiles_ref, after_ref, left_ref, corner_ref):
    tiles = tiles_ref[...].astype(F32)[:, :8].astype(BF)
    corner_ref[...] = tiles[:8]
    left_ref[...] = tiles[8:]


def edges(tiles):
    small = jax.ShapeDtypeStruct((8, 8, D), BF)
    above = pl.pallas_call(
        above_kernel,
        grid=(1,),
        in_specs=[pl.BlockSpec((8, 32, D), lambda g: (0, 0, 0))],
        out_specs=full((8, 24, D)),
        out_shape=jax.ShapeDtypeStruct((8, 24, D), BF),
        compiler_params=pltpu.CompilerParams(vmem_limit_bytes=VMEM),
        cost_estimate=cost(3e10, 1e6),
        name="above",
    )(tiles)
    left, corner = pl.pallas_call(
        left_kernel,
        grid=(1,),
        in_specs=[
            pl.BlockSpec((16, 16, D), lambda g: (0, 0, 0)),
            pl.BlockSpec(memory_space=pl.ANY),
        ],
        out_specs=[full((8, 8, D))] * 2,
        out_shape=[small, small],
        compiler_params=pltpu.CompilerParams(vmem_limit_bytes=VMEM),
        cost_estimate=cost(1e3, 1e3),
        name="left",
    )(tiles, above)
    return above, left, corner


def branch_kernel(
    cot_hbm, tissue_hbm, wp_hbm, db_ref, da_ref, tis_ref, live_ref, cot_ref, tissue_ref, wp_ref, sem
):
    copies = [
        pltpu.make_async_copy(tissue_hbm, tissue_ref, sem.at[0]),
        pltpu.make_async_copy(cot_hbm, cot_ref, sem.at[1]),
        pltpu.make_async_copy(wp_hbm, wp_ref, sem.at[2]),
    ]
    for copy in copies:
        copy.start()
    copies[0].wait()
    grid = tissue_ref[...].astype(F32).astype(BF)
    cell = lax.broadcasted_iota(jnp.int32, (CELLS, 1), 0)
    row_of = lax.broadcasted_iota(jnp.int32, (CELLS, WIN), 1) == (cell >> 4)
    rows = nn(row_of.astype(F32).astype(BF), grid)
    lane = lax.broadcasted_iota(jnp.int32, (CELLS, 2 * WIN), 1)
    ones = jnp.ones((2 * WIN, 128), BF)
    copies[1].wait()
    copies[2].wait()
    for w in range(2):
        own = jnp.where(lane == (cell & 15) + w * WIN, rows, 0.0).astype(BF)
        tis = nn(own, ones)
        some = jnp.max(jnp.max(tis, 0, keepdims=True), 1, keepdims=True)
        tis_ref[w] = tis.astype(BF)
        live_ref[w] = jnp.maximum(tis, 1.0 - some).astype(BF)
        db = cot_ref[:, w].reshape(CELLS, D) * jnp.tile(tis.astype(BF), (1, D // 128))
        db_ref[w] = db
        da_ref[w] = nt(db, wp_ref[...]).astype(BF)


def branch(cot, tissue, w_proj):
    shape = jax.ShapeDtypeStruct((2, CELLS, D), BF)
    mask = jax.ShapeDtypeStruct((2, CELLS, 128), BF)
    return pl.pallas_call(
        branch_kernel,
        in_specs=[pl.BlockSpec(memory_space=pltpu.HBM)] * 3,
        out_shape=[shape, shape, mask, mask],
        scratch_shapes=[
            pltpu.VMEM((WIN, 2, WIN, D), BF),
            pltpu.VMEM((WIN, 2 * WIN), jnp.int32),
            pltpu.VMEM((D, D), BF),
            pltpu.SemaphoreType.DMA((3,)),
        ],
        compiler_params=pltpu.CompilerParams(vmem_limit_bytes=VMEM),
        cost_estimate=cost(2e10, 4e6),
        name="branch",
    )(cot, tissue, w_proj)


def row_order():
    gy = lax.axis_index("gy")
    dp, y, core = lax.axis_index("dp"), gy >> 1, gy & 1
    at = lax.broadcasted_iota(jnp.int32, (D, 1), 0)
    third = ((at.astype(F32) + 0.5) * (1.0 / 3)).astype(jnp.int32)
    dp_of = ((third >> 6) & 1) ^ (((third >> 5) & 1) * 3) ^ dp
    y_of = ((third >> 4) & 1) ^ (((third >> 3) & 1) * 3) ^ y
    core_of = (third >> 7) ^ core
    source = ((dp_of * 8 + y_of * 2 + core_of) * 8 + (third & 7)) * 3 + at - third * 3
    column = lax.broadcasted_iota(jnp.int32, (D, D), 1)
    return jnp.where(column == source, 1.0, 0.0).astype(BF)


def moments(x):
    mean = jnp.mean(x, -1, keepdims=True)
    centred = x - mean
    inv = lax.rsqrt(jnp.mean(centred * centred, -1, keepdims=True) + 1e-05)
    return centred * inv, inv


def put(grad, keep_ref, send_ref, y_first):
    if y_first:
        size = D // 32
        places = [(c * 4 + x) * 4 + y for c in range(2) for y in range(4) for x in range(4)]
        grad = jnp.concatenate([grad[at * size : (at + 1) * size] for at in places], 0)
    keep_ref[...] = grad[: D // 2].astype(BF)
    send_ref[...] = grad[D // 2 :].astype(BF)


def heads_group(
    hid_ref, hid_t_ref, tis_ref, live_ref, wq_ref, wk_ref, wv_ref, da_ref,
    keep_ref, send_ref, att_ref, dqkv_ref, y_first,
):
    hidden = hid_ref[...].reshape(2 * CELLS, D)
    query = nn(hidden, wq_ref[...]).astype(BF) * BF(HEAD_SCALE)
    key = nn(hidden, wk_ref[...]).astype(BF)
    value = nn(hidden, wv_ref[...]).astype(BF)
    lane = lax.broadcasted_iota(jnp.int32, (1, 128), 1)
    sel = [(lane < 64).astype(BF), (lane >= 64).astype(BF)]
    units = [(w, p) for w in range(2) for p in range(2)]
    q, k, v, da, weight, ds, rinv, att = {}, {}, {}, {}, {}, {}, {}, {}
    for u in units:
        w, p = u
        rows, lanes = slice(w * CELLS, (w + 1) * CELLS), slice(p * 128, (p + 1) * 128)
        q[u] = query[rows, lanes]
        k[u] = key[rows, lanes] * tis_ref[w]
        v[u] = value[rows, lanes] * tis_ref[w]
        da[u] = da_ref[w, :, lanes]
    for u in units:
        for h in range(2):
            weight[u, h] = jnp.exp(nt(q[u], k[u] * sel[h])).astype(BF)
    for u in units:
        live = live_ref[u[0]]
        both = nn(weight[u, 0], jnp.concatenate([v[u] * sel[0], live * sel[0]], 1)) + nn(
            weight[u, 1], jnp.concatenate([v[u] * sel[1], live * sel[1]], 1)
        )
        rinv[u] = 1.0 / both[:, 128:]
        att[u] = both[:, :128] * rinv[u]
        att_ref[u[0], :, u[1] * 128 : (u[1] + 1) * 128] = att[u].astype(BF)
    for u in units:
        terms = da[u].astype(F32) * att[u]
        for h in range(2):
            delta = jnp.sum(terms * sel[h].astype(F32), 1, keepdims=True)
            dprobs = nt(da[u], v[u] * sel[h]) - delta
            ds[u, h] = (weight[u, h].astype(F32) * dprobs).astype(BF)
    for u in units:
        w, p = u
        dq = (nn(ds[u, 0], k[u] * sel[0]) + nn(ds[u, 1], k[u] * sel[1])) * (rinv[u] * HEAD_SCALE)
        dan = (da[u].astype(F32) * rinv[u]).astype(BF)
        qn = (q[u].astype(F32) * rinv[u]).astype(BF)
        dv = tn(weight[u, 0], dan * sel[0]) + tn(weight[u, 1], dan * sel[1])
        dk = tn(ds[u, 0], qn * sel[0]) + tn(ds[u, 1], qn * sel[1])
        for i, grad in enumerate((dq, dk, dv)):
            at = i * GW + p * 128
            dqkv_ref[0, w, :, at : at + 128] = grad.astype(BF)
    grad = nn(hid_t_ref[...], dqkv_ref[0].reshape(2 * CELLS, D))
    put(grad, keep_ref, send_ref, y_first)


def first_kernel(
    tiles_ref, below_ref, right_ref, diag_ref, tis_ref, live_ref,
    wq_ref, wk_ref, wv_ref, da_ref,
    keep_ref, send_ref, att_ref, dqkv_ref, xw_ref, hid_ref, hid_t_ref,
):
    @pl.when(pl.program_id(0) == 0)
    def _():
        own = tiles_ref[8:16].astype(F32)
        low = below_ref[...].astype(F32)
        right = right_ref[...].astype(F32)
        diag = diag_ref[...].astype(F32)
        perm = row_order()
        for w in range(2):
            if w == 0:
                top, bottom = own[:, 8:24], low[:, :16]
            else:
                top = jnp.concatenate([own[:, 24:32], right], 1)
                bottom = jnp.concatenate([low[:, 16:24], diag], 1)
            x = jnp.concatenate([top, bottom], 0).reshape(CELLS, D)
            xw_ref[w] = x.astype(BF)
            normed, _ = moments(x)
            hidden = normed.astype(BF)
            hid_ref[w] = hidden
            masked = hidden * jnp.tile(tis_ref[w], (1, D // 128))
            hid_t_ref[:, w * CELLS : (w + 1) * CELLS] = nt(perm, masked).astype(BF)

    heads_group(
        hid_ref, hid_t_ref, tis_ref, live_ref, wq_ref, wk_ref, wv_ref, da_ref,
        keep_ref, send_ref, att_ref, dqkv_ref, False,
    )


def last_kernel(*refs):
    heads_group(*refs, True)


def columns(block, first):
    return pl.BlockSpec((D, GW), lambda g: (0, block * GROUPS + first + g))


def heads_specs(first, groups):
    inputs = [
        full((2, CELLS, 128)), full((2, CELLS, 128)),
        columns(0, first), columns(1, first), columns(2, first),
        pl.BlockSpec((2, CELLS, GW), lambda g: (0, 0, first + g)),
    ]
    half = pl.BlockSpec((D // 2, D), lambda g: (0, g))
    outputs = [
        half, half,
        pl.BlockSpec((2, CELLS, GW), lambda g: (0, 0, g)),
        pl.BlockSpec((1, 2, CELLS, D), lambda g: (g, 0, 0, 0)),
    ]
    shapes = [
        jax.ShapeDtypeStruct((D // 2, groups * D), BF),
        jax.ShapeDtypeStruct((D // 2, groups * D), BF),
        jax.ShapeDtypeStruct((2, CELLS, groups * GW), BF),
        jax.ShapeDtypeStruct((groups, 2, CELLS, D), BF),
    ]
    return inputs, outputs, shapes


def first_heads(tiles, below, right, diag, tis, live, w_qkv, da):
    inputs, outputs, shapes = heads_specs(0, 2)
    rows = jax.ShapeDtypeStruct((2, CELLS, D), BF)
    return pl.pallas_call(
        first_kernel,
        grid=(2,),
        in_specs=[full((16, 32, D)), full((8, 24, D)), full((8, 8, D)), full((8, 8, D))] + inputs,
        out_specs=outputs + [full((2, CELLS, D))] * 2 + [full((D, 2 * CELLS))],
        out_shape=shapes + [rows, rows, jax.ShapeDtypeStruct((D, 2 * CELLS), BF)],
        compiler_params=pltpu.CompilerParams(vmem_limit_bytes=VMEM),
        cost_estimate=cost(6e9, 10e6),
        name="first_heads",
    )(tiles, below, right, diag, tis, live, w_qkv, w_qkv, w_qkv, da)


def last_heads(hid, hid_t, tis, live, w_qkv, da):
    inputs, outputs, shapes = heads_specs(2, 1)
    return pl.pallas_call(
        last_kernel,
        grid=(1,),
        in_specs=[full((2, CELLS, D)), full((D, 2 * CELLS))] + inputs,
        out_specs=outputs,
        out_shape=shapes,
        compiler_params=pltpu.CompilerParams(vmem_limit_bytes=VMEM),
        cost_estimate=cost(4e9, 6e6),
        name="last_heads",
    )(hid, hid_t, tis, live, w_qkv, w_qkv, w_qkv, da)


def proj_kernel(att0_ref, att1_ref, db_ref, keep_ref, send_ref):
    attended = jnp.concatenate([att0_ref[...], att1_ref[...]], 2).reshape(2 * CELLS, D)
    att_t = nt(row_order(), attended).astype(BF)
    put(nn(att_t, db_ref[...].reshape(2 * CELLS, D)), keep_ref, send_ref, True)


def proj_grad(att0, att1, db):
    shape = jax.ShapeDtypeStruct((D // 2, D), BF)
    return pl.pallas_call(
        proj_kernel,
        out_shape=[shape, shape],
        compiler_params=pltpu.CompilerParams(vmem_limit_bytes=VMEM),
        cost_estimate=cost(2e9, 4e6),
        name="proj_grad",
    )(att0, att1, db)


def out_kernel(xw_ref, tis_ref, att0_ref, att1_ref, wp_ref, out_ref):
    for w in range(2):
        tis = jnp.tile(tis_ref[w].astype(F32), (1, D // 128))
        attended = jnp.concatenate([att0_ref[w], att1_ref[w]], 1)
        out = xw_ref[w].astype(F32) + tis * nn(attended, wp_ref[...])
        out_ref[:, w] = out.astype(BF).reshape(WIN, WIN, D)


def out_part(xw, tis, att0, att1, w_proj):
    out = pl.pallas_call(
        out_kernel,
        out_shape=jax.ShapeDtypeStruct((WIN, 2, WIN, D), BF),
        compiler_params=pltpu.CompilerParams(vmem_limit_bytes=VMEM),
        cost_estimate=cost(1e3, 1e3),
        name="out_part",
    )(xw, tis, att0, att1, w_proj)
    return out.reshape(1, WIN, 2 * WIN, D)


def grad_kernel(
    xw_ref, cot_ref, tis_ref, dqkv0_ref, dqkv1_ref, wq_ref, wk_ref, wv_ref, grad_ref, acc_ref
):
    step = pl.program_id(0)
    weights = jnp.concatenate([wq_ref[...], wk_ref[...], wv_ref[...]], 1)
    dqkv = jnp.where(step < GROUPS - 1, dqkv0_ref[0], dqkv1_ref[0])
    part = nt(dqkv.reshape(2 * CELLS, D), weights)

    @pl.when(step == 0)
    def _():
        acc_ref[...] = part

    @pl.when((step > 0) & (step < GROUPS - 1))
    def _():
        acc_ref[...] += part

    @pl.when(step == GROUPS - 1)
    def _():
        acc_ref[...] += part
        for w in range(2):
            normed, inv = moments(xw_ref[w].astype(F32))
            tis = jnp.tile(tis_ref[w].astype(F32), (1, D // 128))
            dh = acc_ref[w * CELLS : (w + 1) * CELLS] * tis
            dnorm = inv * (
                dh
                - jnp.mean(dh, -1, keepdims=True)
                - normed * jnp.mean(dh * normed, -1, keepdims=True)
            )
            grad = cot_ref[:, w].reshape(CELLS, D).astype(F32) + dnorm
            grad_ref[:, w] = grad.astype(BF).reshape(WIN, WIN, D)


def grad_part(xw, cot, tis, dqkv0, dqkv1, w_qkv):
    grad = pl.pallas_call(
        grad_kernel,
        grid=(GROUPS,),
        in_specs=[
            full((2, CELLS, D)), full((WIN, 2, WIN, D)), full((2, CELLS, 128)),
            pl.BlockSpec((1, 2, CELLS, D), lambda g: (jnp.minimum(g, 1), 0, 0, 0)),
            full((1, 2, CELLS, D)),
            columns(0, 0), columns(1, 0), columns(2, 0),
        ],
        out_specs=full((WIN, 2, WIN, D)),
        out_shape=jax.ShapeDtypeStruct((WIN, 2, WIN, D), BF),
        scratch_shapes=[pltpu.VMEM((2 * CELLS, D), F32)],
        compiler_params=pltpu.CompilerParams(vmem_limit_bytes=VMEM),
        cost_estimate=cost(1e3, 1e3),
        name="grad_part",
    )(xw, cot, tis, dqkv0, dqkv1, w_qkv, w_qkv, w_qkv)
    return grad.reshape(1, WIN, 2 * WIN, D)


def finish_kernel(parts_ref, qkv_ref, proj_ref):
    total = parts_ref[0].astype(F32)
    for part in range(1, parts_ref.shape[0]):
        total = total + parts_ref[part].astype(F32)
    total = total * (1.0 / math.sqrt(512))
    for i in range(3):
        for g in range(GROUPS):
            at = g * D + i * GW
            qkv_ref[:, i * D + g * GW : i * D + (g + 1) * GW] = total[:, at : at + GW]
    proj_ref[...] = total[:, 3 * D :]


def finish(parts):
    rows = parts.shape[1]
    return pl.pallas_call(
        finish_kernel,
        out_shape=[
            jax.ShapeDtypeStruct((rows, 3 * D), F32),
            jax.ShapeDtypeStruct((rows, D), F32),
        ],
        compiler_params=pltpu.CompilerParams(vmem_limit_bytes=VMEM),
        name="finish",
    )(parts)


def send(value, axis, move):
    devices = lax.axis_size(axis)
    return lax.ppermute(value, axis, [(i, move(i) % devices) for i in range(devices)])


def add(*terms):
    total = terms[0].astype(F32)
    for term in terms[1:]:
        total = total + term.astype(F32)
    return total.astype(BF)


def ring_start(low, high, axis, flips):
    one, three = flips
    return send(low[3], axis, lambda j: j ^ one), send(high[3], axis, lambda j: j ^ three)


def ring_pass(low, high, came, axis, flips):
    one, three = flips
    to_one = jnp.concatenate([low[2], add(high[2], came[1])], 1)
    to_three = jnp.concatenate([add(low[1], came[0]), high[1]], 1)
    return send(to_one, axis, lambda j: j ^ one), send(to_three, axis, lambda j: j ^ three)


def ring_end(low, high, came):
    n = low.shape[2]
    up, down = came
    low = add(low[0], up[:, :n], down[:, :n])
    high = add(high[0], up[:, n:], down[:, n:])
    return jnp.concatenate([low, high], 1)


def halve_start(rows, axis, flip):
    return send(rows[rows.shape[0] // 2 :], axis, lambda j: j ^ flip)


def halve_end(rows, came):
    return add(rows[: rows.shape[0] // 2], came)


def exchange(rows, axis, groups=None):
    parts = len(groups[0]) if groups else math.prod(lax.axis_size(a) for a in axis)
    rows = rows.reshape(parts, rows.shape[0] // parts, rows.shape[1])
    return lax.all_to_all(rows, axis, 0, 0, axis_index_groups=groups)


def tie(*values):
    return lax.optimization_barrier(values)


def blocks(value):
    return value.reshape(4, value.shape[0] // 4, value.shape[1])


def shards(tiles, cotangent, tissue, w_qkv, w_proj):
    mine = tiles[0]
    above, left, corner = edges(mine)
    below = send(above, "gy", lambda i: i - 1)
    right = send(left, "gx", lambda i: i - 1)
    ny, nx = lax.axis_size("gy"), lax.axis_size("gx")
    diag = lax.ppermute(
        corner,
        ("gy", "gx"),
        [
            (a * nx + b, (a - 1) % ny * nx + (b - 1) % nx)
            for a in range(ny)
            for b in range(nx)
        ],
    )
    cot = cotangent.reshape(WIN, 2, WIN, D)
    db, da, tis, live = branch(cot, tissue[0], w_proj)
    along_x, along_y = ("dp", (1, 3)), ("gy", (2, 6))
    keep0, send0, att0, dqkv0, xw, hid, hid_t = first_heads(
        mine, below, right, diag, tis, live, w_qkv, da
    )
    came = send(send0, "gy", lambda i: i ^ 1)
    keep1, send1, att1, dqkv1 = last_heads(hid, hid_t, tis, live, w_qkv, da)
    came, send1, att1 = tie(came, send1, att1)
    first = add(keep0, came)
    low_a, high_a = blocks(first[:, :D]), blocks(first[:, D:])
    low_a, high_a, att1 = tie(low_a, high_a, att1)
    came_a = ring_start(low_a, high_a, *along_x)
    came = send(send1, "gy", lambda i: i ^ 1)
    keep2, send2 = proj_grad(att0, att1, db)
    came_a, came, send2, keep2 = tie(came_a, came, send2, keep2)
    came_a = ring_pass(low_a, high_a, came_a, *along_x)
    low_b = add(keep1, came)
    high_b = add(keep2, send(send2, "gy", lambda i: i ^ 1))
    low_b, high_b, att1 = tie(blocks(low_b), blocks(high_b), att1)
    came_b = ring_start(low_b, high_b, *along_y)
    out = out_part(xw, tis, att0, att1, w_proj)
    came_b, out, xw, low_a, high_a = tie(came_b, out, xw, low_a, high_a)
    came_b = ring_pass(low_b, high_b, came_b, *along_y)
    rows_a = ring_end(low_a, high_a, came_a)
    came_a = halve_start(rows_a, "gy", 2)
    grad = grad_part(xw, cot, tis, dqkv0, dqkv1, w_qkv)
    came_a, came_b, grad = tie(came_a, came_b, grad)
    rows_a = halve_end(rows_a, came_a)
    rows_b = ring_end(low_b, high_b, came_b)
    came_a = halve_start(rows_a, "gy", 6)
    came_b = halve_start(rows_b, "dp", 1)
    rows_b = halve_end(rows_b, came_b)
    came_b = halve_start(rows_b, "dp", 3)
    rows = jnp.concatenate([halve_end(rows_a, came_a), halve_end(rows_b, came_b)], 1)
    grad_qkv, grad_proj = finish(exchange(rows, ("gx",)))
    return out, grad, grad_qkv, grad_proj


def solution(mesh):
    block = P("dp", "gy", "gx", None)
    in_specs = (block, block, P("dp", "gy", "gx"), P(), P())
    out_specs = (block, block, P(("dp", "gy", "gx"), None), P(("dp", "gy", "gx"), None))
    return jax.shard_map(
        shards, mesh=mesh, in_specs=in_specs, out_specs=out_specs, check_vma=False
    )
```

```python
import math

import jax
import jax.numpy as jnp
from jax import lax
from jax.experimental import pallas as pl
from jax.experimental.pallas import tpu as pltpu
from jax.sharding import PartitionSpec as P

F32 = jnp.float32
BF = jnp.bfloat16
D = 768
WIN = 16
CELLS = WIN * WIN
GROUPS = 3
GW = D // GROUPS
HEAD_SCALE = 0.125
VMEM = 32 * 1024 * 1024


def nn(a, b):
    return lax.dot_general(a, b, (((1,), (0,)), ((), ())), preferred_element_type=F32)


def nt(a, b):
    return lax.dot_general(a, b, (((1,), (1,)), ((), ())), preferred_element_type=F32)


def tn(a, b):
    return lax.dot_general(a, b, (((0,), (0,)), ((), ())), preferred_element_type=F32)


def full(shape):
    return pl.BlockSpec(shape, lambda *g: (0,) * len(shape))


def cost(flops, size):
    return pl.CostEstimate(flops=int(flops), bytes_accessed=int(size), transcendentals=0)


def above_kernel(tiles_ref, above_ref):
    above_ref[...] = tiles_ref[...].astype(F32)[:, 8:].astype(BF)


def left_kernel(tiles_ref, after_ref, left_ref, corner_ref):
    tiles = tiles_ref[...].astype(F32)[:, :8].astype(BF)
    corner_ref[...] = tiles[:8]
    left_ref[...] = tiles[8:]


def edges(tiles):
    small = jax.ShapeDtypeStruct((8, 8, D), BF)
    above = pl.pallas_call(
        above_kernel,
        grid=(1,),
        in_specs=[pl.BlockSpec((8, 32, D), lambda g: (0, 0, 0))],
        out_specs=full((8, 24, D)),
        out_shape=jax.ShapeDtypeStruct((8, 24, D), BF),
        compiler_params=pltpu.CompilerParams(vmem_limit_bytes=VMEM),
        cost_estimate=cost(3e10, 1e6),
        name="above",
    )(tiles)
    left, corner = pl.pallas_call(
        left_kernel,
        grid=(1,),
        in_specs=[
            pl.BlockSpec((16, 16, D), lambda g: (0, 0, 0)),
            pl.BlockSpec(memory_space=pl.ANY),
        ],
        out_specs=[full((8, 8, D))] * 2,
        out_shape=[small, small],
        compiler_params=pltpu.CompilerParams(vmem_limit_bytes=VMEM),
        cost_estimate=cost(1e3, 1e3),
        name="left",
    )(tiles, above)
    return above, left, corner


def branch_kernel(
    cot_hbm, tissue_hbm, wp_hbm, db_ref, da_ref, tis_ref, live_ref, cot_ref, tissue_ref, wp_ref, sem
):
    copies = [
        pltpu.make_async_copy(tissue_hbm, tissue_ref, sem.at[0]),
        pltpu.make_async_copy(cot_hbm, cot_ref, sem.at[1]),
        pltpu.make_async_copy(wp_hbm, wp_ref, sem.at[2]),
    ]
    for copy in copies:
        copy.start()
    copies[0].wait()
    grid = tissue_ref[...].astype(F32).astype(BF)
    cell = lax.broadcasted_iota(jnp.int32, (CELLS, 1), 0)
    row_of = lax.broadcasted_iota(jnp.int32, (CELLS, WIN), 1) == (cell >> 4)
    rows = nn(row_of.astype(F32).astype(BF), grid)
    lane = lax.broadcasted_iota(jnp.int32, (CELLS, 2 * WIN), 1)
    ones = jnp.ones((2 * WIN, 128), BF)
    copies[1].wait()
    copies[2].wait()
    for w in range(2):
        own = jnp.where(lane == (cell & 15) + w * WIN, rows, 0.0).astype(BF)
        tis = nn(own, ones)
        some = jnp.max(jnp.max(tis, 0, keepdims=True), 1, keepdims=True)
        tis_ref[w] = tis.astype(BF)
        live_ref[w] = jnp.maximum(tis, 1.0 - some).astype(BF)
        db = cot_ref[:, w].reshape(CELLS, D) * jnp.tile(tis.astype(BF), (1, D // 128))
        db_ref[w] = db
        da_ref[w] = nt(db, wp_ref[...]).astype(BF)


def branch(cot, tissue, w_proj):
    shape = jax.ShapeDtypeStruct((2, CELLS, D), BF)
    mask = jax.ShapeDtypeStruct((2, CELLS, 128), BF)
    return pl.pallas_call(
        branch_kernel,
        in_specs=[pl.BlockSpec(memory_space=pltpu.HBM)] * 3,
        out_shape=[shape, shape, mask, mask],
        scratch_shapes=[
            pltpu.VMEM((WIN, 2, WIN, D), BF),
            pltpu.VMEM((WIN, 2 * WIN), jnp.int32),
            pltpu.VMEM((D, D), BF),
            pltpu.SemaphoreType.DMA((3,)),
        ],
        compiler_params=pltpu.CompilerParams(vmem_limit_bytes=VMEM),
        cost_estimate=cost(2e10, 4e6),
        name="branch",
    )(cot, tissue, w_proj)


def row_order():
    gy = lax.axis_index("gy")
    dp, y, core = lax.axis_index("dp"), gy >> 1, gy & 1
    at = lax.broadcasted_iota(jnp.int32, (D, 1), 0)
    third = ((at.astype(F32) + 0.5) * (1.0 / 3)).astype(jnp.int32)
    dp_of = ((third >> 6) & 1) ^ (((third >> 5) & 1) * 3) ^ dp
    y_of = ((third >> 4) & 1) ^ (((third >> 3) & 1) * 3) ^ y
    core_of = (third >> 7) ^ core
    source = ((dp_of * 8 + y_of * 2 + core_of) * 8 + (third & 7)) * 3 + at - third * 3
    column = lax.broadcasted_iota(jnp.int32, (D, D), 1)
    return jnp.where(column == source, 1.0, 0.0).astype(BF)


def moments(x):
    mean = jnp.mean(x, -1, keepdims=True)
    centred = x - mean
    inv = lax.rsqrt(jnp.mean(centred * centred, -1, keepdims=True) + 1e-05)
    return centred * inv, inv


def put(grad, keep_ref, send_ref, y_first):
    if y_first:
        size = D // 32
        places = [(c * 4 + x) * 4 + y for c in range(2) for y in range(4) for x in range(4)]
        grad = jnp.concatenate([grad[at * size : (at + 1) * size] for at in places], 0)
    keep_ref[...] = grad[: D // 2].astype(BF)
    send_ref[...] = grad[D // 2 :].astype(BF)


def heads_group(
    hid_ref, hid_t_ref, tis_ref, live_ref, wq_ref, wk_ref, wv_ref, da_ref,
    keep_ref, send_ref, att_ref, dqkv_ref, y_first,
):
    hidden = hid_ref[...].reshape(2 * CELLS, D)
    query = nn(hidden, wq_ref[...]).astype(BF) * BF(HEAD_SCALE)
    key = nn(hidden, wk_ref[...]).astype(BF)
    value = nn(hidden, wv_ref[...]).astype(BF)
    lane = lax.broadcasted_iota(jnp.int32, (1, 128), 1)
    sel = [(lane < 64).astype(BF), (lane >= 64).astype(BF)]
    units = [(w, p) for w in range(2) for p in range(2)]
    q, k, v, da, weight, ds, rinv, att = {}, {}, {}, {}, {}, {}, {}, {}
    for u in units:
        w, p = u
        rows, lanes = slice(w * CELLS, (w + 1) * CELLS), slice(p * 128, (p + 1) * 128)
        q[u] = query[rows, lanes]
        k[u] = key[rows, lanes] * tis_ref[w]
        v[u] = value[rows, lanes] * tis_ref[w]
        da[u] = da_ref[w, :, lanes]
    for u in units:
        for h in range(2):
            weight[u, h] = jnp.exp(nt(q[u], k[u] * sel[h])).astype(BF)
    for u in units:
        live = live_ref[u[0]]
        both = nn(weight[u, 0], jnp.concatenate([v[u] * sel[0], live * sel[0]], 1)) + nn(
            weight[u, 1], jnp.concatenate([v[u] * sel[1], live * sel[1]], 1)
        )
        rinv[u] = 1.0 / both[:, 128:]
        att[u] = both[:, :128] * rinv[u]
        att_ref[u[0], :, u[1] * 128 : (u[1] + 1) * 128] = att[u].astype(BF)
    for u in units:
        terms = da[u].astype(F32) * att[u]
        for h in range(2):
            delta = jnp.sum(terms * sel[h].astype(F32), 1, keepdims=True)
            dprobs = nt(da[u], v[u] * sel[h]) - delta
            ds[u, h] = (weight[u, h].astype(F32) * dprobs).astype(BF)
    for u in units:
        w, p = u
        dq = (nn(ds[u, 0], k[u] * sel[0]) + nn(ds[u, 1], k[u] * sel[1])) * (rinv[u] * HEAD_SCALE)
        dan = (da[u].astype(F32) * rinv[u]).astype(BF)
        qn = (q[u].astype(F32) * rinv[u]).astype(BF)
        dv = tn(weight[u, 0], dan * sel[0]) + tn(weight[u, 1], dan * sel[1])
        dk = tn(ds[u, 0], qn * sel[0]) + tn(ds[u, 1], qn * sel[1])
        for i, grad in enumerate((dq, dk, dv)):
            at = i * GW + p * 128
            dqkv_ref[0, w, :, at : at + 128] = grad.astype(BF)
    grad = nn(hid_t_ref[...], dqkv_ref[0].reshape(2 * CELLS, D))
    put(grad, keep_ref, send_ref, y_first)


def first_kernel(
    tiles_ref, below_ref, right_ref, diag_ref, tis_ref, live_ref,
    wq_ref, wk_ref, wv_ref, da_ref,
    keep_ref, send_ref, att_ref, dqkv_ref, xw_ref, hid_ref, hid_t_ref,
):
    @pl.when(pl.program_id(0) == 0)
    def _():
        own = tiles_ref[8:16].astype(F32)
        low = below_ref[...].astype(F32)
        right = right_ref[...].astype(F32)
        diag = diag_ref[...].astype(F32)
        perm = row_order()
        for w in range(2):
            if w == 0:
                top, bottom = own[:, 8:24], low[:, :16]
            else:
                top = jnp.concatenate([own[:, 24:32], right], 1)
                bottom = jnp.concatenate([low[:, 16:24], diag], 1)
            x = jnp.concatenate([top, bottom], 0).reshape(CELLS, D)
            xw_ref[w] = x.astype(BF)
            normed, _ = moments(x)
            hidden = normed.astype(BF)
            hid_ref[w] = hidden
            masked = hidden * jnp.tile(tis_ref[w], (1, D // 128))
            hid_t_ref[:, w * CELLS : (w + 1) * CELLS] = nt(perm, masked).astype(BF)

    heads_group(
        hid_ref, hid_t_ref, tis_ref, live_ref, wq_ref, wk_ref, wv_ref, da_ref,
        keep_ref, send_ref, att_ref, dqkv_ref, False,
    )


def last_kernel(
    hid_ref, hid_t_ref, tis_ref, live_ref, wq_ref, wk_ref, wv_ref, da_ref, att0_ref, db_ref,
    keep_ref, send_ref, att_ref, dqkv_ref,
):
    heads_group(
        hid_ref, hid_t_ref, tis_ref, live_ref, wq_ref, wk_ref, wv_ref, da_ref,
        keep_ref.at[:, :D], send_ref.at[:, :D], att_ref, dqkv_ref, True,
    )
    attended = jnp.concatenate([att0_ref[...], att_ref[...]], 2).reshape(2 * CELLS, D)
    att_t = nt(row_order(), attended).astype(BF)
    grad = nn(att_t, db_ref[...].reshape(2 * CELLS, D))
    put(grad, keep_ref.at[:, D:], send_ref.at[:, D:], True)


def columns(block, first):
    return pl.BlockSpec((D, GW), lambda g: (0, block * GROUPS + first + g))


def heads_specs(first, groups):
    inputs = [
        full((2, CELLS, 128)), full((2, CELLS, 128)),
        columns(0, first), columns(1, first), columns(2, first),
        pl.BlockSpec((2, CELLS, GW), lambda g: (0, 0, first + g)),
    ]
    half = pl.BlockSpec((D // 2, D), lambda g: (0, g))
    outputs = [
        half, half,
        pl.BlockSpec((2, CELLS, GW), lambda g: (0, 0, g)),
        pl.BlockSpec((1, 2, CELLS, D), lambda g: (g, 0, 0, 0)),
    ]
    shapes = [
        jax.ShapeDtypeStruct((D // 2, groups * D), BF),
        jax.ShapeDtypeStruct((D // 2, groups * D), BF),
        jax.ShapeDtypeStruct((2, CELLS, groups * GW), BF),
        jax.ShapeDtypeStruct((groups, 2, CELLS, D), BF),
    ]
    return inputs, outputs, shapes


def first_heads(tiles, below, right, diag, tis, live, w_qkv, da):
    inputs, outputs, shapes = heads_specs(0, 2)
    rows = jax.ShapeDtypeStruct((2, CELLS, D), BF)
    return pl.pallas_call(
        first_kernel,
        grid=(2,),
        in_specs=[full((16, 32, D)), full((8, 24, D)), full((8, 8, D)), full((8, 8, D))] + inputs,
        out_specs=outputs + [full((2, CELLS, D))] * 2 + [full((D, 2 * CELLS))],
        out_shape=shapes + [rows, rows, jax.ShapeDtypeStruct((D, 2 * CELLS), BF)],
        compiler_params=pltpu.CompilerParams(vmem_limit_bytes=VMEM),
        cost_estimate=cost(6e9, 10e6),
        name="first_heads",
    )(tiles, below, right, diag, tis, live, w_qkv, w_qkv, w_qkv, da)


def last_heads(hid, hid_t, tis, live, w_qkv, da, att0, db):
    inputs, outputs, shapes = heads_specs(2, 1)
    half = jax.ShapeDtypeStruct((D // 2, 2 * D), BF)
    rows = full((2, CELLS, D))
    return pl.pallas_call(
        last_kernel,
        grid=(1,),
        in_specs=[rows, full((D, 2 * CELLS))] + inputs + [full((2, CELLS, 2 * GW)), rows],
        out_specs=[full((D // 2, 2 * D))] * 2 + outputs[2:],
        out_shape=[half, half] + shapes[2:],
        compiler_params=pltpu.CompilerParams(vmem_limit_bytes=VMEM),
        cost_estimate=cost(4e9, 6e6),
        name="last_heads",
    )(hid, hid_t, tis, live, w_qkv, w_qkv, w_qkv, da, att0, db)


def out_kernel(xw_ref, tis_ref, att0_ref, att1_ref, wp_ref, out_ref):
    for w in range(2):
        tis = jnp.tile(tis_ref[w].astype(F32), (1, D // 128))
        attended = jnp.concatenate([att0_ref[w], att1_ref[w]], 1)
        out = xw_ref[w].astype(F32) + tis * nn(attended, wp_ref[...])
        out_ref[:, w] = out.astype(BF).reshape(WIN, WIN, D)


def out_part(xw, tis, att0, att1, w_proj):
    out = pl.pallas_call(
        out_kernel,
        out_shape=jax.ShapeDtypeStruct((WIN, 2, WIN, D), BF),
        compiler_params=pltpu.CompilerParams(vmem_limit_bytes=VMEM),
        cost_estimate=cost(1e3, 1e3),
        name="out_part",
    )(xw, tis, att0, att1, w_proj)
    return out.reshape(1, WIN, 2 * WIN, D)


def grad_kernel(
    xw_ref, cot_ref, tis_ref, dqkv0_ref, dqkv1_ref, wq_ref, wk_ref, wv_ref, grad_ref, acc_ref
):
    step = pl.program_id(0)
    weights = jnp.concatenate([wq_ref[...], wk_ref[...], wv_ref[...]], 1)
    dqkv = jnp.where(step < GROUPS - 1, dqkv0_ref[0], dqkv1_ref[0])
    part = nt(dqkv.reshape(2 * CELLS, D), weights)

    @pl.when(step == 0)
    def _():
        acc_ref[...] = part

    @pl.when((step > 0) & (step < GROUPS - 1))
    def _():
        acc_ref[...] += part

    @pl.when(step == GROUPS - 1)
    def _():
        acc_ref[...] += part
        for w in range(2):
            normed, inv = moments(xw_ref[w].astype(F32))
            tis = jnp.tile(tis_ref[w].astype(F32), (1, D // 128))
            dh = acc_ref[w * CELLS : (w + 1) * CELLS] * tis
            dnorm = inv * (
                dh
                - jnp.mean(dh, -1, keepdims=True)
                - normed * jnp.mean(dh * normed, -1, keepdims=True)
            )
            grad = cot_ref[:, w].reshape(CELLS, D).astype(F32) + dnorm
            grad_ref[:, w] = grad.astype(BF).reshape(WIN, WIN, D)


def grad_part(xw, cot, tis, dqkv0, dqkv1, w_qkv):
    grad = pl.pallas_call(
        grad_kernel,
        grid=(GROUPS,),
        in_specs=[
            full((2, CELLS, D)), full((WIN, 2, WIN, D)), full((2, CELLS, 128)),
            pl.BlockSpec((1, 2, CELLS, D), lambda g: (jnp.minimum(g, 1), 0, 0, 0)),
            full((1, 2, CELLS, D)),
            columns(0, 0), columns(1, 0), columns(2, 0),
        ],
        out_specs=full((WIN, 2, WIN, D)),
        out_shape=jax.ShapeDtypeStruct((WIN, 2, WIN, D), BF),
        scratch_shapes=[pltpu.VMEM((2 * CELLS, D), F32)],
        compiler_params=pltpu.CompilerParams(vmem_limit_bytes=VMEM),
        cost_estimate=cost(1e3, 1e3),
        name="grad_part",
    )(xw, cot, tis, dqkv0, dqkv1, w_qkv, w_qkv, w_qkv)
    return grad.reshape(1, WIN, 2 * WIN, D)


def finish_kernel(parts_ref, qkv_ref, proj_ref):
    total = parts_ref[0].astype(F32)
    for part in range(1, parts_ref.shape[0]):
        total = total + parts_ref[part].astype(F32)
    total = total * (1.0 / math.sqrt(512))
    for i in range(3):
        for g in range(GROUPS):
            at = g * D + i * GW
            qkv_ref[:, i * D + g * GW : i * D + (g + 1) * GW] = total[:, at : at + GW]
    proj_ref[...] = total[:, 3 * D :]


def finish(parts):
    rows = parts.shape[1]
    return pl.pallas_call(
        finish_kernel,
        out_shape=[
            jax.ShapeDtypeStruct((rows, 3 * D), F32),
            jax.ShapeDtypeStruct((rows, D), F32),
        ],
        compiler_params=pltpu.CompilerParams(vmem_limit_bytes=VMEM),
        name="finish",
    )(parts)


def send(value, axis, move):
    devices = lax.axis_size(axis)
    return lax.ppermute(value, axis, [(i, move(i) % devices) for i in range(devices)])


def add(*terms):
    total = terms[0].astype(F32)
    for term in terms[1:]:
        total = total + term.astype(F32)
    return total.astype(BF)


def ring_start(low, high, axis, flips):
    one, three = flips
    return send(low[3], axis, lambda j: j ^ one), send(high[3], axis, lambda j: j ^ three)


def ring_pass(low, high, came, axis, flips):
    one, three = flips
    to_one = jnp.concatenate([low[2], add(high[2], came[1])], 1)
    to_three = jnp.concatenate([add(low[1], came[0]), high[1]], 1)
    return send(to_one, axis, lambda j: j ^ one), send(to_three, axis, lambda j: j ^ three)


def ring_end(low, high, came):
    n = low.shape[2]
    up, down = came
    low = add(low[0], up[:, :n], down[:, :n])
    high = add(high[0], up[:, n:], down[:, n:])
    return jnp.concatenate([low, high], 1)


def halve_start(rows, axis, flip):
    return send(rows[rows.shape[0] // 2 :], axis, lambda j: j ^ flip)


def halve_end(rows, came):
    return add(rows[: rows.shape[0] // 2], came)


def exchange(rows, axis, groups=None):
    parts = len(groups[0]) if groups else math.prod(lax.axis_size(a) for a in axis)
    rows = rows.reshape(parts, rows.shape[0] // parts, rows.shape[1])
    return lax.all_to_all(rows, axis, 0, 0, axis_index_groups=groups)


def tie(*values):
    return lax.optimization_barrier(values)


def blocks(value):
    return value.reshape(4, value.shape[0] // 4, value.shape[1])


def shards(tiles, cotangent, tissue, w_qkv, w_proj):
    mine = tiles[0]
    above, left, corner = edges(mine)
    below = send(above, "gy", lambda i: i - 1)
    right = send(left, "gx", lambda i: i - 1)
    ny, nx = lax.axis_size("gy"), lax.axis_size("gx")
    diag = lax.ppermute(
        corner,
        ("gy", "gx"),
        [
            (a * nx + b, (a - 1) % ny * nx + (b - 1) % nx)
            for a in range(ny)
            for b in range(nx)
        ],
    )
    cot = cotangent.reshape(WIN, 2, WIN, D)
    db, da, tis, live = branch(cot, tissue[0], w_proj)
    along_x, along_y = ("dp", (1, 3)), ("gy", (2, 6))
    keep0, send0, att0, dqkv0, xw, hid, hid_t = first_heads(
        mine, below, right, diag, tis, live, w_qkv, da
    )
    came = send(send0, "gy", lambda i: i ^ 1)
    keep1, send1, att1, dqkv1 = last_heads(hid, hid_t, tis, live, w_qkv, da, att0, db)
    came, send1 = tie(came, send1)
    first = add(keep0, came)
    low_a, high_a = blocks(first[:, :D]), blocks(first[:, D:])
    came_a = ring_start(low_a, high_a, *along_x)
    second = add(keep1, send(send1, "gy", lambda i: i ^ 1))
    second, att1 = tie(second, att1)
    low_b, high_b = blocks(second[:, :D]), blocks(second[:, D:])
    came_b = ring_start(low_b, high_b, *along_y)
    out = out_part(xw, tis, att0, att1, w_proj)
    came_b, out, xw, low_a, high_a = tie(came_b, out, xw, low_a, high_a)
    came_b = ring_pass(low_b, high_b, came_b, *along_y)
    came_a = ring_pass(low_a, high_a, came_a, *along_x)
    grad = grad_part(xw, cot, tis, dqkv0, dqkv1, w_qkv)
    came_a, came_b, grad = tie(came_a, came_b, grad)
    rows_a = ring_end(low_a, high_a, came_a)
    rows_b = ring_end(low_b, high_b, came_b)
    came_a = halve_start(rows_a, "gy", 2)
    came_b = halve_start(rows_b, "dp", 1)
    came_a, came_b = tie(came_a, came_b)
    rows_a = halve_end(rows_a, came_a)
    rows_b = halve_end(rows_b, came_b)
    came_a = halve_start(rows_a, "gy", 6)
    came_b = halve_start(rows_b, "dp", 3)
    rows = jnp.concatenate([halve_end(rows_a, came_a), halve_end(rows_b, came_b)], 1)
    grad_qkv, grad_proj = finish(exchange(rows, ("gx",)))
    return out, grad, grad_qkv, grad_proj


def solution(mesh):
    block = P("dp", "gy", "gx", None)
    in_specs = (block, block, P("dp", "gy", "gx"), P(), P())
    out_specs = (block, block, P(("dp", "gy", "gx"), None), P(("dp", "gy", "gx"), None))
    return jax.shard_map(
        shards, mesh=mesh, in_specs=in_specs, out_specs=out_specs, check_vma=False
    )
```

```python
import math

import jax
import jax.numpy as jnp
from jax import lax
from jax.experimental import pallas as pl
from jax.experimental.pallas import tpu as pltpu
from jax.sharding import PartitionSpec as P

F32 = jnp.float32
BF = jnp.bfloat16
D = 768
WIN = 16
CELLS = WIN * WIN
GROUPS = 3
GW = D // GROUPS
HEAD_SCALE = 0.125
VMEM = 32 * 1024 * 1024
EDGE_VMEM = 60 * 1024 * 1024


def nn(a, b):
    return lax.dot_general(a, b, (((1,), (0,)), ((), ())), preferred_element_type=F32)


def nt(a, b):
    return lax.dot_general(a, b, (((1,), (1,)), ((), ())), preferred_element_type=F32)


def tn(a, b):
    return lax.dot_general(a, b, (((0,), (0,)), ((), ())), preferred_element_type=F32)


def full(shape):
    return pl.BlockSpec(shape, lambda *g: (0,) * len(shape))


def cost(flops, size):
    return pl.CostEstimate(flops=int(flops), bytes_accessed=int(size), transcendentals=0)


def above_kernel(tiles_ref, above_ref):
    above_ref[...] = tiles_ref[...].astype(F32)[:, 8:].astype(BF)


def left_kernel(tiles_ref, after_ref, left_ref, corner_ref):
    tiles = tiles_ref[...].astype(F32)[:, :8].astype(BF)
    corner_ref[...] = tiles[:8]
    left_ref[...] = tiles[8:]


def edges(tiles):
    small = jax.ShapeDtypeStruct((8, 8, D), BF)
    above = pl.pallas_call(
        above_kernel,
        grid=(1,),
        in_specs=[pl.BlockSpec((8, 32, D), lambda g: (0, 0, 0))],
        out_specs=full((8, 24, D)),
        out_shape=jax.ShapeDtypeStruct((8, 24, D), BF),
        compiler_params=pltpu.CompilerParams(vmem_limit_bytes=EDGE_VMEM),
        cost_estimate=cost(3e10, 1e6),
        name="above",
    )(tiles)
    left, corner = pl.pallas_call(
        left_kernel,
        grid=(1,),
        in_specs=[
            pl.BlockSpec((16, 16, D), lambda g: (0, 0, 0)),
            pl.BlockSpec(memory_space=pl.ANY),
        ],
        out_specs=[full((8, 8, D))] * 2,
        out_shape=[small, small],
        compiler_params=pltpu.CompilerParams(vmem_limit_bytes=EDGE_VMEM),
        cost_estimate=cost(1e3, 1e3),
        name="left",
    )(tiles, above)
    return above, left, corner


def branch_kernel(
    cot_hbm, tissue_hbm, wp_hbm, db_ref, da_ref, tis_ref, live_ref, cot_ref, tissue_ref, wp_ref, sem
):
    copies = [
        pltpu.make_async_copy(tissue_hbm, tissue_ref, sem.at[0]),
        pltpu.make_async_copy(cot_hbm, cot_ref, sem.at[1]),
        pltpu.make_async_copy(wp_hbm, wp_ref, sem.at[2]),
    ]
    for copy in copies:
        copy.start()
    copies[0].wait()
    grid = tissue_ref[...].astype(F32).astype(BF)
    cell = lax.broadcasted_iota(jnp.int32, (CELLS, 1), 0)
    row_of = lax.broadcasted_iota(jnp.int32, (CELLS, WIN), 1) == (cell >> 4)
    rows = nn(row_of.astype(F32).astype(BF), grid)
    lane = lax.broadcasted_iota(jnp.int32, (CELLS, 2 * WIN), 1)
    ones = jnp.ones((2 * WIN, 128), BF)
    copies[1].wait()
    copies[2].wait()
    for w in range(2):
        own = jnp.where(lane == (cell & 15) + w * WIN, rows, 0.0).astype(BF)
        tis = nn(own, ones)
        some = jnp.max(jnp.max(tis, 0, keepdims=True), 1, keepdims=True)
        tis_ref[w] = tis.astype(BF)
        live_ref[w] = jnp.maximum(tis, 1.0 - some).astype(BF)
        db = cot_ref[:, w].reshape(CELLS, D) * jnp.tile(tis.astype(BF), (1, D // 128))
        db_ref[w] = db
        da_ref[w] = nt(db, wp_ref[...]).astype(BF)


def branch(cot, tissue, w_proj):
    shape = jax.ShapeDtypeStruct((2, CELLS, D), BF)
    mask = jax.ShapeDtypeStruct((2, CELLS, 128), BF)
    return pl.pallas_call(
        branch_kernel,
        in_specs=[pl.BlockSpec(memory_space=pltpu.HBM)] * 3,
        out_shape=[shape, shape, mask, mask],
        scratch_shapes=[
            pltpu.VMEM((WIN, 2, WIN, D), BF),
            pltpu.VMEM((WIN, 2 * WIN), jnp.int32),
            pltpu.VMEM((D, D), BF),
            pltpu.SemaphoreType.DMA((3,)),
        ],
        compiler_params=pltpu.CompilerParams(vmem_limit_bytes=VMEM),
        cost_estimate=cost(2e10, 4e6),
        name="branch",
    )(cot, tissue, w_proj)


def row_order():
    gy = lax.axis_index("gy")
    dp, y, core = lax.axis_index("dp"), gy >> 1, gy & 1
    at = lax.broadcasted_iota(jnp.int32, (D, 1), 0)
    third = ((at.astype(F32) + 0.5) * (1.0 / 3)).astype(jnp.int32)
    dp_of = ((third >> 6) & 1) ^ (((third >> 5) & 1) * 3) ^ dp
    y_of = ((third >> 4) & 1) ^ (((third >> 3) & 1) * 3) ^ y
    core_of = (third >> 7) ^ core
    source = ((dp_of * 8 + y_of * 2 + core_of) * 8 + (third & 7)) * 3 + at - third * 3
    column = lax.broadcasted_iota(jnp.int32, (D, D), 1)
    return jnp.where(column == source, 1.0, 0.0).astype(BF)


def moments(x):
    mean = jnp.mean(x, -1, keepdims=True)
    centred = x - mean
    inv = lax.rsqrt(jnp.mean(centred * centred, -1, keepdims=True) + 1e-05)
    return centred * inv, inv


def put(grad, keep_ref, send_ref, y_first):
    if y_first:
        size = D // 32
        places = [(c * 4 + x) * 4 + y for c in range(2) for y in range(4) for x in range(4)]
        grad = jnp.concatenate([grad[at * size : (at + 1) * size] for at in places], 0)
    keep_ref[...] = grad[: D // 2].astype(BF)
    send_ref[...] = grad[D // 2 :].astype(BF)


def heads_group(
    hid_ref, hid_t_ref, tis_ref, live_ref, wq_ref, wk_ref, wv_ref, da_ref,
    keep_ref, send_ref, att_ref, dqkv_ref, y_first,
):
    hidden = hid_ref[...].reshape(2 * CELLS, D)
    query = nn(hidden, wq_ref[...]).astype(BF) * BF(HEAD_SCALE)
    key = nn(hidden, wk_ref[...]).astype(BF)
    value = nn(hidden, wv_ref[...]).astype(BF)
    lane = lax.broadcasted_iota(jnp.int32, (1, 128), 1)
    sel = [(lane < 64).astype(BF), (lane >= 64).astype(BF)]
    units = [(w, p) for w in range(2) for p in range(2)]
    q, k, v, da, weight, ds, rinv, att = {}, {}, {}, {}, {}, {}, {}, {}
    for u in units:
        w, p = u
        rows, lanes = slice(w * CELLS, (w + 1) * CELLS), slice(p * 128, (p + 1) * 128)
        q[u] = query[rows, lanes]
        k[u] = key[rows, lanes] * tis_ref[w]
        v[u] = value[rows, lanes] * tis_ref[w]
        da[u] = da_ref[w, :, lanes]
    for u in units:
        for h in range(2):
            weight[u, h] = jnp.exp(nt(q[u], k[u] * sel[h])).astype(BF)
    for u in units:
        live = live_ref[u[0]]
        both = nn(weight[u, 0], jnp.concatenate([v[u] * sel[0], live * sel[0]], 1)) + nn(
            weight[u, 1], jnp.concatenate([v[u] * sel[1], live * sel[1]], 1)
        )
        rinv[u] = 1.0 / both[:, 128:]
        att[u] = both[:, :128] * rinv[u]
        att_ref[u[0], :, u[1] * 128 : (u[1] + 1) * 128] = att[u].astype(BF)
    for u in units:
        terms = da[u].astype(F32) * att[u]
        for h in range(2):
            delta = jnp.sum(terms * sel[h].astype(F32), 1, keepdims=True)
            dprobs = nt(da[u], v[u] * sel[h]) - delta
            ds[u, h] = (weight[u, h].astype(F32) * dprobs).astype(BF)
    for u in units:
        w, p = u
        dq = (nn(ds[u, 0], k[u] * sel[0]) + nn(ds[u, 1], k[u] * sel[1])) * (rinv[u] * HEAD_SCALE)
        dan = (da[u].astype(F32) * rinv[u]).astype(BF)
        qn = (q[u].astype(F32) * rinv[u]).astype(BF)
        dv = tn(weight[u, 0], dan * sel[0]) + tn(weight[u, 1], dan * sel[1])
        dk = tn(ds[u, 0], qn * sel[0]) + tn(ds[u, 1], qn * sel[1])
        for i, grad in enumerate((dq, dk, dv)):
            at = i * GW + p * 128
            dqkv_ref[0, w, :, at : at + 128] = grad.astype(BF)
    grad = nn(hid_t_ref[...], dqkv_ref[0].reshape(2 * CELLS, D))
    put(grad, keep_ref, send_ref, y_first)


def first_kernel(
    tiles_ref, below_ref, right_ref, diag_ref, tis_ref, live_ref,
    wq_ref, wk_ref, wv_ref, da_ref,
    keep_ref, send_ref, att_ref, dqkv_ref, xw_ref, hid_ref, hid_t_ref,
):
    @pl.when(pl.program_id(0) == 0)
    def _():
        own = tiles_ref[8:16].astype(F32)
        low = below_ref[...].astype(F32)
        right = right_ref[...].astype(F32)
        diag = diag_ref[...].astype(F32)
        perm = row_order()
        for w in range(2):
            if w == 0:
                top, bottom = own[:, 8:24], low[:, :16]
            else:
                top = jnp.concatenate([own[:, 24:32], right], 1)
                bottom = jnp.concatenate([low[:, 16:24], diag], 1)
            x = jnp.concatenate([top, bottom], 0).reshape(CELLS, D)
            xw_ref[w] = x.astype(BF)
            normed, _ = moments(x)
            hidden = normed.astype(BF)
            hid_ref[w] = hidden
            masked = hidden * jnp.tile(tis_ref[w], (1, D // 128))
            hid_t_ref[:, w * CELLS : (w + 1) * CELLS] = nt(perm, masked).astype(BF)

    heads_group(
        hid_ref, hid_t_ref, tis_ref, live_ref, wq_ref, wk_ref, wv_ref, da_ref,
        keep_ref, send_ref, att_ref, dqkv_ref, False,
    )


def last_kernel(
    hid_ref, hid_t_ref, tis_ref, live_ref, wq_ref, wk_ref, wv_ref, da_ref, att0_ref, db_ref,
    keep_ref, send_ref, att_ref, dqkv_ref,
):
    heads_group(
        hid_ref, hid_t_ref, tis_ref, live_ref, wq_ref, wk_ref, wv_ref, da_ref,
        keep_ref.at[:, :D], send_ref.at[:, :D], att_ref, dqkv_ref, True,
    )
    attended = jnp.concatenate([att0_ref[...], att_ref[...]], 2).reshape(2 * CELLS, D)
    att_t = nt(row_order(), attended).astype(BF)
    grad = nn(att_t, db_ref[...].reshape(2 * CELLS, D))
    put(grad, keep_ref.at[:, D:], send_ref.at[:, D:], True)


def columns(block, first):
    return pl.BlockSpec((D, GW), lambda g: (0, block * GROUPS + first + g))


def heads_specs(first, groups):
    inputs = [
        full((2, CELLS, 128)), full((2, CELLS, 128)),
        columns(0, first), columns(1, first), columns(2, first),
        pl.BlockSpec((2, CELLS, GW), lambda g: (0, 0, first + g)),
    ]
    half = pl.BlockSpec((D // 2, D), lambda g: (0, g))
    outputs = [
        half, half,
        pl.BlockSpec((2, CELLS, GW), lambda g: (0, 0, g)),
        pl.BlockSpec((1, 2, CELLS, D), lambda g: (g, 0, 0, 0)),
    ]
    shapes = [
        jax.ShapeDtypeStruct((D // 2, groups * D), BF),
        jax.ShapeDtypeStruct((D // 2, groups * D), BF),
        jax.ShapeDtypeStruct((2, CELLS, groups * GW), BF),
        jax.ShapeDtypeStruct((groups, 2, CELLS, D), BF),
    ]
    return inputs, outputs, shapes


def first_heads(tiles, below, right, diag, tis, live, w_qkv, da):
    inputs, outputs, shapes = heads_specs(0, 2)
    rows = jax.ShapeDtypeStruct((2, CELLS, D), BF)
    return pl.pallas_call(
        first_kernel,
        grid=(2,),
        in_specs=[full((16, 32, D)), full((8, 24, D)), full((8, 8, D)), full((8, 8, D))] + inputs,
        out_specs=outputs + [full((2, CELLS, D))] * 2 + [full((D, 2 * CELLS))],
        out_shape=shapes + [rows, rows, jax.ShapeDtypeStruct((D, 2 * CELLS), BF)],
        compiler_params=pltpu.CompilerParams(vmem_limit_bytes=VMEM),
        cost_estimate=cost(6e9, 10e6),
        name="first_heads",
    )(tiles, below, right, diag, tis, live, w_qkv, w_qkv, w_qkv, da)


def last_heads(hid, hid_t, tis, live, w_qkv, da, att0, db):
    inputs, outputs, shapes = heads_specs(2, 1)
    half = jax.ShapeDtypeStruct((D // 2, 2 * D), BF)
    rows = full((2, CELLS, D))
    return pl.pallas_call(
        last_kernel,
        grid=(1,),
        in_specs=[rows, full((D, 2 * CELLS))] + inputs + [full((2, CELLS, 2 * GW)), rows],
        out_specs=[full((D // 2, 2 * D))] * 2 + outputs[2:],
        out_shape=[half, half] + shapes[2:],
        compiler_params=pltpu.CompilerParams(vmem_limit_bytes=VMEM),
        cost_estimate=cost(4e9, 6e6),
        name="last_heads",
    )(hid, hid_t, tis, live, w_qkv, w_qkv, w_qkv, da, att0, db)


def out_kernel(xw_ref, tis_ref, att0_ref, att1_ref, wp_ref, out_ref):
    for w in range(2):
        tis = jnp.tile(tis_ref[w].astype(F32), (1, D // 128))
        attended = jnp.concatenate([att0_ref[w], att1_ref[w]], 1)
        out = xw_ref[w].astype(F32) + tis * nn(attended, wp_ref[...])
        out_ref[:, w] = out.astype(BF).reshape(WIN, WIN, D)


def out_part(xw, tis, att0, att1, w_proj):
    out = pl.pallas_call(
        out_kernel,
        out_shape=jax.ShapeDtypeStruct((WIN, 2, WIN, D), BF),
        compiler_params=pltpu.CompilerParams(vmem_limit_bytes=VMEM),
        cost_estimate=cost(1e3, 1e3),
        name="out_part",
    )(xw, tis, att0, att1, w_proj)
    return out.reshape(1, WIN, 2 * WIN, D)


def grad_kernel(
    xw_ref, cot_ref, tis_ref, dqkv0_ref, dqkv1_ref, wq_ref, wk_ref, wv_ref, grad_ref, acc_ref
):
    step = pl.program_id(0)
    weights = jnp.concatenate([wq_ref[...], wk_ref[...], wv_ref[...]], 1)
    dqkv = jnp.where(step < GROUPS - 1, dqkv0_ref[0], dqkv1_ref[0])
    part = nt(dqkv.reshape(2 * CELLS, D), weights)

    @pl.when(step == 0)
    def _():
        acc_ref[...] = part

    @pl.when((step > 0) & (step < GROUPS - 1))
    def _():
        acc_ref[...] += part

    @pl.when(step == GROUPS - 1)
    def _():
        acc_ref[...] += part
        for w in range(2):
            normed, inv = moments(xw_ref[w].astype(F32))
            tis = jnp.tile(tis_ref[w].astype(F32), (1, D // 128))
            dh = acc_ref[w * CELLS : (w + 1) * CELLS] * tis
            dnorm = inv * (
                dh
                - jnp.mean(dh, -1, keepdims=True)
                - normed * jnp.mean(dh * normed, -1, keepdims=True)
            )
            grad = cot_ref[:, w].reshape(CELLS, D).astype(F32) + dnorm
            grad_ref[:, w] = grad.astype(BF).reshape(WIN, WIN, D)


def grad_part(xw, cot, tis, dqkv0, dqkv1, w_qkv):
    grad = pl.pallas_call(
        grad_kernel,
        grid=(GROUPS,),
        in_specs=[
            full((2, CELLS, D)), full((WIN, 2, WIN, D)), full((2, CELLS, 128)),
            pl.BlockSpec((1, 2, CELLS, D), lambda g: (jnp.minimum(g, 1), 0, 0, 0)),
            full((1, 2, CELLS, D)),
            columns(0, 0), columns(1, 0), columns(2, 0),
        ],
        out_specs=full((WIN, 2, WIN, D)),
        out_shape=jax.ShapeDtypeStruct((WIN, 2, WIN, D), BF),
        scratch_shapes=[pltpu.VMEM((2 * CELLS, D), F32)],
        compiler_params=pltpu.CompilerParams(vmem_limit_bytes=VMEM),
        cost_estimate=cost(1e3, 1e3),
        name="grad_part",
    )(xw, cot, tis, dqkv0, dqkv1, w_qkv, w_qkv, w_qkv)
    return grad.reshape(1, WIN, 2 * WIN, D)


def finish_kernel(parts_ref, qkv_ref, proj_ref):
    total = parts_ref[0].astype(F32)
    for part in range(1, parts_ref.shape[0]):
        total = total + parts_ref[part].astype(F32)
    total = total * (1.0 / math.sqrt(512))
    for i in range(3):
        for g in range(GROUPS):
            at = g * D + i * GW
            qkv_ref[:, i * D + g * GW : i * D + (g + 1) * GW] = total[:, at : at + GW]
    proj_ref[...] = total[:, 3 * D :]


def finish(parts):
    rows = parts.shape[1]
    return pl.pallas_call(
        finish_kernel,
        out_shape=[
            jax.ShapeDtypeStruct((rows, 3 * D), F32),
            jax.ShapeDtypeStruct((rows, D), F32),
        ],
        compiler_params=pltpu.CompilerParams(vmem_limit_bytes=VMEM),
        name="finish",
    )(parts)


def send(value, axis, move):
    devices = lax.axis_size(axis)
    return lax.ppermute(value, axis, [(i, move(i) % devices) for i in range(devices)])


def add(*terms):
    total = terms[0].astype(F32)
    for term in terms[1:]:
        total = total + term.astype(F32)
    return total.astype(BF)


def ring_start(low, high, axis, flips):
    one, three = flips
    return send(low[3], axis, lambda j: j ^ one), send(high[3], axis, lambda j: j ^ three)


def ring_pass(low, high, came, axis, flips):
    one, three = flips
    to_one = jnp.concatenate([low[2], add(high[2], came[1])], 1)
    to_three = jnp.concatenate([add(low[1], came[0]), high[1]], 1)
    return send(to_one, axis, lambda j: j ^ one), send(to_three, axis, lambda j: j ^ three)


def ring_end(low, high, came):
    n = low.shape[2]
    up, down = came
    low = add(low[0], up[:, :n], down[:, :n])
    high = add(high[0], up[:, n:], down[:, n:])
    return jnp.concatenate([low, high], 1)


def direct_start(rows, axis, flips):
    one, three = flips
    part = blocks(rows)
    return [
        send(part[at], axis, lambda j, flip=flip: j ^ flip)
        for at, flip in ((3, one ^ three), (1, three), (2, one))
    ]


def direct_end(rows, came):
    return add(blocks(rows)[0], *came)


def exchange(rows, axis, groups=None):
    parts = len(groups[0]) if groups else math.prod(lax.axis_size(a) for a in axis)
    rows = rows.reshape(parts, rows.shape[0] // parts, rows.shape[1])
    return lax.all_to_all(rows, axis, 0, 0, axis_index_groups=groups)


def tie(*values):
    return lax.optimization_barrier(values)


def blocks(value):
    return value.reshape(4, value.shape[0] // 4, value.shape[1])


def shards(tiles, cotangent, tissue, w_qkv, w_proj):
    mine = tiles[0]
    above, left, corner = edges(mine)
    below = send(above, "gy", lambda i: i - 1)
    right = send(left, "gx", lambda i: i - 1)
    ny, nx = lax.axis_size("gy"), lax.axis_size("gx")
    diag = lax.ppermute(
        corner,
        ("gy", "gx"),
        [
            (a * nx + b, (a - 1) % ny * nx + (b - 1) % nx)
            for a in range(ny)
            for b in range(nx)
        ],
    )
    cot = cotangent.reshape(WIN, 2, WIN, D)
    db, da, tis, live = branch(cot, tissue[0], w_proj)
    along_x, along_y = ("dp", (1, 3)), ("gy", (2, 6))
    keep0, send0, att0, dqkv0, xw, hid, hid_t = first_heads(
        mine, below, right, diag, tis, live, w_qkv, da
    )
    came = send(send0, "gy", lambda i: i ^ 1)
    keep1, send1, att1, dqkv1 = last_heads(hid, hid_t, tis, live, w_qkv, da, att0, db)
    came, send1 = tie(came, send1)
    first = add(keep0, came)
    low_a, high_a = blocks(first[:, :D]), blocks(first[:, D:])
    came_a = ring_start(low_a, high_a, *along_x)
    second = add(keep1, send(send1, "gy", lambda i: i ^ 1))
    second, att1 = tie(second, att1)
    low_b, high_b = blocks(second[:, :D]), blocks(second[:, D:])
    came_b = ring_start(low_b, high_b, *along_y)
    out = out_part(xw, tis, att0, att1, w_proj)
    came_b, out, xw, low_a, high_a = tie(came_b, out, xw, low_a, high_a)
    came_b = ring_pass(low_b, high_b, came_b, *along_y)
    came_a = ring_pass(low_a, high_a, came_a, *along_x)
    grad = grad_part(xw, cot, tis, dqkv0, dqkv1, w_qkv)
    came_a, came_b, grad = tie(came_a, came_b, grad)
    rows_a = ring_end(low_a, high_a, came_a)
    rows_b = ring_end(low_b, high_b, came_b)
    came_a = direct_start(rows_a, *along_y)
    came_b = direct_start(rows_b, *along_x)
    rows = jnp.concatenate([direct_end(rows_a, came_a), direct_end(rows_b, came_b)], 1)
    grad_qkv, grad_proj = finish(exchange(rows, ("gx",)))
    return out, grad, grad_qkv, grad_proj


def solution(mesh):
    block = P("dp", "gy", "gx", None)
    in_specs = (block, block, P("dp", "gy", "gx"), P(), P())
    out_specs = (block, block, P(("dp", "gy", "gx"), None), P(("dp", "gy", "gx"), None))
    return jax.shard_map(
        shards, mesh=mesh, in_specs=in_specs, out_specs=out_specs, check_vma=False
    )
```

```python
import math

import jax
import jax.numpy as jnp
from jax import lax
from jax.experimental import pallas as pl
from jax.experimental.pallas import tpu as pltpu
from jax.sharding import PartitionSpec as P

F32 = jnp.float32
BF = jnp.bfloat16
D = 768
WIN = 16
CELLS = WIN * WIN
GROUPS = 3
GW = D // GROUPS
HEAD_SCALE = 0.125
VMEM = 32 * 1024 * 1024


def nn(a, b):
    return lax.dot_general(a, b, (((1,), (0,)), ((), ())), preferred_element_type=F32)


def nt(a, b):
    return lax.dot_general(a, b, (((1,), (1,)), ((), ())), preferred_element_type=F32)


def tn(a, b):
    return lax.dot_general(a, b, (((0,), (0,)), ((), ())), preferred_element_type=F32)


def full(shape):
    return pl.BlockSpec(shape, lambda *g: (0,) * len(shape))


def cost(flops, size):
    return pl.CostEstimate(flops=int(flops), bytes_accessed=int(size), transcendentals=0)


def corner_kernel(tiles_ref, corner_ref):
    corner_ref[...] = tiles_ref[...].astype(F32)[:, :8].astype(BF)


def above_kernel(tiles_ref, after_ref, above_ref):
    above_ref[...] = tiles_ref[...].astype(F32)[:, 8:].astype(BF)


def left_kernel(tiles_ref, after_ref, left_ref):
    left_ref[...] = tiles_ref[...].astype(F32)[:, :8].astype(BF)


def cut(kernel, name, flops, tiles, after, block, first, columns):
    place = pl.BlockSpec(memory_space=pl.ANY)
    return pl.pallas_call(
        kernel,
        grid=(1,),
        in_specs=[pl.BlockSpec(block + (D,), lambda g: (first, 0, 0))] + [place] * len(after),
        out_specs=full((8, columns, D)),
        out_shape=jax.ShapeDtypeStruct((8, columns, D), BF),
        compiler_params=pltpu.CompilerParams(vmem_limit_bytes=VMEM),
        cost_estimate=cost(flops, 1e3),
        name=name,
    )(tiles, *after)


def edges(tiles):
    corner = cut(corner_kernel, "corner", 3e10, tiles, [], (8, 16), 0, 8)
    above = cut(above_kernel, "above", 1e3, tiles, [corner], (8, 32), 0, 24)
    left = cut(left_kernel, "left", 1e3, tiles, [above], (8, 16), 1, 8)
    return above, left, corner


def branch_kernel(
    cot_hbm, tissue_hbm, wp_hbm, db_ref, da_ref, tis_ref, live_ref, cot_ref, tissue_ref, wp_ref, sem
):
    copies = [
        pltpu.make_async_copy(tissue_hbm, tissue_ref, sem.at[0]),
        pltpu.make_async_copy(cot_hbm, cot_ref, sem.at[1]),
        pltpu.make_async_copy(wp_hbm, wp_ref, sem.at[2]),
    ]
    for copy in copies:
        copy.start()
    copies[0].wait()
    grid = tissue_ref[...].astype(F32).astype(BF)
    cell = lax.broadcasted_iota(jnp.int32, (CELLS, 1), 0)
    row_of = lax.broadcasted_iota(jnp.int32, (CELLS, WIN), 1) == (cell >> 4)
    rows = nn(row_of.astype(F32).astype(BF), grid)
    lane = lax.broadcasted_iota(jnp.int32, (CELLS, 2 * WIN), 1)
    ones = jnp.ones((2 * WIN, 128), BF)
    copies[1].wait()
    copies[2].wait()
    for w in range(2):
        own = jnp.where(lane == (cell & 15) + w * WIN, rows, 0.0).astype(BF)
        tis = nn(own, ones)
        some = jnp.max(jnp.max(tis, 0, keepdims=True), 1, keepdims=True)
        tis_ref[w] = tis.astype(BF)
        live_ref[w] = jnp.maximum(tis, 1.0 - some).astype(BF)
        db = cot_ref[:, w].reshape(CELLS, D) * jnp.tile(tis.astype(BF), (1, D // 128))
        db_ref[w] = db
        da_ref[w] = nt(db, wp_ref[...]).astype(BF)


def branch(cot, tissue, w_proj):
    shape = jax.ShapeDtypeStruct((2, CELLS, D), BF)
    mask = jax.ShapeDtypeStruct((2, CELLS, 128), BF)
    return pl.pallas_call(
        branch_kernel,
        in_specs=[pl.BlockSpec(memory_space=pltpu.HBM)] * 3,
        out_shape=[shape, shape, mask, mask],
        scratch_shapes=[
            pltpu.VMEM((WIN, 2, WIN, D), BF),
            pltpu.VMEM((WIN, 2 * WIN), jnp.int32),
            pltpu.VMEM((D, D), BF),
            pltpu.SemaphoreType.DMA((3,)),
        ],
        compiler_params=pltpu.CompilerParams(vmem_limit_bytes=VMEM),
        cost_estimate=cost(2e10, 4e6),
        name="branch",
    )(cot, tissue, w_proj)


def row_order():
    gy = lax.axis_index("gy")
    dp, y, core = lax.axis_index("dp"), gy >> 1, gy & 1
    at = lax.broadcasted_iota(jnp.int32, (D, 1), 0)
    third = ((at.astype(F32) + 0.5) * (1.0 / 3)).astype(jnp.int32)
    dp_of = ((third >> 6) & 1) ^ (((third >> 5) & 1) * 3) ^ dp
    y_of = ((third >> 4) & 1) ^ (((third >> 3) & 1) * 3) ^ y
    core_of = (third >> 7) ^ core
    source = ((dp_of * 8 + y_of * 2 + core_of) * 8 + (third & 7)) * 3 + at - third * 3
    column = lax.broadcasted_iota(jnp.int32, (D, D), 1)
    return jnp.where(column == source, 1.0, 0.0).astype(BF)


def moments(x):
    mean = jnp.mean(x, -1, keepdims=True)
    centred = x - mean
    inv = lax.rsqrt(jnp.mean(centred * centred, -1, keepdims=True) + 1e-05)
    return centred * inv, inv


def put(grad, keep_ref, send_ref, y_first):
    if y_first:
        size = D // 32
        places = [(c * 4 + x) * 4 + y for c in range(2) for y in range(4) for x in range(4)]
        grad = jnp.concatenate([grad[at * size : (at + 1) * size] for at in places], 0)
    keep_ref[...] = grad[: D // 2].astype(BF)
    send_ref[...] = grad[D // 2 :].astype(BF)


def heads_group(
    hid_ref, hid_t_ref, tis_ref, live_ref, wq_ref, wk_ref, wv_ref, da_ref,
    keep_ref, send_ref, att_ref, dqkv_ref, y_first,
):
    hidden = hid_ref[...].reshape(2 * CELLS, D)
    query = nn(hidden, wq_ref[...]).astype(BF) * BF(HEAD_SCALE)
    key = nn(hidden, wk_ref[...]).astype(BF)
    value = nn(hidden, wv_ref[...]).astype(BF)
    lane = lax.broadcasted_iota(jnp.int32, (1, 128), 1)
    sel = [(lane < 64).astype(BF), (lane >= 64).astype(BF)]
    units = [(w, p) for w in range(2) for p in range(2)]
    q, k, v, da, weight, ds, rinv, att = {}, {}, {}, {}, {}, {}, {}, {}
    for u in units:
        w, p = u
        rows, lanes = slice(w * CELLS, (w + 1) * CELLS), slice(p * 128, (p + 1) * 128)
        q[u] = query[rows, lanes]
        k[u] = key[rows, lanes] * tis_ref[w]
        v[u] = value[rows, lanes] * tis_ref[w]
        da[u] = da_ref[w, :, lanes]
    for u in units:
        for h in range(2):
            weight[u, h] = jnp.exp(nt(q[u], k[u] * sel[h])).astype(BF)
    for u in units:
        live = live_ref[u[0]]
        both = nn(weight[u, 0], jnp.concatenate([v[u] * sel[0], live * sel[0]], 1)) + nn(
            weight[u, 1], jnp.concatenate([v[u] * sel[1], live * sel[1]], 1)
        )
        rinv[u] = 1.0 / both[:, 128:]
        att[u] = both[:, :128] * rinv[u]
        att_ref[u[0], :, u[1] * 128 : (u[1] + 1) * 128] = att[u].astype(BF)
    for u in units:
        terms = da[u].astype(F32) * att[u]
        for h in range(2):
            delta = jnp.sum(terms * sel[h].astype(F32), 1, keepdims=True)
            dprobs = nt(da[u], v[u] * sel[h]) - delta
            ds[u, h] = (weight[u, h].astype(F32) * dprobs).astype(BF)
    for u in units:
        w, p = u
        dq = (nn(ds[u, 0], k[u] * sel[0]) + nn(ds[u, 1], k[u] * sel[1])) * (rinv[u] * HEAD_SCALE)
        dan = (da[u].astype(F32) * rinv[u]).astype(BF)
        qn = (q[u].astype(F32) * rinv[u]).astype(BF)
        dv = tn(weight[u, 0], dan * sel[0]) + tn(weight[u, 1], dan * sel[1])
        dk = tn(ds[u, 0], qn * sel[0]) + tn(ds[u, 1], qn * sel[1])
        for i, grad in enumerate((dq, dk, dv)):
            at = i * GW + p * 128
            dqkv_ref[0, w, :, at : at + 128] = grad.astype(BF)
    grad = nn(hid_t_ref[...], dqkv_ref[0].reshape(2 * CELLS, D))
    put(grad, keep_ref, send_ref, y_first)


def first_kernel(
    tiles_ref, below_ref, right_ref, diag_ref, tis_ref, live_ref,
    wq_ref, wk_ref, wv_ref, da_ref,
    keep_ref, send_ref, att_ref, dqkv_ref, xw_ref, hid_ref, hid_t_ref,
):
    @pl.when(pl.program_id(0) == 0)
    def _():
        own = tiles_ref[8:16].astype(F32)
        low = below_ref[...].astype(F32)
        right = right_ref[...].astype(F32)
        diag = diag_ref[...].astype(F32)
        perm = row_order()
        for w in range(2):
            if w == 0:
                top, bottom = own[:, 8:24], low[:, :16]
            else:
                top = jnp.concatenate([own[:, 24:32], right], 1)
                bottom = jnp.concatenate([low[:, 16:24], diag], 1)
            x = jnp.concatenate([top, bottom], 0).reshape(CELLS, D)
            xw_ref[w] = x.astype(BF)
            normed, _ = moments(x)
            hidden = normed.astype(BF)
            hid_ref[w] = hidden
            masked = hidden * jnp.tile(tis_ref[w], (1, D // 128))
            hid_t_ref[:, w * CELLS : (w + 1) * CELLS] = nt(perm, masked).astype(BF)

    heads_group(
        hid_ref, hid_t_ref, tis_ref, live_ref, wq_ref, wk_ref, wv_ref, da_ref,
        keep_ref, send_ref, att_ref, dqkv_ref, False,
    )


def last_kernel(
    hid_ref, hid_t_ref, tis_ref, live_ref, wq_ref, wk_ref, wv_ref, da_ref, att0_ref, db_ref,
    keep_ref, send_ref, att_ref, dqkv_ref,
):
    heads_group(
        hid_ref, hid_t_ref, tis_ref, live_ref, wq_ref, wk_ref, wv_ref, da_ref,
        keep_ref.at[:, :D], send_ref.at[:, :D], att_ref, dqkv_ref, True,
    )
    attended = jnp.concatenate([att0_ref[...], att_ref[...]], 2).reshape(2 * CELLS, D)
    att_t = nt(row_order(), attended).astype(BF)
    grad = nn(att_t, db_ref[...].reshape(2 * CELLS, D))
    put(grad, keep_ref.at[:, D:], send_ref.at[:, D:], True)


def columns(block, first):
    return pl.BlockSpec((D, GW), lambda g: (0, block * GROUPS + first + g))


def heads_specs(first, groups):
    inputs = [
        full((2, CELLS, 128)), full((2, CELLS, 128)),
        columns(0, first), columns(1, first), columns(2, first),
        pl.BlockSpec((2, CELLS, GW), lambda g: (0, 0, first + g)),
    ]
    half = pl.BlockSpec((D // 2, D), lambda g: (0, g))
    outputs = [
        half, half,
        pl.BlockSpec((2, CELLS, GW), lambda g: (0, 0, g)),
        pl.BlockSpec((1, 2, CELLS, D), lambda g: (g, 0, 0, 0)),
    ]
    shapes = [
        jax.ShapeDtypeStruct((D // 2, groups * D), BF),
        jax.ShapeDtypeStruct((D // 2, groups * D), BF),
        jax.ShapeDtypeStruct((2, CELLS, groups * GW), BF),
        jax.ShapeDtypeStruct((groups, 2, CELLS, D), BF),
    ]
    return inputs, outputs, shapes


def first_heads(tiles, below, right, diag, tis, live, w_qkv, da):
    inputs, outputs, shapes = heads_specs(0, 2)
    rows = jax.ShapeDtypeStruct((2, CELLS, D), BF)
    return pl.pallas_call(
        first_kernel,
        grid=(2,),
        in_specs=[full((16, 32, D)), full((8, 24, D)), full((8, 8, D)), full((8, 8, D))] + inputs,
        out_specs=outputs + [full((2, CELLS, D))] * 2 + [full((D, 2 * CELLS))],
        out_shape=shapes + [rows, rows, jax.ShapeDtypeStruct((D, 2 * CELLS), BF)],
        compiler_params=pltpu.CompilerParams(vmem_limit_bytes=VMEM),
        cost_estimate=cost(6e9, 10e6),
        name="first_heads",
    )(tiles, below, right, diag, tis, live, w_qkv, w_qkv, w_qkv, da)


def last_heads(hid, hid_t, tis, live, w_qkv, da, att0, db):
    inputs, outputs, shapes = heads_specs(2, 1)
    half = jax.ShapeDtypeStruct((D // 2, 2 * D), BF)
    rows = full((2, CELLS, D))
    return pl.pallas_call(
        last_kernel,
        grid=(1,),
        in_specs=[rows, full((D, 2 * CELLS))] + inputs + [full((2, CELLS, 2 * GW)), rows],
        out_specs=[full((D // 2, 2 * D))] * 2 + outputs[2:],
        out_shape=[half, half] + shapes[2:],
        compiler_params=pltpu.CompilerParams(vmem_limit_bytes=VMEM),
        cost_estimate=cost(4e9, 6e6),
        name="last_heads",
    )(hid, hid_t, tis, live, w_qkv, w_qkv, w_qkv, da, att0, db)


def out_kernel(xw_ref, tis_ref, att0_ref, att1_ref, wp_ref, out_ref):
    for w in range(2):
        tis = jnp.tile(tis_ref[w].astype(F32), (1, D // 128))
        attended = jnp.concatenate([att0_ref[w], att1_ref[w]], 1)
        out = xw_ref[w].astype(F32) + tis * nn(attended, wp_ref[...])
        out_ref[:, w] = out.astype(BF).reshape(WIN, WIN, D)


def out_part(xw, tis, att0, att1, w_proj):
    out = pl.pallas_call(
        out_kernel,
        out_shape=jax.ShapeDtypeStruct((WIN, 2, WIN, D), BF),
        compiler_params=pltpu.CompilerParams(vmem_limit_bytes=VMEM),
        cost_estimate=cost(1e3, 1e3),
        name="out_part",
    )(xw, tis, att0, att1, w_proj)
    return out.reshape(1, WIN, 2 * WIN, D)


def grad_kernel(
    xw_ref, cot_ref, tis_ref, dqkv0_ref, dqkv1_ref, wq_ref, wk_ref, wv_ref, grad_ref, acc_ref
):
    step = pl.program_id(0)
    weights = jnp.concatenate([wq_ref[...], wk_ref[...], wv_ref[...]], 1)
    dqkv = jnp.where(step < GROUPS - 1, dqkv0_ref[0], dqkv1_ref[0])
    part = nt(dqkv.reshape(2 * CELLS, D), weights)

    @pl.when(step == 0)
    def _():
        acc_ref[...] = part

    @pl.when((step > 0) & (step < GROUPS - 1))
    def _():
        acc_ref[...] += part

    @pl.when(step == GROUPS - 1)
    def _():
        acc_ref[...] += part
        for w in range(2):
            normed, inv = moments(xw_ref[w].astype(F32))
            tis = jnp.tile(tis_ref[w].astype(F32), (1, D // 128))
            dh = acc_ref[w * CELLS : (w + 1) * CELLS] * tis
            dnorm = inv * (
                dh
                - jnp.mean(dh, -1, keepdims=True)
                - normed * jnp.mean(dh * normed, -1, keepdims=True)
            )
            grad = cot_ref[:, w].reshape(CELLS, D).astype(F32) + dnorm
            grad_ref[:, w] = grad.astype(BF).reshape(WIN, WIN, D)


def grad_part(xw, cot, tis, dqkv0, dqkv1, w_qkv):
    grad = pl.pallas_call(
        grad_kernel,
        grid=(GROUPS,),
        in_specs=[
            full((2, CELLS, D)), full((WIN, 2, WIN, D)), full((2, CELLS, 128)),
            pl.BlockSpec((1, 2, CELLS, D), lambda g: (jnp.minimum(g, 1), 0, 0, 0)),
            full((1, 2, CELLS, D)),
            columns(0, 0), columns(1, 0), columns(2, 0),
        ],
        out_specs=full((WIN, 2, WIN, D)),
        out_shape=jax.ShapeDtypeStruct((WIN, 2, WIN, D), BF),
        scratch_shapes=[pltpu.VMEM((2 * CELLS, D), F32)],
        compiler_params=pltpu.CompilerParams(vmem_limit_bytes=VMEM),
        cost_estimate=cost(1e3, 1e3),
        name="grad_part",
    )(xw, cot, tis, dqkv0, dqkv1, w_qkv, w_qkv, w_qkv)
    return grad.reshape(1, WIN, 2 * WIN, D)


def finish_kernel(parts_ref, qkv_ref, proj_ref):
    total = parts_ref[0].astype(F32)
    for part in range(1, parts_ref.shape[0]):
        total = total + parts_ref[part].astype(F32)
    total = total * (1.0 / math.sqrt(512))
    for i in range(3):
        for g in range(GROUPS):
            at = g * D + i * GW
            qkv_ref[:, i * D + g * GW : i * D + (g + 1) * GW] = total[:, at : at + GW]
    proj_ref[...] = total[:, 3 * D :]


def finish(parts):
    rows = parts.shape[1]
    return pl.pallas_call(
        finish_kernel,
        out_shape=[
            jax.ShapeDtypeStruct((rows, 3 * D), F32),
            jax.ShapeDtypeStruct((rows, D), F32),
        ],
        compiler_params=pltpu.CompilerParams(vmem_limit_bytes=VMEM),
        name="finish",
    )(parts)


def send(value, axis, move):
    devices = lax.axis_size(axis)
    return lax.ppermute(value, axis, [(i, move(i) % devices) for i in range(devices)])


def add(*terms):
    total = terms[0].astype(F32)
    for term in terms[1:]:
        total = total + term.astype(F32)
    return total.astype(BF)


def ring_start(low, high, axis, flips):
    one, three = flips
    return send(low[3], axis, lambda j: j ^ one), send(high[3], axis, lambda j: j ^ three)


def ring_pass(low, high, came, axis, flips):
    one, three = flips
    to_one = jnp.concatenate([low[2], add(high[2], came[1])], 1)
    to_three = jnp.concatenate([add(low[1], came[0]), high[1]], 1)
    return send(to_one, axis, lambda j: j ^ one), send(to_three, axis, lambda j: j ^ three)


def ring_end(low, high, came):
    n = low.shape[2]
    up, down = came
    low = add(low[0], up[:, :n], down[:, :n])
    high = add(high[0], up[:, n:], down[:, n:])
    return jnp.concatenate([low, high], 1)


def direct_start(rows, axis, flips):
    one, three = flips
    part = blocks(rows)
    return [
        send(part[at], axis, lambda j, flip=flip: j ^ flip)
        for at, flip in ((3, one ^ three), (1, three), (2, one))
    ]


def direct_end(rows, came):
    return add(blocks(rows)[0], *came)


def exchange(rows, axis, groups=None):
    parts = len(groups[0]) if groups else math.prod(lax.axis_size(a) for a in axis)
    rows = rows.reshape(parts, rows.shape[0] // parts, rows.shape[1])
    return lax.all_to_all(rows, axis, 0, 0, axis_index_groups=groups)


def tie(*values):
    return lax.optimization_barrier(values)


def blocks(value):
    return value.reshape(4, value.shape[0] // 4, value.shape[1])


def shards(tiles, cotangent, tissue, w_qkv, w_proj):
    mine = tiles[0]
    above, left, corner = edges(mine)
    below = send(above, "gy", lambda i: i - 1)
    right = send(left, "gx", lambda i: i - 1)
    ny, nx = lax.axis_size("gy"), lax.axis_size("gx")
    diag = lax.ppermute(
        corner,
        ("gy", "gx"),
        [
            (a * nx + b, (a - 1) % ny * nx + (b - 1) % nx)
            for a in range(ny)
            for b in range(nx)
        ],
    )
    cot = cotangent.reshape(WIN, 2, WIN, D)
    db, da, tis, live = branch(cot, tissue[0], w_proj)
    along_x, along_y = ("dp", (1, 3)), ("gy", (2, 6))
    keep0, send0, att0, dqkv0, xw, hid, hid_t = first_heads(
        mine, below, right, diag, tis, live, w_qkv, da
    )
    came = send(send0, "gy", lambda i: i ^ 1)
    keep1, send1, att1, dqkv1 = last_heads(hid, hid_t, tis, live, w_qkv, da, att0, db)
    came, send1 = tie(came, send1)
    first = add(keep0, came)
    low_a, high_a = blocks(first[:, :D]), blocks(first[:, D:])
    came_a = ring_start(low_a, high_a, *along_x)
    second = add(keep1, send(send1, "gy", lambda i: i ^ 1))
    second, att1 = tie(second, att1)
    low_b, high_b = blocks(second[:, :D]), blocks(second[:, D:])
    came_b = ring_start(low_b, high_b, *along_y)
    out = out_part(xw, tis, att0, att1, w_proj)
    came_b, out, xw, low_a, high_a = tie(came_b, out, xw, low_a, high_a)
    came_b = ring_pass(low_b, high_b, came_b, *along_y)
    came_a = ring_pass(low_a, high_a, came_a, *along_x)
    grad = grad_part(xw, cot, tis, dqkv0, dqkv1, w_qkv)
    came_a, came_b, grad = tie(came_a, came_b, grad)
    rows_a = ring_end(low_a, high_a, came_a)
    rows_b = ring_end(low_b, high_b, came_b)
    came_a = direct_start(rows_a, *along_y)
    came_b = direct_start(rows_b, *along_x)
    rows = jnp.concatenate([direct_end(rows_a, came_a), direct_end(rows_b, came_b)], 1)
    grad_qkv, grad_proj = finish(exchange(rows, ("gx",)))
    return out, grad, grad_qkv, grad_proj


def solution(mesh):
    block = P("dp", "gy", "gx", None)
    in_specs = (block, block, P("dp", "gy", "gx"), P(), P())
    out_specs = (block, block, P(("dp", "gy", "gx"), None), P(("dp", "gy", "gx"), None))
    return jax.shard_map(
        shards, mesh=mesh, in_specs=in_specs, out_specs=out_specs, check_vma=False
    )
```

```python
import math

import jax
import jax.numpy as jnp
from jax import lax
from jax.experimental import pallas as pl
from jax.experimental.pallas import tpu as pltpu
from jax.sharding import PartitionSpec as P

F32 = jnp.float32
BF = jnp.bfloat16
D = 768
WIN = 16
CELLS = WIN * WIN
GROUPS = 3
GW = D // GROUPS
HEAD_SCALE = 0.125
VMEM = 32 * 1024 * 1024


def nn(a, b):
    return lax.dot_general(a, b, (((1,), (0,)), ((), ())), preferred_element_type=F32)


def nt(a, b):
    return lax.dot_general(a, b, (((1,), (1,)), ((), ())), preferred_element_type=F32)


def tn(a, b):
    return lax.dot_general(a, b, (((0,), (0,)), ((), ())), preferred_element_type=F32)


def full(shape):
    return pl.BlockSpec(shape, lambda *g: (0,) * len(shape))


def cost(flops, size):
    return pl.CostEstimate(flops=int(flops), bytes_accessed=int(size), transcendentals=0)


def corner_kernel(tiles_ref, after_ref, corner_ref):
    corner_ref[...] = tiles_ref[...].astype(F32)[:, :8].astype(BF)


def above_kernel(tiles_ref, above_ref):
    above_ref[...] = tiles_ref[...].astype(F32)[:, 8:].astype(BF)


def left_kernel(tiles_ref, after_ref, left_ref):
    left_ref[...] = tiles_ref[...].astype(F32)[:, :8].astype(BF)


def cut(kernel, name, flops, tiles, after, block, first, columns):
    place = pl.BlockSpec(memory_space=pl.ANY)
    return pl.pallas_call(
        kernel,
        grid=(1,),
        in_specs=[pl.BlockSpec(block + (D,), lambda g: (first, 0, 0))] + [place] * len(after),
        out_specs=full((8, columns, D)),
        out_shape=jax.ShapeDtypeStruct((8, columns, D), BF),
        compiler_params=pltpu.CompilerParams(vmem_limit_bytes=VMEM),
        cost_estimate=cost(flops, 1e3),
        name=name,
    )(tiles, *after)


def edges(tiles):
    above = cut(above_kernel, "above", 3e10, tiles, [], (8, 32), 0, 24)
    corner = cut(corner_kernel, "corner", 1e3, tiles, [above], (8, 16), 0, 8)
    left = cut(left_kernel, "left", 1e3, tiles, [corner], (8, 16), 1, 8)
    return above, left, corner


def branch_kernel(
    cot_hbm, tissue_hbm, wp_hbm, db_ref, da_ref, tis_ref, live_ref, cot_ref, tissue_ref, wp_ref, sem
):
    copies = [
        pltpu.make_async_copy(tissue_hbm, tissue_ref, sem.at[0]),
        pltpu.make_async_copy(cot_hbm, cot_ref, sem.at[1]),
        pltpu.make_async_copy(wp_hbm, wp_ref, sem.at[2]),
    ]
    for copy in copies:
        copy.start()
    copies[0].wait()
    grid = tissue_ref[...].astype(F32).astype(BF)
    cell = lax.broadcasted_iota(jnp.int32, (CELLS, 1), 0)
    row_of = lax.broadcasted_iota(jnp.int32, (CELLS, WIN), 1) == (cell >> 4)
    rows = nn(row_of.astype(F32).astype(BF), grid)
    lane = lax.broadcasted_iota(jnp.int32, (CELLS, 2 * WIN), 1)
    ones = jnp.ones((2 * WIN, 128), BF)
    copies[1].wait()
    copies[2].wait()
    for w in range(2):
        own = jnp.where(lane == (cell & 15) + w * WIN, rows, 0.0).astype(BF)
        tis = nn(own, ones)
        some = jnp.max(jnp.max(tis, 0, keepdims=True), 1, keepdims=True)
        tis_ref[w] = tis.astype(BF)
        live_ref[w] = jnp.maximum(tis, 1.0 - some).astype(BF)
        db = cot_ref[:, w].reshape(CELLS, D) * jnp.tile(tis.astype(BF), (1, D // 128))
        db_ref[w] = db
        da_ref[w] = nt(db, wp_ref[...]).astype(BF)


def branch(cot, tissue, w_proj):
    shape = jax.ShapeDtypeStruct((2, CELLS, D), BF)
    mask = jax.ShapeDtypeStruct((2, CELLS, 128), BF)
    return pl.pallas_call(
        branch_kernel,
        in_specs=[pl.BlockSpec(memory_space=pltpu.HBM)] * 3,
        out_shape=[shape, shape, mask, mask],
        scratch_shapes=[
            pltpu.VMEM((WIN, 2, WIN, D), BF),
            pltpu.VMEM((WIN, 2 * WIN), jnp.int32),
            pltpu.VMEM((D, D), BF),
            pltpu.SemaphoreType.DMA((3,)),
        ],
        compiler_params=pltpu.CompilerParams(vmem_limit_bytes=VMEM),
        cost_estimate=cost(2e10, 4e6),
        name="branch",
    )(cot, tissue, w_proj)


def row_order():
    gy = lax.axis_index("gy")
    dp, y, core = lax.axis_index("dp"), gy >> 1, gy & 1
    at = lax.broadcasted_iota(jnp.int32, (D, 1), 0)
    third = ((at.astype(F32) + 0.5) * (1.0 / 3)).astype(jnp.int32)
    dp_of = ((third >> 6) & 1) ^ (((third >> 5) & 1) * 3) ^ dp
    y_of = ((third >> 4) & 1) ^ (((third >> 3) & 1) * 3) ^ y
    core_of = (third >> 7) ^ core
    source = ((dp_of * 8 + y_of * 2 + core_of) * 8 + (third & 7)) * 3 + at - third * 3
    column = lax.broadcasted_iota(jnp.int32, (D, D), 1)
    return jnp.where(column == source, 1.0, 0.0).astype(BF)


def moments(x):
    mean = jnp.mean(x, -1, keepdims=True)
    centred = x - mean
    inv = lax.rsqrt(jnp.mean(centred * centred, -1, keepdims=True) + 1e-05)
    return centred * inv, inv


def put(grad, keep_ref, send_ref, y_first):
    if y_first:
        size = D // 32
        places = [(c * 4 + x) * 4 + y for c in range(2) for y in range(4) for x in range(4)]
        grad = jnp.concatenate([grad[at * size : (at + 1) * size] for at in places], 0)
    keep_ref[...] = grad[: D // 2].astype(BF)
    send_ref[...] = grad[D // 2 :].astype(BF)


def attention(units, q, k, v, da, live, store):
    lane = lax.broadcasted_iota(jnp.int32, (1, 128), 1)
    sel = [(lane < 64).astype(BF), (lane >= 64).astype(BF)]
    weight, ds, rinv, att = {}, {}, {}, {}
    for u in units:
        for h in range(2):
            weight[u, h] = jnp.exp(nt(q[u], k[u] * sel[h])).astype(BF)
    for u in units:
        both = nn(weight[u, 0], jnp.concatenate([v[u] * sel[0], live[u] * sel[0]], 1)) + nn(
            weight[u, 1], jnp.concatenate([v[u] * sel[1], live[u] * sel[1]], 1)
        )
        rinv[u] = 1.0 / both[:, 128:]
        att[u] = both[:, :128] * rinv[u]
    for u in units:
        terms = da[u].astype(F32) * att[u]
        for h in range(2):
            delta = jnp.sum(terms * sel[h].astype(F32), 1, keepdims=True)
            dprobs = nt(da[u], v[u] * sel[h]) - delta
            ds[u, h] = (weight[u, h].astype(F32) * dprobs).astype(BF)
    for u in units:
        dq = (nn(ds[u, 0], k[u] * sel[0]) + nn(ds[u, 1], k[u] * sel[1])) * (rinv[u] * HEAD_SCALE)
        dan = (da[u].astype(F32) * rinv[u]).astype(BF)
        qn = (q[u].astype(F32) * rinv[u]).astype(BF)
        dv = tn(weight[u, 0], dan * sel[0]) + tn(weight[u, 1], dan * sel[1])
        dk = tn(ds[u, 0], qn * sel[0]) + tn(ds[u, 1], qn * sel[1])
        store(u, att[u].astype(BF), (dq.astype(BF), dk.astype(BF), dv.astype(BF)))


def window_heads(w, x, tis_ref, live_ref, weights, da_ref, outs):
    att_ref, dqkv_ref, xw_ref, hid_ref, hid_t_ref = outs
    tis = tis_ref[w]
    xw_ref[...] = x.astype(BF)
    normed, _ = moments(x)
    hidden = normed.astype(BF)
    hid_ref[...] = hidden
    hid_t_ref[...] = nt(row_order(), hidden * jnp.tile(tis, (1, D // 128))).astype(BF)
    units = [(g, p) for g in range(2) for p in range(2)]
    q, k, v, da = {}, {}, {}, {}
    for g in range(2):
        query = nn(hidden, weights[g][...]).astype(BF) * BF(HEAD_SCALE)
        key = nn(hidden, weights[2 + g][...]).astype(BF)
        value = nn(hidden, weights[4 + g][...]).astype(BF)
        for p in range(2):
            lanes = slice(p * 128, (p + 1) * 128)
            q[g, p] = query[:, lanes]
            k[g, p] = key[:, lanes] * tis
            v[g, p] = value[:, lanes] * tis
            da[g, p] = da_ref[w, :, g * GW + p * 128 : g * GW + (p + 1) * 128]

    def store(u, att, grads):
        g, p = u
        att_ref[:, g * GW + p * 128 : g * GW + (p + 1) * 128] = att
        for i, grad in enumerate(grads):
            dqkv_ref[g, :, i * GW + p * 128 : i * GW + (p + 1) * 128] = grad

    attention(units, q, k, v, da, {u: live_ref[w] for u in units}, store)


def left_window_kernel(
    tiles_ref, below_ref, tis_ref, live_ref, w0, w1, w2, w3, w4, w5, da_ref, *outs
):
    own = tiles_ref[8:16].astype(F32)
    low = below_ref[...].astype(F32)
    x = jnp.concatenate([own[:, 8:24], low[:, :16]], 0).reshape(CELLS, D)
    window_heads(0, x, tis_ref, live_ref, (w0, w1, w2, w3, w4, w5), da_ref, outs)


def right_window_kernel(
    tiles_ref, below_ref, right_ref, diag_ref, hid_t0_ref, dqkv0_ref,
    tis_ref, live_ref, w0, w1, w2, w3, w4, w5, da_ref, keep_ref, send_ref, *outs
):
    own = tiles_ref[8:16].astype(F32)
    low = below_ref[...].astype(F32)
    top = jnp.concatenate([own[:, 24:32], right_ref[...].astype(F32)], 1)
    bottom = jnp.concatenate([low[:, 16:24], diag_ref[...].astype(F32)], 1)
    x = jnp.concatenate([top, bottom], 0).reshape(CELLS, D)
    window_heads(1, x, tis_ref, live_ref, (w0, w1, w2, w3, w4, w5), da_ref, outs)
    dqkv_ref, hid_t_ref = outs[1], outs[4]
    for g in range(2):
        grad = nn(hid_t0_ref[...], dqkv0_ref[g]) + nn(hid_t_ref[...], dqkv_ref[g])
        put(grad, keep_ref.at[:, g * D : (g + 1) * D], send_ref.at[:, g * D : (g + 1) * D], False)


def last_kernel(
    hid0_ref, hid1_ref, hid_t0_ref, hid_t1_ref, tis_ref, live_ref, wq_ref, wk_ref, wv_ref, da_ref,
    att0_ref, att1_ref, db_ref, keep_ref, send_ref, att_ref, dqkv_ref,
):
    hidden = jnp.concatenate([hid0_ref[...], hid1_ref[...]], 0)
    query = nn(hidden, wq_ref[...]).astype(BF) * BF(HEAD_SCALE)
    key = nn(hidden, wk_ref[...]).astype(BF)
    value = nn(hidden, wv_ref[...]).astype(BF)
    units = [(w, p) for w in range(2) for p in range(2)]
    q, k, v, da, live = {}, {}, {}, {}, {}
    for u in units:
        w, p = u
        rows, lanes = slice(w * CELLS, (w + 1) * CELLS), slice(p * 128, (p + 1) * 128)
        q[u] = query[rows, lanes]
        k[u] = key[rows, lanes] * tis_ref[w]
        v[u] = value[rows, lanes] * tis_ref[w]
        da[u] = da_ref[w, :, lanes]
        live[u] = live_ref[w]

    def store(u, att, grads):
        w, p = u
        att_ref[w, :, p * 128 : (p + 1) * 128] = att
        for i, grad in enumerate(grads):
            dqkv_ref[w, :, i * GW + p * 128 : i * GW + (p + 1) * 128] = grad

    attention(units, q, k, v, da, live, store)
    grad = nn(hid_t0_ref[...], dqkv_ref[0]) + nn(hid_t1_ref[...], dqkv_ref[1])
    put(grad, keep_ref.at[:, :D], send_ref.at[:, :D], True)
    first = jnp.concatenate([att0_ref[...], att1_ref[...]], 0)
    attended = jnp.concatenate([first, att_ref[...].reshape(2 * CELLS, GW)], 1)
    att_t = nt(row_order(), attended).astype(BF)
    grad = nn(att_t, db_ref[...].reshape(2 * CELLS, D))
    put(grad, keep_ref.at[:, D:], send_ref.at[:, D:], True)


def columns(block, first):
    return pl.BlockSpec((D, GW), lambda g: (0, block * GROUPS + first + g))


def window_specs():
    shapes = [(CELLS, 2 * GW), (2, CELLS, D), (CELLS, D), (CELLS, D), (D, CELLS)]
    masks = [full((2, CELLS, 128))] * 2
    weights = [columns(block, g) for block in range(3) for g in range(2)]
    inputs = masks + weights + [full((2, CELLS, D))]
    return inputs, [full(s) for s in shapes], [jax.ShapeDtypeStruct(s, BF) for s in shapes]


def left_window(tiles, below, tis, live, w_qkv, da):
    inputs, outputs, shapes = window_specs()
    return pl.pallas_call(
        left_window_kernel,
        grid=(1,),
        in_specs=[full((16, 32, D)), full((8, 24, D))] + inputs,
        out_specs=outputs,
        out_shape=shapes,
        compiler_params=pltpu.CompilerParams(vmem_limit_bytes=VMEM),
        cost_estimate=cost(3e9, 5e6),
        name="left_window",
    )(tiles, below, tis, live, *[w_qkv] * 6, da)


def right_window(tiles, below, right, diag, hid_t0, dqkv0, tis, live, w_qkv, da):
    inputs, outputs, shapes = window_specs()
    half = full((D // 2, 2 * D))
    half_shape = jax.ShapeDtypeStruct((D // 2, 2 * D), BF)
    return pl.pallas_call(
        right_window_kernel,
        grid=(1,),
        in_specs=[
            full((16, 32, D)), full((8, 24, D)), full((8, 8, D)), full((8, 8, D)),
            full((D, CELLS)), full((2, CELLS, D)),
        ] + inputs,
        out_specs=[half, half] + outputs,
        out_shape=[half_shape, half_shape] + shapes,
        compiler_params=pltpu.CompilerParams(vmem_limit_bytes=VMEM),
        cost_estimate=cost(4e9, 6e6),
        name="right_window",
    )(tiles, below, right, diag, hid_t0, dqkv0, tis, live, *[w_qkv] * 6, da)


def last_heads(hids, hid_ts, tis, live, w_qkv, da, atts, db):
    rows, turned, masks = full((CELLS, D)), full((D, CELLS)), full((2, CELLS, 128))
    part = full((CELLS, 2 * GW))
    shapes = [(D // 2, 2 * D), (D // 2, 2 * D), (2, CELLS, GW), (2, CELLS, D)]
    return pl.pallas_call(
        last_kernel,
        grid=(1,),
        in_specs=[
            rows, rows, turned, turned, masks, masks, columns(0, 2), columns(1, 2), columns(2, 2),
            pl.BlockSpec((2, CELLS, GW), lambda g: (0, 0, 2)), part, part, full((2, CELLS, D)),
        ],
        out_specs=[full(s) for s in shapes],
        out_shape=[jax.ShapeDtypeStruct(s, BF) for s in shapes],
        compiler_params=pltpu.CompilerParams(vmem_limit_bytes=VMEM),
        cost_estimate=cost(4e9, 6e6),
        name="last_heads",
    )(*hids, *hid_ts, tis, live, w_qkv, w_qkv, w_qkv, da, *atts, db)


def out_kernel(xw0_ref, xw1_ref, tis_ref, att0_ref, att1_ref, att2_ref, wp_ref, out_ref):
    for w, (xw_ref, att_ref) in enumerate(((xw0_ref, att0_ref), (xw1_ref, att1_ref))):
        tis = jnp.tile(tis_ref[w].astype(F32), (1, D // 128))
        attended = jnp.concatenate([att_ref[...], att2_ref[w]], 1)
        out = xw_ref[...].astype(F32) + tis * nn(attended, wp_ref[...])
        out_ref[:, w] = out.astype(BF).reshape(WIN, WIN, D)


def out_part(xws, tis, atts, att2, w_proj):
    out = pl.pallas_call(
        out_kernel,
        out_shape=jax.ShapeDtypeStruct((WIN, 2, WIN, D), BF),
        compiler_params=pltpu.CompilerParams(vmem_limit_bytes=VMEM),
        cost_estimate=cost(1e3, 1e3),
        name="out_part",
    )(*xws, tis, *atts, att2, w_proj)
    return out.reshape(1, WIN, 2 * WIN, D)


def grad_kernel(
    xw0_ref, xw1_ref, cot_ref, tis_ref, dqkv0_ref, dqkv1_ref, dqkv2_ref,
    wq_ref, wk_ref, wv_ref, grad_ref, acc_ref,
):
    step = pl.program_id(0)
    weights = jnp.concatenate([wq_ref[...], wk_ref[...], wv_ref[...]], 1)
    first = jnp.concatenate([dqkv0_ref[0], dqkv1_ref[0]], 0)
    last = dqkv2_ref[...].reshape(2 * CELLS, D)
    part = nt(jnp.where(step < GROUPS - 1, first, last), weights)

    @pl.when(step == 0)
    def _():
        acc_ref[...] = part

    @pl.when(step > 0)
    def _():
        acc_ref[...] += part

    @pl.when(step == GROUPS - 1)
    def _():
        for w, xw_ref in enumerate((xw0_ref, xw1_ref)):
            normed, inv = moments(xw_ref[...].astype(F32))
            tis = jnp.tile(tis_ref[w].astype(F32), (1, D // 128))
            dh = acc_ref[w * CELLS : (w + 1) * CELLS] * tis
            dnorm = inv * (
                dh
                - jnp.mean(dh, -1, keepdims=True)
                - normed * jnp.mean(dh * normed, -1, keepdims=True)
            )
            grad = cot_ref[:, w].reshape(CELLS, D).astype(F32) + dnorm
            grad_ref[:, w] = grad.astype(BF).reshape(WIN, WIN, D)


def grad_part(xws, cot, tis, dqkvs, dqkv2, w_qkv):
    part = pl.BlockSpec((1, CELLS, D), lambda g: (jnp.minimum(g, 1), 0, 0))
    rows = full((CELLS, D))
    grad = pl.pallas_call(
        grad_kernel,
        grid=(GROUPS,),
        in_specs=[
            rows, rows, full((WIN, 2, WIN, D)), full((2, CELLS, 128)), part, part,
            full((2, CELLS, D)), columns(0, 0), columns(1, 0), columns(2, 0),
        ],
        out_specs=full((WIN, 2, WIN, D)),
        out_shape=jax.ShapeDtypeStruct((WIN, 2, WIN, D), BF),
        scratch_shapes=[pltpu.VMEM((2 * CELLS, D), F32)],
        compiler_params=pltpu.CompilerParams(vmem_limit_bytes=VMEM),
        cost_estimate=cost(1e3, 1e3),
        name="grad_part",
    )(*xws, cot, tis, *dqkvs, dqkv2, w_qkv, w_qkv, w_qkv)
    return grad.reshape(1, WIN, 2 * WIN, D)


def finish_kernel(parts_ref, qkv_ref, proj_ref):
    total = parts_ref[0].astype(F32)
    for part in range(1, parts_ref.shape[0]):
        total = total + parts_ref[part].astype(F32)
    total = total * (1.0 / math.sqrt(512))
    for i in range(3):
        for g in range(GROUPS):
            at = g * D + i * GW
            qkv_ref[:, i * D + g * GW : i * D + (g + 1) * GW] = total[:, at : at + GW]
    proj_ref[...] = total[:, 3 * D :]


def finish(parts):
    rows = parts.shape[1]
    return pl.pallas_call(
        finish_kernel,
        out_shape=[
            jax.ShapeDtypeStruct((rows, 3 * D), F32),
            jax.ShapeDtypeStruct((rows, D), F32),
        ],
        compiler_params=pltpu.CompilerParams(vmem_limit_bytes=VMEM),
        name="finish",
    )(parts)


def send(value, axis, move):
    devices = lax.axis_size(axis)
    return lax.ppermute(value, axis, [(i, move(i) % devices) for i in range(devices)])


def add(*terms):
    total = terms[0].astype(F32)
    for term in terms[1:]:
        total = total + term.astype(F32)
    return total.astype(BF)


def ring_start(low, high, axis, flips):
    one, three = flips
    return send(low[3], axis, lambda j: j ^ one), send(high[3], axis, lambda j: j ^ three)


def ring_pass(low, high, came, axis, flips):
    one, three = flips
    to_one = jnp.concatenate([low[2], add(high[2], came[1])], 1)
    to_three = jnp.concatenate([add(low[1], came[0]), high[1]], 1)
    return send(to_one, axis, lambda j: j ^ one), send(to_three, axis, lambda j: j ^ three)


def ring_end(low, high, came):
    n = low.shape[2]
    up, down = came
    low = add(low[0], up[:, :n], down[:, :n])
    high = add(high[0], up[:, n:], down[:, n:])
    return jnp.concatenate([low, high], 1)


def direct_start(rows, axis, flips):
    one, three = flips
    part = blocks(rows)
    return [
        send(part[at], axis, lambda j, flip=flip: j ^ flip)
        for at, flip in ((3, one ^ three), (1, three), (2, one))
    ]


def direct_end(rows, came):
    return add(blocks(rows)[0], *came)


def exchange(rows, axis, groups=None):
    parts = len(groups[0]) if groups else math.prod(lax.axis_size(a) for a in axis)
    rows = rows.reshape(parts, rows.shape[0] // parts, rows.shape[1])
    return lax.all_to_all(rows, axis, 0, 0, axis_index_groups=groups)


def tie(*values):
    return lax.optimization_barrier(values)


def blocks(value):
    return value.reshape(4, value.shape[0] // 4, value.shape[1])


def shards(tiles, cotangent, tissue, w_qkv, w_proj):
    mine = tiles[0]
    above, left, corner = edges(mine)
    below = send(above, "gy", lambda i: i - 1)
    right = send(left, "gx", lambda i: i - 1)
    ny, nx = lax.axis_size("gy"), lax.axis_size("gx")
    diag = lax.ppermute(
        corner,
        ("gy", "gx"),
        [
            (a * nx + b, (a - 1) % ny * nx + (b - 1) % nx)
            for a in range(ny)
            for b in range(nx)
        ],
    )
    cot = cotangent.reshape(WIN, 2, WIN, D)
    db, da, tis, live = branch(cot, tissue[0], w_proj)
    along_x, along_y = ("dp", (1, 3)), ("gy", (2, 6))
    att0, dqkv0, xw0, hid0, hid_t0 = left_window(mine, below, tis, live, w_qkv, da)
    keep0, send0, att1, dqkv1, xw1, hid1, hid_t1 = right_window(
        mine, below, right, diag, hid_t0, dqkv0, tis, live, w_qkv, da
    )
    came = send(send0, "gy", lambda i: i ^ 1)
    keep1, send1, att2, dqkv2 = last_heads(
        (hid0, hid1), (hid_t0, hid_t1), tis, live, w_qkv, da, (att0, att1), db
    )
    came, send1 = tie(came, send1)
    first = add(keep0, came)
    low_a, high_a = blocks(first[:, :D]), blocks(first[:, D:])
    came_a = ring_start(low_a, high_a, *along_x)
    second = add(keep1, send(send1, "gy", lambda i: i ^ 1))
    second, att2 = tie(second, att2)
    low_b, high_b = blocks(second[:, :D]), blocks(second[:, D:])
    came_b = ring_start(low_b, high_b, *along_y)
    out = out_part((xw0, xw1), tis, (att0, att1), att2, w_proj)
    came_b, out, xw0, low_a, high_a = tie(came_b, out, xw0, low_a, high_a)
    came_b = ring_pass(low_b, high_b, came_b, *along_y)
    came_a = ring_pass(low_a, high_a, came_a, *along_x)
    grad = grad_part((xw0, xw1), cot, tis, (dqkv0, dqkv1), dqkv2, w_qkv)
    came_a, came_b, grad = tie(came_a, came_b, grad)
    rows_a = ring_end(low_a, high_a, came_a)
    rows_b = ring_end(low_b, high_b, came_b)
    came_a = direct_start(rows_a, *along_y)
    came_b = direct_start(rows_b, *along_x)
    rows = jnp.concatenate([direct_end(rows_a, came_a), direct_end(rows_b, came_b)], 1)
    grad_qkv, grad_proj = finish(exchange(rows, ("gx",)))
    return out, grad, grad_qkv, grad_proj


def solution(mesh):
    block = P("dp", "gy", "gx", None)
    in_specs = (block, block, P("dp", "gy", "gx"), P(), P())
    out_specs = (block, block, P(("dp", "gy", "gx"), None), P(("dp", "gy", "gx"), None))
    return jax.shard_map(
        shards, mesh=mesh, in_specs=in_specs, out_specs=out_specs, check_vma=False
    )
```

```python
import math

import jax
import jax.numpy as jnp
from jax import lax
from jax.experimental import pallas as pl
from jax.experimental.pallas import tpu as pltpu
from jax.sharding import PartitionSpec as P

F32 = jnp.float32
BF = jnp.bfloat16
D = 768
WIN = 16
CELLS = WIN * WIN
GROUPS = 3
GW = D // GROUPS
HEAD_SCALE = 0.125
VMEM = 32 * 1024 * 1024
LATE_VMEM = 60 * 1024 * 1024


def nn(a, b):
    return lax.dot_general(a, b, (((1,), (0,)), ((), ())), preferred_element_type=F32)


def nt(a, b):
    return lax.dot_general(a, b, (((1,), (1,)), ((), ())), preferred_element_type=F32)


def tn(a, b):
    return lax.dot_general(a, b, (((0,), (0,)), ((), ())), preferred_element_type=F32)


def full(shape):
    return pl.BlockSpec(shape, lambda *g: (0,) * len(shape))


def cost(flops, size):
    return pl.CostEstimate(flops=int(flops), bytes_accessed=int(size), transcendentals=0)


def corner_kernel(tiles_ref, after_ref, corner_ref):
    corner_ref[...] = tiles_ref[...].astype(F32)[:, :8].astype(BF)


def above_kernel(tiles_ref, above_ref):
    above_ref[...] = tiles_ref[...].astype(F32)[:, 8:].astype(BF)


def left_kernel(tiles_ref, after_ref, left_ref):
    left_ref[...] = tiles_ref[...].astype(F32)[:, :8].astype(BF)


def cut(kernel, name, flops, tiles, after, block, first, columns):
    place = pl.BlockSpec(memory_space=pl.ANY)
    return pl.pallas_call(
        kernel,
        grid=(1,),
        in_specs=[pl.BlockSpec(block + (D,), lambda g: (first, 0, 0))] + [place] * len(after),
        out_specs=full((8, columns, D)),
        out_shape=jax.ShapeDtypeStruct((8, columns, D), BF),
        compiler_params=pltpu.CompilerParams(vmem_limit_bytes=VMEM),
        cost_estimate=cost(flops, 1e3),
        name=name,
    )(tiles, *after)


def edges(tiles):
    above = cut(above_kernel, "above", 3e10, tiles, [], (8, 32), 0, 24)
    corner = cut(corner_kernel, "corner", 1e3, tiles, [above], (8, 16), 0, 8)
    left = cut(left_kernel, "left", 1e3, tiles, [corner], (8, 16), 1, 8)
    return above, left, corner


def branch_kernel(
    cot_hbm, tissue_hbm, wp_hbm, db_ref, da_ref, tis_ref, live_ref, cot_ref, tissue_ref, wp_ref, sem
):
    copies = [
        pltpu.make_async_copy(tissue_hbm, tissue_ref, sem.at[0]),
        pltpu.make_async_copy(cot_hbm, cot_ref, sem.at[1]),
        pltpu.make_async_copy(wp_hbm, wp_ref, sem.at[2]),
    ]
    for copy in copies:
        copy.start()
    copies[0].wait()
    grid = tissue_ref[...].astype(F32).astype(BF)
    cell = lax.broadcasted_iota(jnp.int32, (CELLS, 1), 0)
    row_of = lax.broadcasted_iota(jnp.int32, (CELLS, WIN), 1) == (cell >> 4)
    rows = nn(row_of.astype(F32).astype(BF), grid)
    lane = lax.broadcasted_iota(jnp.int32, (CELLS, 2 * WIN), 1)
    ones = jnp.ones((2 * WIN, 128), BF)
    copies[1].wait()
    copies[2].wait()
    for w in range(2):
        own = jnp.where(lane == (cell & 15) + w * WIN, rows, 0.0).astype(BF)
        tis = nn(own, ones)
        some = jnp.max(jnp.max(tis, 0, keepdims=True), 1, keepdims=True)
        tis_ref[w] = tis.astype(BF)
        live_ref[w] = jnp.maximum(tis, 1.0 - some).astype(BF)
        db = cot_ref[:, w].reshape(CELLS, D) * jnp.tile(tis.astype(BF), (1, D // 128))
        db_ref[w] = db
        da_ref[w] = nt(db, wp_ref[...]).astype(BF)


def branch(cot, tissue, w_proj):
    shape = jax.ShapeDtypeStruct((2, CELLS, D), BF)
    mask = jax.ShapeDtypeStruct((2, CELLS, 128), BF)
    return pl.pallas_call(
        branch_kernel,
        in_specs=[pl.BlockSpec(memory_space=pltpu.HBM)] * 3,
        out_shape=[shape, shape, mask, mask],
        scratch_shapes=[
            pltpu.VMEM((WIN, 2, WIN, D), BF),
            pltpu.VMEM((WIN, 2 * WIN), jnp.int32),
            pltpu.VMEM((D, D), BF),
            pltpu.SemaphoreType.DMA((3,)),
        ],
        compiler_params=pltpu.CompilerParams(vmem_limit_bytes=VMEM),
        cost_estimate=cost(2e10, 4e6),
        name="branch",
    )(cot, tissue, w_proj)


def row_order():
    gy = lax.axis_index("gy")
    dp, y, core = lax.axis_index("dp"), gy >> 1, gy & 1
    at = lax.broadcasted_iota(jnp.int32, (D, 1), 0)
    third = ((at.astype(F32) + 0.5) * (1.0 / 3)).astype(jnp.int32)
    dp_of = ((third >> 6) & 1) ^ (((third >> 5) & 1) * 3) ^ dp
    y_of = ((third >> 4) & 1) ^ (((third >> 3) & 1) * 3) ^ y
    core_of = (third >> 7) ^ core
    source = ((dp_of * 8 + y_of * 2 + core_of) * 8 + (third & 7)) * 3 + at - third * 3
    column = lax.broadcasted_iota(jnp.int32, (D, D), 1)
    return jnp.where(column == source, 1.0, 0.0).astype(BF)


def moments(x):
    mean = jnp.mean(x, -1, keepdims=True)
    centred = x - mean
    inv = lax.rsqrt(jnp.mean(centred * centred, -1, keepdims=True) + 1e-05)
    return centred * inv, inv


def put(grad, keep_ref, send_ref, y_first):
    if y_first:
        size = D // 32
        places = [(c * 4 + x) * 4 + y for c in range(2) for y in range(4) for x in range(4)]
        grad = jnp.concatenate([grad[at * size : (at + 1) * size] for at in places], 0)
    keep_ref[...] = grad[: D // 2].astype(BF)
    send_ref[...] = grad[D // 2 :].astype(BF)


def attention(units, q, k, v, da, live, store):
    lane = lax.broadcasted_iota(jnp.int32, (1, 128), 1)
    sel = [(lane < 64).astype(BF), (lane >= 64).astype(BF)]
    weight, ds, rinv, att = {}, {}, {}, {}
    for u in units:
        for h in range(2):
            weight[u, h] = jnp.exp(nt(q[u], k[u] * sel[h])).astype(BF)
    for u in units:
        both = nn(weight[u, 0], jnp.concatenate([v[u] * sel[0], live[u] * sel[0]], 1)) + nn(
            weight[u, 1], jnp.concatenate([v[u] * sel[1], live[u] * sel[1]], 1)
        )
        rinv[u] = 1.0 / both[:, 128:]
        att[u] = both[:, :128] * rinv[u]
    for u in units:
        terms = da[u].astype(F32) * att[u]
        for h in range(2):
            delta = jnp.sum(terms * sel[h].astype(F32), 1, keepdims=True)
            dprobs = nt(da[u], v[u] * sel[h]) - delta
            ds[u, h] = (weight[u, h].astype(F32) * dprobs).astype(BF)
    for u in units:
        dq = (nn(ds[u, 0], k[u] * sel[0]) + nn(ds[u, 1], k[u] * sel[1])) * (rinv[u] * HEAD_SCALE)
        dan = (da[u].astype(F32) * rinv[u]).astype(BF)
        qn = (q[u].astype(F32) * rinv[u]).astype(BF)
        dv = tn(weight[u, 0], dan * sel[0]) + tn(weight[u, 1], dan * sel[1])
        dk = tn(ds[u, 0], qn * sel[0]) + tn(ds[u, 1], qn * sel[1])
        store(u, att[u].astype(BF), (dq.astype(BF), dk.astype(BF), dv.astype(BF)))


def window_heads(w, x, tis_ref, live_ref, weights, da_ref, outs):
    att_ref, dqkv_ref, xw_ref, hid_ref, hid_t_ref = outs
    tis = tis_ref[w]
    xw_ref[...] = x.astype(BF)
    normed, _ = moments(x)
    hidden = normed.astype(BF)
    hid_ref[...] = hidden
    hid_t_ref[...] = nt(row_order(), hidden * jnp.tile(tis, (1, D // 128))).astype(BF)
    units = [(g, p) for g in range(2) for p in range(2)]
    q, k, v, da = {}, {}, {}, {}
    for g in range(2):
        query = nn(hidden, weights[g][...]).astype(BF) * BF(HEAD_SCALE)
        key = nn(hidden, weights[2 + g][...]).astype(BF)
        value = nn(hidden, weights[4 + g][...]).astype(BF)
        for p in range(2):
            lanes = slice(p * 128, (p + 1) * 128)
            q[g, p] = query[:, lanes]
            k[g, p] = key[:, lanes] * tis
            v[g, p] = value[:, lanes] * tis
            da[g, p] = da_ref[w, :, g * GW + p * 128 : g * GW + (p + 1) * 128]

    def store(u, att, grads):
        g, p = u
        att_ref[:, g * GW + p * 128 : g * GW + (p + 1) * 128] = att
        for i, grad in enumerate(grads):
            dqkv_ref[g, :, i * GW + p * 128 : i * GW + (p + 1) * 128] = grad

    attention(units, q, k, v, da, {u: live_ref[w] for u in units}, store)


def left_window_kernel(
    tiles_ref, below_ref, tis_ref, live_ref, w0, w1, w2, w3, w4, w5, da_ref, *outs
):
    own = tiles_ref[8:16].astype(F32)
    low = below_ref[...].astype(F32)
    x = jnp.concatenate([own[:, 8:24], low[:, :16]], 0).reshape(CELLS, D)
    window_heads(0, x, tis_ref, live_ref, (w0, w1, w2, w3, w4, w5), da_ref, outs)


def right_window_kernel(
    tiles_ref, below_ref, right_ref, diag_ref, hid_t0_ref, dqkv0_ref,
    tis_ref, live_ref, w0, w1, w2, w3, w4, w5, da_ref, keep_ref, send_ref, *outs
):
    own = tiles_ref[8:16].astype(F32)
    low = below_ref[...].astype(F32)
    top = jnp.concatenate([own[:, 24:32], right_ref[...].astype(F32)], 1)
    bottom = jnp.concatenate([low[:, 16:24], diag_ref[...].astype(F32)], 1)
    x = jnp.concatenate([top, bottom], 0).reshape(CELLS, D)
    window_heads(1, x, tis_ref, live_ref, (w0, w1, w2, w3, w4, w5), da_ref, outs)
    dqkv_ref, hid_t_ref = outs[1], outs[4]
    for g in range(2):
        grad = nn(hid_t0_ref[...], dqkv0_ref[g]) + nn(hid_t_ref[...], dqkv_ref[g])
        put(grad, keep_ref.at[:, g * D : (g + 1) * D], send_ref.at[:, g * D : (g + 1) * D], False)


def last_kernel(
    hid0_ref, hid1_ref, hid_t0_ref, hid_t1_ref, tis_ref, live_ref, wq_ref, wk_ref, wv_ref, da_ref,
    att0_ref, att1_ref, db_ref, keep_ref, send_ref, att_ref, dqkv_ref,
):
    hidden = jnp.concatenate([hid0_ref[...], hid1_ref[...]], 0)
    query = nn(hidden, wq_ref[...]).astype(BF) * BF(HEAD_SCALE)
    key = nn(hidden, wk_ref[...]).astype(BF)
    value = nn(hidden, wv_ref[...]).astype(BF)
    units = [(w, p) for w in range(2) for p in range(2)]
    q, k, v, da, live = {}, {}, {}, {}, {}
    for u in units:
        w, p = u
        rows, lanes = slice(w * CELLS, (w + 1) * CELLS), slice(p * 128, (p + 1) * 128)
        q[u] = query[rows, lanes]
        k[u] = key[rows, lanes] * tis_ref[w]
        v[u] = value[rows, lanes] * tis_ref[w]
        da[u] = da_ref[w, :, lanes]
        live[u] = live_ref[w]

    def store(u, att, grads):
        w, p = u
        att_ref[w, :, p * 128 : (p + 1) * 128] = att
        for i, grad in enumerate(grads):
            dqkv_ref[w, :, i * GW + p * 128 : i * GW + (p + 1) * 128] = grad

    attention(units, q, k, v, da, live, store)
    grad = nn(hid_t0_ref[...], dqkv_ref[0]) + nn(hid_t1_ref[...], dqkv_ref[1])
    put(grad, keep_ref.at[:, :D], send_ref.at[:, :D], True)
    first = jnp.concatenate([att0_ref[...], att1_ref[...]], 0)
    attended = jnp.concatenate([first, att_ref[...].reshape(2 * CELLS, GW)], 1)
    att_t = nt(row_order(), attended).astype(BF)
    grad = nn(att_t, db_ref[...].reshape(2 * CELLS, D))
    put(grad, keep_ref.at[:, D:], send_ref.at[:, D:], True)


def columns(block, first):
    return pl.BlockSpec((D, GW), lambda g: (0, block * GROUPS + first + g))


def window_specs():
    shapes = [(CELLS, 2 * GW), (2, CELLS, D), (CELLS, D), (CELLS, D), (D, CELLS)]
    masks = [full((2, CELLS, 128))] * 2
    weights = [columns(block, g) for block in range(3) for g in range(2)]
    inputs = masks + weights + [full((2, CELLS, D))]
    return inputs, [full(s) for s in shapes], [jax.ShapeDtypeStruct(s, BF) for s in shapes]


def left_window(tiles, below, tis, live, w_qkv, da):
    inputs, outputs, shapes = window_specs()
    return pl.pallas_call(
        left_window_kernel,
        grid=(1,),
        in_specs=[full((16, 32, D)), full((8, 24, D))] + inputs,
        out_specs=outputs,
        out_shape=shapes,
        compiler_params=pltpu.CompilerParams(vmem_limit_bytes=VMEM),
        cost_estimate=cost(3e9, 5e6),
        name="left_window",
    )(tiles, below, tis, live, *[w_qkv] * 6, da)


def right_window(tiles, below, right, diag, hid_t0, dqkv0, tis, live, w_qkv, da):
    inputs, outputs, shapes = window_specs()
    half = full((D // 2, 2 * D))
    half_shape = jax.ShapeDtypeStruct((D // 2, 2 * D), BF)
    return pl.pallas_call(
        right_window_kernel,
        grid=(1,),
        in_specs=[
            full((16, 32, D)), full((8, 24, D)), full((8, 8, D)), full((8, 8, D)),
            full((D, CELLS)), full((2, CELLS, D)),
        ] + inputs,
        out_specs=[half, half] + outputs,
        out_shape=[half_shape, half_shape] + shapes,
        compiler_params=pltpu.CompilerParams(vmem_limit_bytes=VMEM),
        cost_estimate=cost(4e9, 6e6),
        name="right_window",
    )(tiles, below, right, diag, hid_t0, dqkv0, tis, live, *[w_qkv] * 6, da)


def last_heads(hids, hid_ts, tis, live, w_qkv, da, atts, db):
    rows, turned, masks = full((CELLS, D)), full((D, CELLS)), full((2, CELLS, 128))
    part = full((CELLS, 2 * GW))
    shapes = [(D // 2, 2 * D), (D // 2, 2 * D), (2, CELLS, GW), (2, CELLS, D)]
    return pl.pallas_call(
        last_kernel,
        grid=(1,),
        in_specs=[
            rows, rows, turned, turned, masks, masks, columns(0, 2), columns(1, 2), columns(2, 2),
            pl.BlockSpec((2, CELLS, GW), lambda g: (0, 0, 2)), part, part, full((2, CELLS, D)),
        ],
        out_specs=[full(s) for s in shapes],
        out_shape=[jax.ShapeDtypeStruct(s, BF) for s in shapes],
        compiler_params=pltpu.CompilerParams(vmem_limit_bytes=VMEM),
        cost_estimate=cost(4e9, 6e6),
        name="last_heads",
    )(*hids, *hid_ts, tis, live, w_qkv, w_qkv, w_qkv, da, *atts, db)


def out_kernel(xw0_ref, xw1_ref, tis_ref, att0_ref, att1_ref, att2_ref, wp_ref, out_ref):
    for w, (xw_ref, att_ref) in enumerate(((xw0_ref, att0_ref), (xw1_ref, att1_ref))):
        tis = jnp.tile(tis_ref[w].astype(F32), (1, D // 128))
        attended = jnp.concatenate([att_ref[...], att2_ref[w]], 1)
        out = xw_ref[...].astype(F32) + tis * nn(attended, wp_ref[...])
        out_ref[:, w] = out.astype(BF).reshape(WIN, WIN, D)


def out_part(xws, tis, atts, att2, w_proj):
    out = pl.pallas_call(
        out_kernel,
        out_shape=jax.ShapeDtypeStruct((WIN, 2, WIN, D), BF),
        compiler_params=pltpu.CompilerParams(vmem_limit_bytes=LATE_VMEM),
        cost_estimate=cost(1e3, 1e3),
        name="out_part",
    )(*xws, tis, *atts, att2, w_proj)
    return out.reshape(1, WIN, 2 * WIN, D)


def grad_kernel(
    xw0_ref, xw1_ref, cot_ref, tis_ref, dqkv0_ref, dqkv1_ref, dqkv2_ref,
    wq_ref, wk_ref, wv_ref, grad_ref, acc_ref,
):
    step = pl.program_id(0)
    weights = jnp.concatenate([wq_ref[...], wk_ref[...], wv_ref[...]], 1)
    first = jnp.concatenate([dqkv0_ref[0], dqkv1_ref[0]], 0)
    last = dqkv2_ref[...].reshape(2 * CELLS, D)
    part = nt(jnp.where(step < GROUPS - 1, first, last), weights)

    @pl.when(step == 0)
    def _():
        acc_ref[...] = part

    @pl.when(step > 0)
    def _():
        acc_ref[...] += part

    @pl.when(step == GROUPS - 1)
    def _():
        for w, xw_ref in enumerate((xw0_ref, xw1_ref)):
            normed, inv = moments(xw_ref[...].astype(F32))
            tis = jnp.tile(tis_ref[w].astype(F32), (1, D // 128))
            dh = acc_ref[w * CELLS : (w + 1) * CELLS] * tis
            dnorm = inv * (
                dh
                - jnp.mean(dh, -1, keepdims=True)
                - normed * jnp.mean(dh * normed, -1, keepdims=True)
            )
            grad = cot_ref[:, w].reshape(CELLS, D).astype(F32) + dnorm
            grad_ref[:, w] = grad.astype(BF).reshape(WIN, WIN, D)


def grad_part(xws, cot, tis, dqkvs, dqkv2, w_qkv):
    part = pl.BlockSpec((1, CELLS, D), lambda g: (jnp.minimum(g, 1), 0, 0))
    rows = full((CELLS, D))
    grad = pl.pallas_call(
        grad_kernel,
        grid=(GROUPS,),
        in_specs=[
            rows, rows, full((WIN, 2, WIN, D)), full((2, CELLS, 128)), part, part,
            full((2, CELLS, D)), columns(0, 0), columns(1, 0), columns(2, 0),
        ],
        out_specs=full((WIN, 2, WIN, D)),
        out_shape=jax.ShapeDtypeStruct((WIN, 2, WIN, D), BF),
        scratch_shapes=[pltpu.VMEM((2 * CELLS, D), F32)],
        compiler_params=pltpu.CompilerParams(vmem_limit_bytes=LATE_VMEM),
        cost_estimate=cost(1e3, 1e3),
        name="grad_part",
    )(*xws, cot, tis, *dqkvs, dqkv2, w_qkv, w_qkv, w_qkv)
    return grad.reshape(1, WIN, 2 * WIN, D)


def finish_kernel(parts_ref, qkv_ref, proj_ref):
    total = parts_ref[0].astype(F32)
    for part in range(1, parts_ref.shape[0]):
        total = total + parts_ref[part].astype(F32)
    total = total * (1.0 / math.sqrt(512))
    for i in range(3):
        for g in range(GROUPS):
            at = g * D + i * GW
            qkv_ref[:, i * D + g * GW : i * D + (g + 1) * GW] = total[:, at : at + GW]
    proj_ref[...] = total[:, 3 * D :]


def finish(parts):
    rows = parts.shape[1]
    return pl.pallas_call(
        finish_kernel,
        out_shape=[
            jax.ShapeDtypeStruct((rows, 3 * D), F32),
            jax.ShapeDtypeStruct((rows, D), F32),
        ],
        compiler_params=pltpu.CompilerParams(vmem_limit_bytes=VMEM),
        name="finish",
    )(parts)


def send(value, axis, move):
    devices = lax.axis_size(axis)
    return lax.ppermute(value, axis, [(i, move(i) % devices) for i in range(devices)])


def add(*terms):
    total = terms[0].astype(F32)
    for term in terms[1:]:
        total = total + term.astype(F32)
    return total.astype(BF)


def ring_start(low, high, axis, flips):
    one, three = flips
    return send(low[3], axis, lambda j: j ^ one), send(high[3], axis, lambda j: j ^ three)


def ring_pass(low, high, came, axis, flips):
    one, three = flips
    to_one = jnp.concatenate([low[2], add(high[2], came[1])], 1)
    to_three = jnp.concatenate([add(low[1], came[0]), high[1]], 1)
    return send(to_one, axis, lambda j: j ^ one), send(to_three, axis, lambda j: j ^ three)


def ring_end(low, high, came):
    n = low.shape[2]
    up, down = came
    low = add(low[0], up[:, :n], down[:, :n])
    high = add(high[0], up[:, n:], down[:, n:])
    return jnp.concatenate([low, high], 1)


def direct_start(rows, axis, flips):
    one, three = flips
    part = blocks(rows)
    return [
        send(part[at], axis, lambda j, flip=flip: j ^ flip)
        for at, flip in ((3, one ^ three), (1, three), (2, one))
    ]


def direct_end(rows, came):
    return add(blocks(rows)[0], *came)


def exchange(rows, axis, groups=None):
    parts = len(groups[0]) if groups else math.prod(lax.axis_size(a) for a in axis)
    rows = rows.reshape(parts, rows.shape[0] // parts, rows.shape[1])
    return lax.all_to_all(rows, axis, 0, 0, axis_index_groups=groups)


def tie(*values):
    return lax.optimization_barrier(values)


def blocks(value):
    return value.reshape(4, value.shape[0] // 4, value.shape[1])


def shards(tiles, cotangent, tissue, w_qkv, w_proj):
    mine = tiles[0]
    above, left, corner = edges(mine)
    below = send(above, "gy", lambda i: i - 1)
    right = send(left, "gx", lambda i: i - 1)
    ny, nx = lax.axis_size("gy"), lax.axis_size("gx")
    diag = lax.ppermute(
        corner,
        ("gy", "gx"),
        [
            (a * nx + b, (a - 1) % ny * nx + (b - 1) % nx)
            for a in range(ny)
            for b in range(nx)
        ],
    )
    cot = cotangent.reshape(WIN, 2, WIN, D)
    db, da, tis, live = branch(cot, tissue[0], w_proj)
    along_x, along_y = ("dp", (1, 3)), ("gy", (2, 6))
    att0, dqkv0, xw0, hid0, hid_t0 = left_window(mine, below, tis, live, w_qkv, da)
    keep0, send0, att1, dqkv1, xw1, hid1, hid_t1 = right_window(
        mine, below, right, diag, hid_t0, dqkv0, tis, live, w_qkv, da
    )
    came = send(send0, "gy", lambda i: i ^ 1)
    keep1, send1, att2, dqkv2 = last_heads(
        (hid0, hid1), (hid_t0, hid_t1), tis, live, w_qkv, da, (att0, att1), db
    )
    came, send1 = tie(came, send1)
    first = add(keep0, came)
    low_a, high_a = blocks(first[:, :D]), blocks(first[:, D:])
    came_a = ring_start(low_a, high_a, *along_x)
    second = add(keep1, send(send1, "gy", lambda i: i ^ 1))
    low_b, high_b = blocks(second[:, :D]), blocks(second[:, D:])
    came_b = ring_start(low_b, high_b, *along_y)
    came_b, low_a, high_a = tie(came_b, low_a, high_a)
    came_b = ring_pass(low_b, high_b, came_b, *along_y)
    came_a = ring_pass(low_a, high_a, came_a, *along_x)
    rows_a = ring_end(low_a, high_a, came_a)
    came_a = direct_start(rows_a, *along_y)
    rows_b = ring_end(low_b, high_b, came_b)
    came_b = direct_start(rows_b, *along_x)
    rows = jnp.concatenate([direct_end(rows_a, came_a), direct_end(rows_b, came_b)], 1)
    rows, xw0, att2 = tie(rows, xw0, att2)
    parts = exchange(rows, ("gx",))
    out = out_part((xw0, xw1), tis, (att0, att1), att2, w_proj)
    grad = grad_part((xw0, xw1), cot, tis, (dqkv0, dqkv1), dqkv2, w_qkv)
    out, grad, parts = tie(out, grad, parts)
    grad_qkv, grad_proj = finish(parts)
    return out, grad, grad_qkv, grad_proj


def solution(mesh):
    block = P("dp", "gy", "gx", None)
    in_specs = (block, block, P("dp", "gy", "gx"), P(), P())
    out_specs = (block, block, P(("dp", "gy", "gx"), None), P(("dp", "gy", "gx"), None))
    return jax.shard_map(
        shards, mesh=mesh, in_specs=in_specs, out_specs=out_specs, check_vma=False
    )
```

```python
import math

import jax
import jax.numpy as jnp
from jax import lax
from jax.experimental import pallas as pl
from jax.experimental.pallas import tpu as pltpu
from jax.sharding import PartitionSpec as P

F32 = jnp.float32
BF = jnp.bfloat16
D = 768
WIN = 16
CELLS = WIN * WIN
GROUPS = 3
GW = D // GROUPS
HEAD_SCALE = 0.125
VMEM = 32 * 1024 * 1024


def nn(a, b):
    return lax.dot_general(a, b, (((1,), (0,)), ((), ())), preferred_element_type=F32)


def nt(a, b):
    return lax.dot_general(a, b, (((1,), (1,)), ((), ())), preferred_element_type=F32)


def tn(a, b):
    return lax.dot_general(a, b, (((0,), (0,)), ((), ())), preferred_element_type=F32)


def full(shape):
    return pl.BlockSpec(shape, lambda *g: (0,) * len(shape))


def cost(flops, size):
    return pl.CostEstimate(flops=int(flops), bytes_accessed=int(size), transcendentals=0)


def corner_kernel(tiles_ref, after_ref, corner_ref):
    corner_ref[...] = tiles_ref[...].astype(F32)[:, :8].astype(BF)


def above_kernel(tiles_ref, above_ref):
    above_ref[...] = tiles_ref[...].astype(F32)[:, 8:].astype(BF)


def left_kernel(tiles_ref, after_ref, left_ref):
    left_ref[...] = tiles_ref[...].astype(F32)[:, :8].astype(BF)


def cut(kernel, name, flops, tiles, after, block, first, columns):
    place = pl.BlockSpec(memory_space=pl.ANY)
    return pl.pallas_call(
        kernel,
        grid=(1,),
        in_specs=[pl.BlockSpec(block + (D,), lambda g: (first, 0, 0))] + [place] * len(after),
        out_specs=full((8, columns, D)),
        out_shape=jax.ShapeDtypeStruct((8, columns, D), BF),
        compiler_params=pltpu.CompilerParams(vmem_limit_bytes=VMEM),
        cost_estimate=cost(flops, 1e3),
        name=name,
    )(tiles, *after)


def edges(tiles):
    above = cut(above_kernel, "above", 3e10, tiles, [], (8, 32), 0, 24)
    corner = cut(corner_kernel, "corner", 1e3, tiles, [above], (8, 16), 0, 8)
    left = cut(left_kernel, "left", 1e3, tiles, [corner], (8, 16), 1, 8)
    return above, left, corner


def branch_kernel(
    cot_hbm, tissue_hbm, wp_hbm, db_ref, da_ref, tis_ref, live_ref, cot_ref, tissue_ref, wp_ref, sem
):
    copies = [
        pltpu.make_async_copy(tissue_hbm, tissue_ref, sem.at[0]),
        pltpu.make_async_copy(cot_hbm, cot_ref, sem.at[1]),
        pltpu.make_async_copy(wp_hbm, wp_ref, sem.at[2]),
    ]
    for copy in copies:
        copy.start()
    copies[0].wait()
    grid = tissue_ref[...].astype(F32).astype(BF)
    cell = lax.broadcasted_iota(jnp.int32, (CELLS, 1), 0)
    row_of = lax.broadcasted_iota(jnp.int32, (CELLS, WIN), 1) == (cell >> 4)
    rows = nn(row_of.astype(F32).astype(BF), grid)
    lane = lax.broadcasted_iota(jnp.int32, (CELLS, 2 * WIN), 1)
    ones = jnp.ones((2 * WIN, 128), BF)
    copies[1].wait()
    copies[2].wait()
    for w in range(2):
        own = jnp.where(lane == (cell & 15) + w * WIN, rows, 0.0).astype(BF)
        tis = nn(own, ones)
        some = jnp.max(jnp.max(tis, 0, keepdims=True), 1, keepdims=True)
        tis_ref[w] = tis.astype(BF)
        live_ref[w] = jnp.maximum(tis, 1.0 - some).astype(BF)
        db = cot_ref[:, w].reshape(CELLS, D) * jnp.tile(tis.astype(BF), (1, D // 128))
        db_ref[w] = db
        da_ref[w] = nt(db, wp_ref[...]).astype(BF)


def branch(cot, tissue, w_proj):
    shape = jax.ShapeDtypeStruct((2, CELLS, D), BF)
    mask = jax.ShapeDtypeStruct((2, CELLS, 128), BF)
    return pl.pallas_call(
        branch_kernel,
        in_specs=[pl.BlockSpec(memory_space=pltpu.HBM)] * 3,
        out_shape=[shape, shape, mask, mask],
        scratch_shapes=[
            pltpu.VMEM((WIN, 2, WIN, D), BF),
            pltpu.VMEM((WIN, 2 * WIN), jnp.int32),
            pltpu.VMEM((D, D), BF),
            pltpu.SemaphoreType.DMA((3,)),
        ],
        compiler_params=pltpu.CompilerParams(vmem_limit_bytes=VMEM),
        cost_estimate=cost(2e10, 4e6),
        name="branch",
    )(cot, tissue, w_proj)


def row_order():
    gy = lax.axis_index("gy")
    dp, y, core = lax.axis_index("dp"), gy >> 1, gy & 1
    at = lax.broadcasted_iota(jnp.int32, (D, 1), 0)
    third = ((at.astype(F32) + 0.5) * (1.0 / 3)).astype(jnp.int32)
    dp_of = ((third >> 6) & 1) ^ (((third >> 5) & 1) * 3) ^ dp
    y_of = ((third >> 4) & 1) ^ (((third >> 3) & 1) * 3) ^ y
    core_of = (third >> 7) ^ core
    source = ((dp_of * 8 + y_of * 2 + core_of) * 8 + (third & 7)) * 3 + at - third * 3
    column = lax.broadcasted_iota(jnp.int32, (D, D), 1)
    return jnp.where(column == source, 1.0, 0.0).astype(BF)


def moments(x):
    mean = jnp.mean(x, -1, keepdims=True)
    centred = x - mean
    inv = lax.rsqrt(jnp.mean(centred * centred, -1, keepdims=True) + 1e-05)
    return centred * inv, inv


def put(grad, keep_ref, send_ref, y_first):
    if y_first:
        size = D // 32
        places = [(c * 4 + x) * 4 + y for c in range(2) for y in range(4) for x in range(4)]
        grad = jnp.concatenate([grad[at * size : (at + 1) * size] for at in places], 0)
    keep_ref[...] = grad[: D // 2].astype(BF)
    send_ref[...] = grad[D // 2 :].astype(BF)


def attention(units, q, k, v, da, live, store):
    lane = lax.broadcasted_iota(jnp.int32, (1, 128), 1)
    sel = [(lane < 64).astype(BF), (lane >= 64).astype(BF)]
    weight, ds, rinv, att = {}, {}, {}, {}
    for u in units:
        for h in range(2):
            weight[u, h] = jnp.exp(nt(q[u], k[u] * sel[h])).astype(BF)
    for u in units:
        both = nn(weight[u, 0], jnp.concatenate([v[u] * sel[0], live[u] * sel[0]], 1)) + nn(
            weight[u, 1], jnp.concatenate([v[u] * sel[1], live[u] * sel[1]], 1)
        )
        rinv[u] = 1.0 / both[:, 128:]
        att[u] = both[:, :128] * rinv[u]
    for u in units:
        terms = da[u].astype(F32) * att[u]
        for h in range(2):
            delta = jnp.sum(terms * sel[h].astype(F32), 1, keepdims=True)
            dprobs = nt(da[u], v[u] * sel[h]) - delta
            ds[u, h] = (weight[u, h].astype(F32) * dprobs).astype(BF)
    for u in units:
        dq = (nn(ds[u, 0], k[u] * sel[0]) + nn(ds[u, 1], k[u] * sel[1])) * (rinv[u] * HEAD_SCALE)
        dan = (da[u].astype(F32) * rinv[u]).astype(BF)
        qn = (q[u].astype(F32) * rinv[u]).astype(BF)
        dv = tn(weight[u, 0], dan * sel[0]) + tn(weight[u, 1], dan * sel[1])
        dk = tn(ds[u, 0], qn * sel[0]) + tn(ds[u, 1], qn * sel[1])
        store(u, att[u].astype(BF), (dq.astype(BF), dk.astype(BF), dv.astype(BF)))


def window_heads(w, x, tis_ref, live_ref, weights, da_ref, outs):
    att_ref, dqkv_ref, xw_ref, hid_ref, hid_t_ref = outs
    tis = tis_ref[w]
    xw_ref[...] = x.astype(BF)
    normed, _ = moments(x)
    hidden = normed.astype(BF)
    hid_ref[...] = hidden
    hid_t_ref[...] = nt(row_order(), hidden * jnp.tile(tis, (1, D // 128))).astype(BF)
    units = [(g, p) for g in range(2) for p in range(2)]
    q, k, v, da = {}, {}, {}, {}
    for g in range(2):
        query = nn(hidden, weights[g][...]).astype(BF) * BF(HEAD_SCALE)
        key = nn(hidden, weights[2 + g][...]).astype(BF)
        value = nn(hidden, weights[4 + g][...]).astype(BF)
        for p in range(2):
            lanes = slice(p * 128, (p + 1) * 128)
            q[g, p] = query[:, lanes]
            k[g, p] = key[:, lanes] * tis
            v[g, p] = value[:, lanes] * tis
            da[g, p] = da_ref[w, :, g * GW + p * 128 : g * GW + (p + 1) * 128]

    def store(u, att, grads):
        g, p = u
        att_ref[:, g * GW + p * 128 : g * GW + (p + 1) * 128] = att
        for i, grad in enumerate(grads):
            dqkv_ref[g, :, i * GW + p * 128 : i * GW + (p + 1) * 128] = grad

    attention(units, q, k, v, da, {u: live_ref[w] for u in units}, store)


def left_window_kernel(
    tiles_ref, below_ref, tis_ref, live_ref, w0, w1, w2, w3, w4, w5, da_ref, *outs
):
    own = tiles_ref[8:16].astype(F32)
    low = below_ref[...].astype(F32)
    x = jnp.concatenate([own[:, 8:24], low[:, :16]], 0).reshape(CELLS, D)
    window_heads(0, x, tis_ref, live_ref, (w0, w1, w2, w3, w4, w5), da_ref, outs)


def right_window_kernel(
    tiles_ref, below_ref, right_ref, diag_ref, hid_t0_ref, dqkv0_ref,
    tis_ref, live_ref, w0, w1, w2, w3, w4, w5, da_ref, keep_ref, send_ref, *outs
):
    own = tiles_ref[8:16].astype(F32)
    low = below_ref[...].astype(F32)
    top = jnp.concatenate([own[:, 24:32], right_ref[...].astype(F32)], 1)
    bottom = jnp.concatenate([low[:, 16:24], diag_ref[...].astype(F32)], 1)
    x = jnp.concatenate([top, bottom], 0).reshape(CELLS, D)
    window_heads(1, x, tis_ref, live_ref, (w0, w1, w2, w3, w4, w5), da_ref, outs)
    dqkv_ref, hid_t_ref = outs[1], outs[4]
    for g in range(2):
        grad = nn(hid_t0_ref[...], dqkv0_ref[g]) + nn(hid_t_ref[...], dqkv_ref[g])
        put(grad, keep_ref.at[:, g * D : (g + 1) * D], send_ref.at[:, g * D : (g + 1) * D], False)


def last_kernel(
    hid0_ref, hid1_ref, hid_t0_ref, hid_t1_ref, tis_ref, live_ref, wq_ref, wk_ref, wv_ref, da_ref,
    att0_ref, att1_ref, db_ref, keep_ref, send_ref, att_ref, dqkv_ref,
):
    hidden = jnp.concatenate([hid0_ref[...], hid1_ref[...]], 0)
    query = nn(hidden, wq_ref[...]).astype(BF) * BF(HEAD_SCALE)
    key = nn(hidden, wk_ref[...]).astype(BF)
    value = nn(hidden, wv_ref[...]).astype(BF)
    units = [(w, p) for w in range(2) for p in range(2)]
    q, k, v, da, live = {}, {}, {}, {}, {}
    for u in units:
        w, p = u
        rows, lanes = slice(w * CELLS, (w + 1) * CELLS), slice(p * 128, (p + 1) * 128)
        q[u] = query[rows, lanes]
        k[u] = key[rows, lanes] * tis_ref[w]
        v[u] = value[rows, lanes] * tis_ref[w]
        da[u] = da_ref[w, :, lanes]
        live[u] = live_ref[w]

    def store(u, att, grads):
        w, p = u
        att_ref[w, :, p * 128 : (p + 1) * 128] = att
        for i, grad in enumerate(grads):
            dqkv_ref[w, :, i * GW + p * 128 : i * GW + (p + 1) * 128] = grad

    attention(units, q, k, v, da, live, store)
    grad = nn(hid_t0_ref[...], dqkv_ref[0]) + nn(hid_t1_ref[...], dqkv_ref[1])
    put(grad, keep_ref.at[:, :D], send_ref.at[:, :D], True)
    first = jnp.concatenate([att0_ref[...], att1_ref[...]], 0)
    attended = jnp.concatenate([first, att_ref[...].reshape(2 * CELLS, GW)], 1)
    att_t = nt(row_order(), attended).astype(BF)
    grad = nn(att_t, db_ref[...].reshape(2 * CELLS, D))
    put(grad, keep_ref.at[:, D:], send_ref.at[:, D:], True)


def columns(block, first):
    return pl.BlockSpec((D, GW), lambda g: (0, block * GROUPS + first + g))


def window_specs():
    shapes = [(CELLS, 2 * GW), (2, CELLS, D), (CELLS, D), (CELLS, D), (D, CELLS)]
    masks = [full((2, CELLS, 128))] * 2
    weights = [columns(block, g) for block in range(3) for g in range(2)]
    inputs = masks + weights + [full((2, CELLS, D))]
    return inputs, [full(s) for s in shapes], [jax.ShapeDtypeStruct(s, BF) for s in shapes]


def left_window(tiles, below, tis, live, w_qkv, da):
    inputs, outputs, shapes = window_specs()
    return pl.pallas_call(
        left_window_kernel,
        grid=(1,),
        in_specs=[full((16, 32, D)), full((8, 24, D))] + inputs,
        out_specs=outputs,
        out_shape=shapes,
        compiler_params=pltpu.CompilerParams(vmem_limit_bytes=VMEM),
        cost_estimate=cost(3e9, 5e6),
        name="left_window",
    )(tiles, below, tis, live, *[w_qkv] * 6, da)


def right_window(tiles, below, right, diag, hid_t0, dqkv0, tis, live, w_qkv, da):
    inputs, outputs, shapes = window_specs()
    half = full((D // 2, 2 * D))
    half_shape = jax.ShapeDtypeStruct((D // 2, 2 * D), BF)
    return pl.pallas_call(
        right_window_kernel,
        grid=(1,),
        in_specs=[
            full((16, 32, D)), full((8, 24, D)), full((8, 8, D)), full((8, 8, D)),
            full((D, CELLS)), full((2, CELLS, D)),
        ] + inputs,
        out_specs=[half, half] + outputs,
        out_shape=[half_shape, half_shape] + shapes,
        compiler_params=pltpu.CompilerParams(vmem_limit_bytes=VMEM),
        cost_estimate=cost(4e9, 6e6),
        name="right_window",
    )(tiles, below, right, diag, hid_t0, dqkv0, tis, live, *[w_qkv] * 6, da)


def last_heads(hids, hid_ts, tis, live, w_qkv, da, atts, db):
    rows, turned, masks = full((CELLS, D)), full((D, CELLS)), full((2, CELLS, 128))
    part = full((CELLS, 2 * GW))
    shapes = [(D // 2, 2 * D), (D // 2, 2 * D), (2, CELLS, GW), (2, CELLS, D)]
    return pl.pallas_call(
        last_kernel,
        grid=(1,),
        in_specs=[
            rows, rows, turned, turned, masks, masks, columns(0, 2), columns(1, 2), columns(2, 2),
            pl.BlockSpec((2, CELLS, GW), lambda g: (0, 0, 2)), part, part, full((2, CELLS, D)),
        ],
        out_specs=[full(s) for s in shapes],
        out_shape=[jax.ShapeDtypeStruct(s, BF) for s in shapes],
        compiler_params=pltpu.CompilerParams(vmem_limit_bytes=VMEM),
        cost_estimate=cost(4e9, 6e6),
        name="last_heads",
    )(*hids, *hid_ts, tis, live, w_qkv, w_qkv, w_qkv, da, *atts, db)


def out_kernel(xw0_ref, xw1_ref, tis_ref, att0_ref, att1_ref, att2_ref, wp_ref, out_ref):
    for w, (xw_ref, att_ref) in enumerate(((xw0_ref, att0_ref), (xw1_ref, att1_ref))):
        tis = jnp.tile(tis_ref[w].astype(F32), (1, D // 128))
        attended = jnp.concatenate([att_ref[...], att2_ref[w]], 1)
        out = xw_ref[...].astype(F32) + tis * nn(attended, wp_ref[...])
        out_ref[:, w] = out.astype(BF).reshape(WIN, WIN, D)


def out_part(xws, tis, atts, att2, w_proj):
    out = pl.pallas_call(
        out_kernel,
        out_shape=jax.ShapeDtypeStruct((WIN, 2, WIN, D), BF),
        compiler_params=pltpu.CompilerParams(vmem_limit_bytes=VMEM),
        cost_estimate=cost(3e9, 1e6),
        name="out_part",
    )(*xws, tis, *atts, att2, w_proj)
    return out.reshape(1, WIN, 2 * WIN, D)


def grad_kernel(
    xw0_ref, xw1_ref, cot_ref, tis_ref, dqkv0_ref, dqkv1_ref, dqkv2_ref,
    wq_ref, wk_ref, wv_ref, grad_ref, acc_ref,
):
    step = pl.program_id(0)
    weights = jnp.concatenate([wq_ref[...], wk_ref[...], wv_ref[...]], 1)
    first = jnp.concatenate([dqkv0_ref[0], dqkv1_ref[0]], 0)
    last = dqkv2_ref[...].reshape(2 * CELLS, D)
    part = nt(jnp.where(step < GROUPS - 1, first, last), weights)

    @pl.when(step == 0)
    def _():
        acc_ref[...] = part

    @pl.when(step > 0)
    def _():
        acc_ref[...] += part

    @pl.when(step == GROUPS - 1)
    def _():
        for w, xw_ref in enumerate((xw0_ref, xw1_ref)):
            normed, inv = moments(xw_ref[...].astype(F32))
            tis = jnp.tile(tis_ref[w].astype(F32), (1, D // 128))
            dh = acc_ref[w * CELLS : (w + 1) * CELLS] * tis
            dnorm = inv * (
                dh
                - jnp.mean(dh, -1, keepdims=True)
                - normed * jnp.mean(dh * normed, -1, keepdims=True)
            )
            grad = cot_ref[:, w].reshape(CELLS, D).astype(F32) + dnorm
            grad_ref[:, w] = grad.astype(BF).reshape(WIN, WIN, D)


def grad_part(xws, cot, tis, dqkvs, dqkv2, w_qkv):
    part = pl.BlockSpec((1, CELLS, D), lambda g: (jnp.minimum(g, 1), 0, 0))
    rows = full((CELLS, D))
    grad = pl.pallas_call(
        grad_kernel,
        grid=(GROUPS,),
        in_specs=[
            rows, rows, full((WIN, 2, WIN, D)), full((2, CELLS, 128)), part, part,
            full((2, CELLS, D)), columns(0, 0), columns(1, 0), columns(2, 0),
        ],
        out_specs=full((WIN, 2, WIN, D)),
        out_shape=jax.ShapeDtypeStruct((WIN, 2, WIN, D), BF),
        scratch_shapes=[pltpu.VMEM((2 * CELLS, D), F32)],
        compiler_params=pltpu.CompilerParams(vmem_limit_bytes=VMEM),
        cost_estimate=cost(6e9, 1e6),
        name="grad_part",
    )(*xws, cot, tis, *dqkvs, dqkv2, w_qkv, w_qkv, w_qkv)
    return grad.reshape(1, WIN, 2 * WIN, D)


def finish_kernel(parts_ref, qkv_ref, proj_ref):
    total = parts_ref[0].astype(F32)
    for part in range(1, parts_ref.shape[0]):
        total = total + parts_ref[part].astype(F32)
    total = total * (1.0 / math.sqrt(512))
    for i in range(3):
        for g in range(GROUPS):
            at = g * D + i * GW
            qkv_ref[:, i * D + g * GW : i * D + (g + 1) * GW] = total[:, at : at + GW]
    proj_ref[...] = total[:, 3 * D :]


def finish(parts):
    rows = parts.shape[1]
    return pl.pallas_call(
        finish_kernel,
        out_shape=[
            jax.ShapeDtypeStruct((rows, 3 * D), F32),
            jax.ShapeDtypeStruct((rows, D), F32),
        ],
        compiler_params=pltpu.CompilerParams(vmem_limit_bytes=VMEM),
        name="finish",
    )(parts)


def send(value, axis, move):
    devices = lax.axis_size(axis)
    return lax.ppermute(value, axis, [(i, move(i) % devices) for i in range(devices)])


def add(*terms):
    total = terms[0].astype(F32)
    for term in terms[1:]:
        total = total + term.astype(F32)
    return total.astype(BF)


def ring_start(low, high, axis, flips):
    one, three = flips
    return send(low[2:], axis, lambda j: j ^ one), send(high[1::2], axis, lambda j: j ^ three)


def ring_pass(low, high, came, axis, flips):
    one, three = flips
    low = add(low[:2], came[0])
    high = add(high[::2], came[1])
    came = send(low[1], axis, lambda j: j ^ three), send(high[1], axis, lambda j: j ^ one)
    return (low[0], high[0]), came


def ring_end(kept, came):
    return jnp.concatenate([add(kept[0], came[0]), add(kept[1], came[1])], 1)


def direct_start(rows, axis, flips):
    one, three = flips
    part = blocks(rows)
    return [
        send(part[at], axis, lambda j, flip=flip: j ^ flip)
        for at, flip in ((3, one ^ three), (1, three), (2, one))
    ]


def direct_end(rows, came):
    return add(blocks(rows)[0], *came)


def exchange(rows, axis, groups=None):
    parts = len(groups[0]) if groups else math.prod(lax.axis_size(a) for a in axis)
    rows = rows.reshape(parts, rows.shape[0] // parts, rows.shape[1])
    return lax.all_to_all(rows, axis, 0, 0, axis_index_groups=groups)


def tie(*values):
    return lax.optimization_barrier(values)


def blocks(value):
    return value.reshape(4, value.shape[0] // 4, value.shape[1])


def shards(tiles, cotangent, tissue, w_qkv, w_proj):
    mine = tiles[0]
    above, left, corner = edges(mine)
    below = send(above, "gy", lambda i: i - 1)
    right = send(left, "gx", lambda i: i - 1)
    ny, nx = lax.axis_size("gy"), lax.axis_size("gx")
    diag = lax.ppermute(
        corner,
        ("gy", "gx"),
        [
            (a * nx + b, (a - 1) % ny * nx + (b - 1) % nx)
            for a in range(ny)
            for b in range(nx)
        ],
    )
    cot = cotangent.reshape(WIN, 2, WIN, D)
    db, da, tis, live = branch(cot, tissue[0], w_proj)
    along_x, along_y = ("dp", (1, 3)), ("gy", (2, 6))
    att0, dqkv0, xw0, hid0, hid_t0 = left_window(mine, below, tis, live, w_qkv, da)
    keep0, send0, att1, dqkv1, xw1, hid1, hid_t1 = right_window(
        mine, below, right, diag, hid_t0, dqkv0, tis, live, w_qkv, da
    )
    came = send(send0, "gy", lambda i: i ^ 1)
    keep1, send1, att2, dqkv2 = last_heads(
        (hid0, hid1), (hid_t0, hid_t1), tis, live, w_qkv, da, (att0, att1), db
    )
    came, send1 = tie(came, send1)
    first = add(keep0, came)
    low_a, high_a = blocks(first[:, :D]), blocks(first[:, D:])
    came_a = ring_start(low_a, high_a, *along_x)
    second = add(keep1, send(send1, "gy", lambda i: i ^ 1))
    second, att2, dqkv2 = tie(second, att2, dqkv2)
    low_b, high_b = blocks(second[:, :D]), blocks(second[:, D:])
    came_b = ring_start(low_b, high_b, *along_y)
    out = out_part((xw0, xw1), tis, (att0, att1), att2, w_proj)
    grad = grad_part((xw0, xw1), cot, tis, (dqkv0, dqkv1), dqkv2, w_qkv)
    came_b, out, grad, low_a, high_a = tie(came_b, out, grad, low_a, high_a)
    kept_b, came_b = ring_pass(low_b, high_b, came_b, *along_y)
    kept_a, came_a = ring_pass(low_a, high_a, came_a, *along_x)
    rows_a = ring_end(kept_a, came_a)
    rows_b = ring_end(kept_b, came_b)
    came_a = direct_start(rows_a, *along_y)
    came_b = direct_start(rows_b, *along_x)
    rows = jnp.concatenate([direct_end(rows_a, came_a), direct_end(rows_b, came_b)], 1)
    grad_qkv, grad_proj = finish(exchange(rows, ("gx",)))
    return out, grad, grad_qkv, grad_proj


def solution(mesh):
    block = P("dp", "gy", "gx", None)
    in_specs = (block, block, P("dp", "gy", "gx"), P(), P())
    out_specs = (block, block, P(("dp", "gy", "gx"), None), P(("dp", "gy", "gx"), None))
    return jax.shard_map(
        shards, mesh=mesh, in_specs=in_specs, out_specs=out_specs, check_vma=False
    )
```

```python
import math

import jax
import jax.numpy as jnp
from jax import lax
from jax.experimental import pallas as pl
from jax.experimental.pallas import tpu as pltpu
from jax.sharding import PartitionSpec as P

F32 = jnp.float32
BF = jnp.bfloat16
D = 768
WIN = 16
CELLS = WIN * WIN
GROUPS = 3
GW = D // GROUPS
HEAD_SCALE = 0.125
VMEM = 32 * 1024 * 1024


def nn(a, b):
    return lax.dot_general(a, b, (((1,), (0,)), ((), ())), preferred_element_type=F32)


def nt(a, b):
    return lax.dot_general(a, b, (((1,), (1,)), ((), ())), preferred_element_type=F32)


def tn(a, b):
    return lax.dot_general(a, b, (((0,), (0,)), ((), ())), preferred_element_type=F32)


def full(shape):
    return pl.BlockSpec(shape, lambda *g: (0,) * len(shape))


def cost(flops, size):
    return pl.CostEstimate(flops=int(flops), bytes_accessed=int(size), transcendentals=0)


def corner_kernel(tiles_ref, after_ref, corner_ref):
    corner_ref[...] = tiles_ref[...].astype(F32)[:, :8].astype(BF)


def above_kernel(tiles_ref, above_ref):
    above_ref[...] = tiles_ref[...].astype(F32)[:, 8:].astype(BF)


def left_kernel(tiles_ref, after_ref, left_ref):
    left_ref[...] = tiles_ref[...].astype(F32)[:, :8].astype(BF)


def cut(kernel, name, flops, tiles, after, block, first, columns):
    place = pl.BlockSpec(memory_space=pl.ANY)
    return pl.pallas_call(
        kernel,
        grid=(1,),
        in_specs=[pl.BlockSpec(block + (D,), lambda g: (first, 0, 0))] + [place] * len(after),
        out_specs=full((8, columns, D)),
        out_shape=jax.ShapeDtypeStruct((8, columns, D), BF),
        compiler_params=pltpu.CompilerParams(vmem_limit_bytes=VMEM),
        cost_estimate=cost(flops, 1e3),
        name=name,
    )(tiles, *after)


def edges(tiles):
    above = cut(above_kernel, "above", 3e10, tiles, [], (8, 32), 0, 24)
    corner = cut(corner_kernel, "corner", 1e3, tiles, [above], (8, 16), 0, 8)
    left = cut(left_kernel, "left", 1e3, tiles, [corner], (8, 16), 1, 8)
    return above, left, corner


def branch_kernel(
    cot_hbm, tissue_hbm, wp_hbm, db_ref, da_ref, tis_ref, live_ref, cot_ref, tissue_ref, wp_ref, sem
):
    copies = [
        pltpu.make_async_copy(tissue_hbm, tissue_ref, sem.at[0]),
        pltpu.make_async_copy(cot_hbm, cot_ref, sem.at[1]),
        pltpu.make_async_copy(wp_hbm, wp_ref, sem.at[2]),
    ]
    for copy in copies:
        copy.start()
    copies[0].wait()
    grid = tissue_ref[...].astype(F32).astype(BF)
    cell = lax.broadcasted_iota(jnp.int32, (CELLS, 1), 0)
    row_of = lax.broadcasted_iota(jnp.int32, (CELLS, WIN), 1) == (cell >> 4)
    rows = nn(row_of.astype(F32).astype(BF), grid)
    lane = lax.broadcasted_iota(jnp.int32, (CELLS, 2 * WIN), 1)
    ones = jnp.ones((2 * WIN, 128), BF)
    copies[1].wait()
    copies[2].wait()
    for w in range(2):
        own = jnp.where(lane == (cell & 15) + w * WIN, rows, 0.0).astype(BF)
        tis = nn(own, ones)
        some = jnp.max(jnp.max(tis, 0, keepdims=True), 1, keepdims=True)
        tis_ref[w] = tis.astype(BF)
        live_ref[w] = jnp.maximum(tis, 1.0 - some).astype(BF)
        db = cot_ref[:, w].reshape(CELLS, D) * jnp.tile(tis.astype(BF), (1, D // 128))
        db_ref[w] = db
        da_ref[w] = nt(db, wp_ref[...]).astype(BF)


def branch(cot, tissue, w_proj):
    shape = jax.ShapeDtypeStruct((2, CELLS, D), BF)
    mask = jax.ShapeDtypeStruct((2, CELLS, 128), BF)
    return pl.pallas_call(
        branch_kernel,
        in_specs=[pl.BlockSpec(memory_space=pltpu.HBM)] * 3,
        out_shape=[shape, shape, mask, mask],
        scratch_shapes=[
            pltpu.VMEM((WIN, 2, WIN, D), BF),
            pltpu.VMEM((WIN, 2 * WIN), jnp.int32),
            pltpu.VMEM((D, D), BF),
            pltpu.SemaphoreType.DMA((3,)),
        ],
        compiler_params=pltpu.CompilerParams(vmem_limit_bytes=VMEM),
        cost_estimate=cost(2e10, 4e6),
        name="branch",
    )(cot, tissue, w_proj)


def row_order():
    gy = lax.axis_index("gy")
    dp, y, core = lax.axis_index("dp"), gy >> 1, gy & 1
    at = lax.broadcasted_iota(jnp.int32, (D, 1), 0)
    third = ((at.astype(F32) + 0.5) * (1.0 / 3)).astype(jnp.int32)
    dp_of = ((third >> 6) & 1) ^ (((third >> 5) & 1) * 3) ^ dp
    y_of = ((third >> 4) & 1) ^ (((third >> 3) & 1) * 3) ^ y
    core_of = (third >> 7) ^ core
    source = ((dp_of * 8 + y_of * 2 + core_of) * 8 + (third & 7)) * 3 + at - third * 3
    column = lax.broadcasted_iota(jnp.int32, (D, D), 1)
    return jnp.where(column == source, 1.0, 0.0).astype(BF)


def moments(x):
    mean = jnp.mean(x, -1, keepdims=True)
    centred = x - mean
    inv = lax.rsqrt(jnp.mean(centred * centred, -1, keepdims=True) + 1e-05)
    return centred * inv, inv


def put(grad, keep_ref, send_ref, y_first):
    if y_first:
        size = D // 32
        places = [(c * 4 + x) * 4 + y for c in range(2) for y in range(4) for x in range(4)]
        grad = jnp.concatenate([grad[at * size : (at + 1) * size] for at in places], 0)
    keep_ref[...] = grad[: D // 2].astype(BF)
    send_ref[...] = grad[D // 2 :].astype(BF)


def attention(units, q, k, v, da, live, store):
    lane = lax.broadcasted_iota(jnp.int32, (1, 128), 1)
    sel = [(lane < 64).astype(BF), (lane >= 64).astype(BF)]
    weight, ds, rinv, att = {}, {}, {}, {}
    for u in units:
        for h in range(2):
            weight[u, h] = jnp.exp(nt(q[u], k[u] * sel[h])).astype(BF)
    for u in units:
        both = nn(weight[u, 0], jnp.concatenate([v[u] * sel[0], live[u] * sel[0]], 1)) + nn(
            weight[u, 1], jnp.concatenate([v[u] * sel[1], live[u] * sel[1]], 1)
        )
        rinv[u] = 1.0 / both[:, 128:]
        att[u] = both[:, :128] * rinv[u]
    for u in units:
        terms = da[u].astype(F32) * att[u]
        for h in range(2):
            delta = jnp.sum(terms * sel[h].astype(F32), 1, keepdims=True)
            dprobs = nt(da[u], v[u] * sel[h]) - delta
            ds[u, h] = (weight[u, h].astype(F32) * dprobs).astype(BF)
    for u in units:
        dq = (nn(ds[u, 0], k[u] * sel[0]) + nn(ds[u, 1], k[u] * sel[1])) * (rinv[u] * HEAD_SCALE)
        dan = (da[u].astype(F32) * rinv[u]).astype(BF)
        qn = (q[u].astype(F32) * rinv[u]).astype(BF)
        dv = tn(weight[u, 0], dan * sel[0]) + tn(weight[u, 1], dan * sel[1])
        dk = tn(ds[u, 0], qn * sel[0]) + tn(ds[u, 1], qn * sel[1])
        store(u, att[u].astype(BF), (dq.astype(BF), dk.astype(BF), dv.astype(BF)))


def window_heads(w, x, tis_ref, live_ref, weights, da_ref, outs):
    att_ref, dqkv_ref, xw_ref, hid_ref, hid_t_ref = outs
    tis = tis_ref[w]
    xw_ref[...] = x.astype(BF)
    normed, _ = moments(x)
    hidden = normed.astype(BF)
    hid_ref[...] = hidden
    hid_t_ref[...] = nt(row_order(), hidden * jnp.tile(tis, (1, D // 128))).astype(BF)
    units = [(g, p) for g in range(2) for p in range(2)]
    q, k, v, da = {}, {}, {}, {}
    for g in range(2):
        query = nn(hidden, weights[g][...]).astype(BF) * BF(HEAD_SCALE)
        key = nn(hidden, weights[2 + g][...]).astype(BF)
        value = nn(hidden, weights[4 + g][...]).astype(BF)
        for p in range(2):
            lanes = slice(p * 128, (p + 1) * 128)
            q[g, p] = query[:, lanes]
            k[g, p] = key[:, lanes] * tis
            v[g, p] = value[:, lanes] * tis
            da[g, p] = da_ref[w, :, g * GW + p * 128 : g * GW + (p + 1) * 128]

    def store(u, att, grads):
        g, p = u
        att_ref[:, g * GW + p * 128 : g * GW + (p + 1) * 128] = att
        for i, grad in enumerate(grads):
            dqkv_ref[g, :, i * GW + p * 128 : i * GW + (p + 1) * 128] = grad

    attention(units, q, k, v, da, {u: live_ref[w] for u in units}, store)


def left_window_kernel(
    tiles_ref, below_ref, tis_ref, live_ref, w0, w1, w2, w3, w4, w5, da_ref, *outs
):
    own = tiles_ref[8:16].astype(F32)
    low = below_ref[...].astype(F32)
    x = jnp.concatenate([own[:, 8:24], low[:, :16]], 0).reshape(CELLS, D)
    window_heads(0, x, tis_ref, live_ref, (w0, w1, w2, w3, w4, w5), da_ref, outs)


def right_window_kernel(
    tiles_ref, below_ref, right_ref, diag_ref, hid_t0_ref, dqkv0_ref,
    tis_ref, live_ref, w0, w1, w2, w3, w4, w5, da_ref, keep_ref, send_ref, *outs
):
    own = tiles_ref[8:16].astype(F32)
    low = below_ref[...].astype(F32)
    top = jnp.concatenate([own[:, 24:32], right_ref[...].astype(F32)], 1)
    bottom = jnp.concatenate([low[:, 16:24], diag_ref[...].astype(F32)], 1)
    x = jnp.concatenate([top, bottom], 0).reshape(CELLS, D)
    window_heads(1, x, tis_ref, live_ref, (w0, w1, w2, w3, w4, w5), da_ref, outs)
    dqkv_ref, hid_t_ref = outs[1], outs[4]
    for g in range(2):
        grad = nn(hid_t0_ref[...], dqkv0_ref[g]) + nn(hid_t_ref[...], dqkv_ref[g])
        put(grad, keep_ref.at[:, g * D : (g + 1) * D], send_ref.at[:, g * D : (g + 1) * D], False)


def last_kernel(
    hid0_ref, hid1_ref, hid_t0_ref, hid_t1_ref, tis_ref, live_ref, wq_ref, wk_ref, wv_ref, da_ref,
    att0_ref, att1_ref, db_ref, keep_ref, send_ref, att_ref, dqkv_ref,
):
    hidden = jnp.concatenate([hid0_ref[...], hid1_ref[...]], 0)
    query = nn(hidden, wq_ref[...]).astype(BF) * BF(HEAD_SCALE)
    key = nn(hidden, wk_ref[...]).astype(BF)
    value = nn(hidden, wv_ref[...]).astype(BF)
    units = [(w, p) for w in range(2) for p in range(2)]
    q, k, v, da, live = {}, {}, {}, {}, {}
    for u in units:
        w, p = u
        rows, lanes = slice(w * CELLS, (w + 1) * CELLS), slice(p * 128, (p + 1) * 128)
        q[u] = query[rows, lanes]
        k[u] = key[rows, lanes] * tis_ref[w]
        v[u] = value[rows, lanes] * tis_ref[w]
        da[u] = da_ref[w, :, lanes]
        live[u] = live_ref[w]

    def store(u, att, grads):
        w, p = u
        att_ref[w, :, p * 128 : (p + 1) * 128] = att
        for i, grad in enumerate(grads):
            dqkv_ref[w, :, i * GW + p * 128 : i * GW + (p + 1) * 128] = grad

    attention(units, q, k, v, da, live, store)
    grad = nn(hid_t0_ref[...], dqkv_ref[0]) + nn(hid_t1_ref[...], dqkv_ref[1])
    put(grad, keep_ref.at[:, :D], send_ref.at[:, :D], True)
    first = jnp.concatenate([att0_ref[...], att1_ref[...]], 0)
    attended = jnp.concatenate([first, att_ref[...].reshape(2 * CELLS, GW)], 1)
    att_t = nt(row_order(), attended).astype(BF)
    grad = nn(att_t, db_ref[...].reshape(2 * CELLS, D))
    put(grad, keep_ref.at[:, D:], send_ref.at[:, D:], True)


def columns(block, first):
    return pl.BlockSpec((D, GW), lambda g: (0, block * GROUPS + first + g))


def window_specs():
    shapes = [(CELLS, 2 * GW), (2, CELLS, D), (CELLS, D), (CELLS, D), (D, CELLS)]
    masks = [full((2, CELLS, 128))] * 2
    weights = [columns(block, g) for block in range(3) for g in range(2)]
    inputs = masks + weights + [full((2, CELLS, D))]
    return inputs, [full(s) for s in shapes], [jax.ShapeDtypeStruct(s, BF) for s in shapes]


def left_window(tiles, below, tis, live, w_qkv, da):
    inputs, outputs, shapes = window_specs()
    return pl.pallas_call(
        left_window_kernel,
        grid=(1,),
        in_specs=[full((16, 32, D)), full((8, 24, D))] + inputs,
        out_specs=outputs,
        out_shape=shapes,
        compiler_params=pltpu.CompilerParams(vmem_limit_bytes=VMEM),
        cost_estimate=cost(3e9, 5e6),
        name="left_window",
    )(tiles, below, tis, live, *[w_qkv] * 6, da)


def right_window(tiles, below, right, diag, hid_t0, dqkv0, tis, live, w_qkv, da):
    inputs, outputs, shapes = window_specs()
    half = full((D // 2, 2 * D))
    half_shape = jax.ShapeDtypeStruct((D // 2, 2 * D), BF)
    return pl.pallas_call(
        right_window_kernel,
        grid=(1,),
        in_specs=[
            full((16, 32, D)), full((8, 24, D)), full((8, 8, D)), full((8, 8, D)),
            full((D, CELLS)), full((2, CELLS, D)),
        ] + inputs,
        out_specs=[half, half] + outputs,
        out_shape=[half_shape, half_shape] + shapes,
        compiler_params=pltpu.CompilerParams(vmem_limit_bytes=VMEM),
        cost_estimate=cost(4e9, 6e6),
        name="right_window",
    )(tiles, below, right, diag, hid_t0, dqkv0, tis, live, *[w_qkv] * 6, da)


def last_heads(hids, hid_ts, tis, live, w_qkv, da, atts, db):
    rows, turned, masks = full((CELLS, D)), full((D, CELLS)), full((2, CELLS, 128))
    part = full((CELLS, 2 * GW))
    shapes = [(D // 2, 2 * D), (D // 2, 2 * D), (2, CELLS, GW), (2, CELLS, D)]
    return pl.pallas_call(
        last_kernel,
        grid=(1,),
        in_specs=[
            rows, rows, turned, turned, masks, masks, columns(0, 2), columns(1, 2), columns(2, 2),
            pl.BlockSpec((2, CELLS, GW), lambda g: (0, 0, 2)), part, part, full((2, CELLS, D)),
        ],
        out_specs=[full(s) for s in shapes],
        out_shape=[jax.ShapeDtypeStruct(s, BF) for s in shapes],
        compiler_params=pltpu.CompilerParams(vmem_limit_bytes=VMEM),
        cost_estimate=cost(4e9, 6e6),
        name="last_heads",
    )(*hids, *hid_ts, tis, live, w_qkv, w_qkv, w_qkv, da, *atts, db)


def out_kernel(xw0_ref, xw1_ref, tis_ref, att0_ref, att1_ref, att2_ref, wp_ref, out_ref):
    for w, (xw_ref, att_ref) in enumerate(((xw0_ref, att0_ref), (xw1_ref, att1_ref))):
        tis = jnp.tile(tis_ref[w].astype(F32), (1, D // 128))
        attended = jnp.concatenate([att_ref[...], att2_ref[w]], 1)
        out = xw_ref[...].astype(F32) + tis * nn(attended, wp_ref[...])
        out_ref[:, w] = out.astype(BF).reshape(WIN, WIN, D)


def out_part(xws, tis, atts, att2, w_proj):
    out = pl.pallas_call(
        out_kernel,
        out_shape=jax.ShapeDtypeStruct((WIN, 2, WIN, D), BF),
        compiler_params=pltpu.CompilerParams(vmem_limit_bytes=VMEM),
        cost_estimate=cost(1e3, 1e3),
        name="out_part",
    )(*xws, tis, *atts, att2, w_proj)
    return out.reshape(1, WIN, 2 * WIN, D)


def grad_kernel(
    xw0_ref, xw1_ref, cot_ref, tis_ref, dqkv0_ref, dqkv1_ref, dqkv2_ref,
    wq_ref, wk_ref, wv_ref, grad_ref, acc_ref,
):
    step = pl.program_id(0)
    weights = jnp.concatenate([wq_ref[...], wk_ref[...], wv_ref[...]], 1)
    first = jnp.concatenate([dqkv0_ref[0], dqkv1_ref[0]], 0)
    last = dqkv2_ref[...].reshape(2 * CELLS, D)
    part = nt(jnp.where(step < GROUPS - 1, first, last), weights)

    @pl.when(step == 0)
    def _():
        acc_ref[...] = part

    @pl.when(step > 0)
    def _():
        acc_ref[...] += part

    @pl.when(step == GROUPS - 1)
    def _():
        for w, xw_ref in enumerate((xw0_ref, xw1_ref)):
            normed, inv = moments(xw_ref[...].astype(F32))
            tis = jnp.tile(tis_ref[w].astype(F32), (1, D // 128))
            dh = acc_ref[w * CELLS : (w + 1) * CELLS] * tis
            dnorm = inv * (
                dh
                - jnp.mean(dh, -1, keepdims=True)
                - normed * jnp.mean(dh * normed, -1, keepdims=True)
            )
            grad = cot_ref[:, w].reshape(CELLS, D).astype(F32) + dnorm
            grad_ref[:, w] = grad.astype(BF).reshape(WIN, WIN, D)


def grad_part(xws, cot, tis, dqkvs, dqkv2, w_qkv):
    part = pl.BlockSpec((1, CELLS, D), lambda g: (jnp.minimum(g, 1), 0, 0))
    rows = full((CELLS, D))
    grad = pl.pallas_call(
        grad_kernel,
        grid=(GROUPS,),
        in_specs=[
            rows, rows, full((WIN, 2, WIN, D)), full((2, CELLS, 128)), part, part,
            full((2, CELLS, D)), columns(0, 0), columns(1, 0), columns(2, 0),
        ],
        out_specs=full((WIN, 2, WIN, D)),
        out_shape=jax.ShapeDtypeStruct((WIN, 2, WIN, D), BF),
        scratch_shapes=[pltpu.VMEM((2 * CELLS, D), F32)],
        compiler_params=pltpu.CompilerParams(vmem_limit_bytes=VMEM),
        cost_estimate=cost(1e3, 1e3),
        name="grad_part",
    )(*xws, cot, tis, *dqkvs, dqkv2, w_qkv, w_qkv, w_qkv)
    return grad.reshape(1, WIN, 2 * WIN, D)


def finish_kernel(parts_ref, qkv_ref, proj_ref):
    total = parts_ref[0].astype(F32)
    for part in range(1, parts_ref.shape[0]):
        total = total + parts_ref[part].astype(F32)
    total = total * (1.0 / math.sqrt(512))
    wide = (GROUPS + 1) * D // 128
    for row in range(total.shape[0] // wide):
        for c in range(wide):
            line = total[row * wide + c : row * wide + c + 1]
            g, i, half = c // 6, c % 6 // 2, c % 2
            if g < GROUPS:
                at = i * D + g * GW + half * 128
                qkv_ref[row : row + 1, at : at + 128] = line
            else:
                at = (c - 6 * GROUPS) * 128
                proj_ref[row : row + 1, at : at + 128] = line


def finish(parts):
    rows = parts.shape[1] * 128 // ((GROUPS + 1) * D)
    return pl.pallas_call(
        finish_kernel,
        out_shape=[
            jax.ShapeDtypeStruct((rows, 3 * D), F32),
            jax.ShapeDtypeStruct((rows, D), F32),
        ],
        compiler_params=pltpu.CompilerParams(vmem_limit_bytes=VMEM),
        name="finish",
    )(parts)


def send(value, axis, move):
    devices = lax.axis_size(axis)
    return lax.ppermute(value, axis, [(i, move(i) % devices) for i in range(devices)])


def add(*terms):
    total = terms[0].astype(F32)
    for term in terms[1:]:
        total = total + term.astype(F32)
    return total.astype(BF)


def ring_start(low, high, axis, flips):
    one, three = flips
    return send(low[3], axis, lambda j: j ^ one), send(high[3], axis, lambda j: j ^ three)


def ring_pass(low, high, came, axis, flips):
    one, three = flips
    to_one = jnp.concatenate([low[2], add(high[2], came[1])], 1)
    to_three = jnp.concatenate([add(low[1], came[0]), high[1]], 1)
    return send(to_one, axis, lambda j: j ^ one), send(to_three, axis, lambda j: j ^ three)


def ring_end(low, high, came):
    n = low.shape[2]
    up, down = came
    low = add(low[0], up[:, :n], down[:, :n])
    high = add(high[0], up[:, n:], down[:, n:])
    return jnp.concatenate([low, high], 1)


def direct_start(rows, axis, flips):
    one, three = flips
    part = blocks(rows)
    return [
        send(part[at], axis, lambda j, flip=flip: j ^ flip)
        for at, flip in ((3, one ^ three), (1, three), (2, one))
    ]


def direct_end(rows, came):
    return add(blocks(rows)[0], *came)


def exchange(rows, axis, groups=None):
    parts = len(groups[0]) if groups else math.prod(lax.axis_size(a) for a in axis)
    rows = rows.reshape(parts, rows.shape[0] // parts, rows.shape[1])
    return lax.all_to_all(rows, axis, 0, 0, axis_index_groups=groups)


def tie(*values):
    return lax.optimization_barrier(values)


def blocks(value):
    return value.reshape(4, value.shape[0] // 4, value.shape[1])


def shards(tiles, cotangent, tissue, w_qkv, w_proj):
    mine = tiles[0]
    above, left, corner = edges(mine)
    below = send(above, "gy", lambda i: i - 1)
    right = send(left, "gx", lambda i: i - 1)
    ny, nx = lax.axis_size("gy"), lax.axis_size("gx")
    diag = lax.ppermute(
        corner,
        ("gy", "gx"),
        [
            (a * nx + b, (a - 1) % ny * nx + (b - 1) % nx)
            for a in range(ny)
            for b in range(nx)
        ],
    )
    cot = cotangent.reshape(WIN, 2, WIN, D)
    db, da, tis, live = branch(cot, tissue[0], w_proj)
    along_x, along_y = ("dp", (1, 3)), ("gy", (2, 6))
    att0, dqkv0, xw0, hid0, hid_t0 = left_window(mine, below, tis, live, w_qkv, da)
    keep0, send0, att1, dqkv1, xw1, hid1, hid_t1 = right_window(
        mine, below, right, diag, hid_t0, dqkv0, tis, live, w_qkv, da
    )
    came = send(send0, "gy", lambda i: i ^ 1)
    keep1, send1, att2, dqkv2 = last_heads(
        (hid0, hid1), (hid_t0, hid_t1), tis, live, w_qkv, da, (att0, att1), db
    )
    came, send1 = tie(came, send1)
    first = add(keep0, came)
    low_a, high_a = blocks(first[:, :D]), blocks(first[:, D:])
    came_a = ring_start(low_a, high_a, *along_x)
    second = add(keep1, send(send1, "gy", lambda i: i ^ 1))
    second, att2 = tie(second, att2)
    low_b, high_b = blocks(second[:, :D]), blocks(second[:, D:])
    came_b = ring_start(low_b, high_b, *along_y)
    out = out_part((xw0, xw1), tis, (att0, att1), att2, w_proj)
    came_b, out, xw0, low_a, high_a = tie(came_b, out, xw0, low_a, high_a)
    came_b = ring_pass(low_b, high_b, came_b, *along_y)
    came_a = ring_pass(low_a, high_a, came_a, *along_x)
    grad = grad_part((xw0, xw1), cot, tis, (dqkv0, dqkv1), dqkv2, w_qkv)
    came_a, came_b, grad = tie(came_a, came_b, grad)
    rows_a = ring_end(low_a, high_a, came_a)
    rows_b = ring_end(low_b, high_b, came_b)
    came_a = direct_start(rows_a, *along_y)
    came_b = direct_start(rows_b, *along_x)
    rows = jnp.concatenate([direct_end(rows_a, came_a), direct_end(rows_b, came_b)], 1)
    grad_qkv, grad_proj = finish(lax.all_to_all(rows.reshape(nx, -1, 128), "gx", 0, 0))
    return out, grad, grad_qkv, grad_proj


def solution(mesh):
    block = P("dp", "gy", "gx", None)
    in_specs = (block, block, P("dp", "gy", "gx"), P(), P())
    out_specs = (block, block, P(("dp", "gy", "gx"), None), P(("dp", "gy", "gx"), None))
    return jax.shard_map(
        shards, mesh=mesh, in_specs=in_specs, out_specs=out_specs, check_vma=False
    )
```
